32 devices in a mesh: wshard: 4 (over y, x), ctx: 8 (over z, core).
Axes of the slice: x: 2, y: 2, z: 4, core: 2. Of those that a mesh axis runs over, the one named last changes fastest.
Arguments:
- tokens: bfloat16 [2, 4, 1024, 768], P(None, 'wshard', 'ctx'), may hold values from -6 to 6
- gain_one: bfloat16 [768], P('wshard'), may hold values from 0.099609375 to 1.8984375
- w_qkv: bfloat16 [768, 2304], P('wshard'), may hold values from -0.21875 to 0.21875
- w_out: bfloat16 [768, 768], P('wshard'), may hold values from -1.75 to 1.75
- gain_two: bfloat16 [768], P('wshard'), may hold values from 0.099609375 to 1.8984375
- w_up: bfloat16 [768, 3072], P('wshard'), may hold values from -0.21875 to 0.21875
- w_down: bfloat16 [3072, 768], P('wshard'), may hold values from -0.109375 to 0.109375
- cotangent: bfloat16 [2, 4, 1024, 768], P(None, 'wshard', 'ctx'), may hold values from -6 to 6
Outputs:
- result: bfloat16 [2, 4, 1024, 768], P(None, 'wshard', 'ctx')
- grad_tokens: float32 [2, 4, 1024, 768], P(None, 'wshard', 'ctx')
- grad_gain_one: float32 [768], P('wshard')
- grad_qkv: float32 [768, 2304], P('wshard')
- grad_out: float32 [768, 768], P('wshard')
- grad_gain_two: float32 [768], P('wshard')
- grad_up: float32 [768, 3072], P('wshard')
- grad_down: float32 [3072, 768], P('wshard')
The draws below stay inside these ranges and needn't reach their ends.
All inputs are finite; a program needn't handle non-finite values.
Results may differ from the reference program's by a relative error of at most 0.02.
Values may be sent and summed in bfloat16 or wider, within the bound.
No kernel may reach another device: no remote copies, remote signals or barrier semaphores. Data moves between devices by JAX's collectives and lax.ppermute only.
A program may use at most 192 MiB of HBM per device.

```python
import jax
import jax.numpy as jnp
from jax import lax

D = 768
HEADS = 12
HEAD_DIM = 64
FF = 3072
MB = 2
ROWS = 4
LENGTH = 1024


def steps_of(key, extent, split, least, high):
    loudness = 1.0
    for axis_at, parts in split:
        steps = jax.random.uniform(jax.random.fold_in(jax.random.fold_in(key, 6), axis_at), (parts,), jnp.float32, least / len(split), high / len(split))
        loudness = loudness * jnp.repeat(jnp.exp(steps), extent[axis_at] // parts).reshape((-1,) + (1,) * (len(extent) - 1 - axis_at))
    return loudness


def scatter_about(key, shape, scale, most, cuts=(), kind=jnp.bfloat16):
    drawn = scale * jax.random.normal(key, shape, jnp.float32)
    if cuts:
        drawn = drawn * steps_of(key, shape, cuts, -0.22, 0.18)
    return jnp.clip(drawn, -most, most).astype(kind)


def setup_inputs(seed: int = 0) -> dict:
    splits = jax.random.split(jax.random.key(seed), 9)
    tokens = scatter_about(splits[0], (MB, ROWS, LENGTH, D), 1.0, 6.0, ((1, 4), (2, 8)))
    gain_one = jnp.clip(1.0 + 0.18 * jax.random.normal(splits[1], (D,), jnp.float32), 0.099609375, 1.8984375).astype(jnp.bfloat16)
    w_qkv = scatter_about(splits[2], (D, 3 * D), D ** -0.5, 0.21875, ((0, 4),))
    w_out = scatter_about(splits[3], (D, D), (max(1, D * 16 // LENGTH)) ** -0.5, 1.75, ((0, 4),))
    gain_two = jnp.clip(1.0 + 0.18 * jax.random.normal(splits[4], (D,), jnp.float32), 0.099609375, 1.8984375).astype(jnp.bfloat16)
    w_up = scatter_about(splits[5], (D, FF), D ** -0.5, 0.21875, ((0, 4),))
    w_down = scatter_about(splits[6], (FF, D), FF ** -0.5, 0.109375, ((0, 4),))
    cotangent = scatter_about(splits[7], (MB, ROWS, LENGTH, D), 1.0, 6.0, ((1, 4), (2, 8)))
    return dict(tokens=tokens, gain_one=gain_one, w_qkv=w_qkv, w_out=w_out, gain_two=gain_two, w_up=w_up, w_down=w_down, cotangent=cotangent)


@jax.custom_vjp
def low(v):
    return lax.optimization_barrier(v.astype(jnp.bfloat16)).astype(jnp.float32)

@jax.custom_vjp
def low_back(v):
    return v

def low_keep(v):
    return (low(v), None)

def low_pass(kept, grad):
    return (grad,)

def back_keep(v):
    return (v, None)

def back_low(kept, grad):
    return (low(grad),)
low.defvjp(low_keep, low_pass)
low_back.defvjp(back_keep, back_low)
EPSILON = 1e-05
HIGHEST = lax.Precision.HIGHEST

def matmul(left_side, right_side):
    return jnp.dot(left_side, right_side, precision=HIGHEST, preferred_element_type=jnp.float32)

def layer_norm(inputs, scaling):
    centred = inputs - lax.optimization_barrier(jnp.mean(inputs, axis=-1, keepdims=True))
    variance = lax.optimization_barrier(jnp.mean(centred * centred, axis=-1, keepdims=True))
    return centred * lax.rsqrt(variance + EPSILON) * scaling

def attend(queries, keys_all, values_all):
    length = queries.shape[0]
    block_rows = min(512, length)
    positions = jnp.arange(length, dtype=jnp.int32)
    scaling = HEAD_DIM ** (-0.5)

    def one_block(number):
        first_row = number * block_rows
        query_rows = lax.dynamic_slice_in_dim(queries, first_row, block_rows, 0)
        scores = low_back(jnp.einsum('qhe,khe->hqk', query_rows, keys_all, precision=HIGHEST) * scaling)
        query_pos = first_row + jnp.arange(block_rows, dtype=jnp.int32)
        visible = positions[None, None, :] <= query_pos[None, :, None]
        magnitude = jnp.sqrt(scores * scores + 1.0)
        top_value = lax.optimization_barrier(jnp.max(jnp.where(visible, magnitude, 0.0), axis=-1, keepdims=True))
        weighted = jnp.exp(jnp.where(visible, magnitude - top_value, -1e+30))
        totals = lax.optimization_barrier(jnp.sum(weighted, axis=-1, keepdims=True))
        signed = low(scores / magnitude * weighted / totals)
        return jnp.einsum('hqk,khe->qhe', signed, values_all, precision=HIGHEST)
    blocks = lax.map(jax.checkpoint(one_block), jnp.arange(length // block_rows, dtype=jnp.int32))
    return blocks.reshape(length, HEADS * HEAD_DIM)

def forward(inputs, gain_one, w_qkv, w_out, gain_two, w_up, w_down):
    length = inputs.shape[0]
    normed = low(layer_norm(inputs, gain_one))
    mixed_all = low_back(low(matmul(normed, w_qkv)))
    queries = mixed_all[:, :D].reshape(length, HEADS, HEAD_DIM)
    keys_all = mixed_all[:, D:2 * D].reshape(length, HEADS, HEAD_DIM)
    values_all = mixed_all[:, 2 * D:].reshape(length, HEADS, HEAD_DIM)
    attended = low_back(low(attend(queries, keys_all, values_all)))
    hidden = inputs + low_back(matmul(attended, w_out))
    normed_two = low(layer_norm(hidden, gain_two))
    upward = low_back(matmul(normed_two, w_up))
    active = low(jax.nn.gelu(upward, approximate=True))
    return hidden + low_back(matmul(active, w_down))

def reference(tokens, gain_one, w_qkv, w_out, gain_two, w_up, w_down, cotangent):
    params = tuple((weight_item.astype(jnp.float32) for weight_item in (gain_one, w_qkv, w_out, gain_two, w_up, w_down)))
    full_shape = tokens.shape
    flat_inputs = tokens.reshape(-1, full_shape[2], full_shape[3])
    flat_cotangent = cotangent.reshape(-1, full_shape[2], full_shape[3])

    def one_sequence(running, sequence_pair):
        seq_inputs, seq_cotangent = sequence_pair
        seq_result, pullback = jax.vjp(forward, seq_inputs.astype(jnp.float32), *params)
        gradients = pullback(seq_cotangent.astype(jnp.float32))
        running = tuple((total_item + grad_item for total_item, grad_item in zip(running, gradients[1:])))
        return (running, (seq_result.astype(jnp.bfloat16), gradients[0]))
    zeros_init = tuple((jnp.zeros(weight_item.shape, jnp.float32) for weight_item in params))
    running, outputs = lax.scan(one_sequence, zeros_init, (flat_inputs, flat_cotangent))
    seq_results, seq_grads = outputs
    return (seq_results.reshape(full_shape), seq_grads.reshape(full_shape), running[0], running[1], running[2], running[3], running[4], running[5])
```

```python
import functools

import jax
import jax.numpy as jnp
from jax import lax
from jax.experimental import pallas as pl
from jax.experimental.pallas import tpu as pltpu
from jax.sharding import PartitionSpec as P

D = 768
HEADS = 12
HEAD_DIM = 64


EPSILON = 1e-05


def passed_along(value, axis, by):
    count = lax.axis_size(axis)
    return lax.ppermute(value, axis, [(i, (i + by) % count) for i in range(count)])


def layer_norm(inputs, scaling):
    centred = inputs - jnp.mean(inputs, axis=-1, keepdims=True)
    variance = jnp.mean(centred * centred, axis=-1, keepdims=True)
    return centred * lax.rsqrt(variance + EPSILON) * scaling


def gelu_smooth(values_in):
    return jax.nn.gelu(values_in, approximate=True)


def contract_rows(left_side, right_side):
    return lax.dot_general(
        left_side, right_side, (((0,), (0,)), ((), ())), preferred_element_type=jnp.float32
    )


def times_rows(left_side, right_side):
    return lax.dot_general(
        left_side, right_side, (((1,), (1,)), ((), ())), preferred_element_type=jnp.float32
    )


def pair_grads(query_h, dout_h, log_total, row_delta, query_pos, key_h, value_h, key_pos):
    scaling = HEAD_DIM ** (-0.5)
    scores = (
        jnp.einsum("qhe,khe->hqk", query_h, key_h, preferred_element_type=jnp.float32) * scaling
    )
    visible = key_pos[None, None, :] <= query_pos[None, :, None]
    magnitude = jnp.sqrt(scores * scores + 1.0)
    tilted = scores / magnitude
    chance = jnp.exp(jnp.where(visible, magnitude - log_total[:, :, None], -1e30))
    signed = (tilted * chance).astype(jnp.bfloat16)
    d_signed = jnp.einsum("qhe,khe->hqk", dout_h, value_h, preferred_element_type=jnp.float32)
    slope = 1.0 / (magnitude * magnitude * magnitude) + tilted * tilted
    d_scores = (chance * (d_signed * slope - tilted * row_delta[:, :, None])).astype(jnp.bfloat16)
    d_query = (
        jnp.einsum("hqk,khe->qhe", d_scores, key_h, preferred_element_type=jnp.float32) * scaling
    )
    d_key = (
        jnp.einsum("hqk,qhe->khe", d_scores, query_h, preferred_element_type=jnp.float32) * scaling
    )
    d_value = jnp.einsum("hqk,qhe->khe", signed, dout_h, preferred_element_type=jnp.float32)
    return (d_query, d_key, d_value)


def keep_state(loop_state):
    return loop_state


def local_any(tokens, gain_one, w_qkv, w_out, gain_two, w_up, w_down, cotangent):
    gathered = (
        lax.all_gather(gain_one, "wshard", axis=0, tiled=True),
        lax.all_gather(w_qkv, "wshard", axis=0, tiled=True),
        lax.all_gather(w_out, "wshard", axis=0, tiled=True),
        lax.all_gather(gain_two, "wshard", axis=0, tiled=True),
        lax.all_gather(w_up, "wshard", axis=0, tiled=True),
        lax.all_gather(w_down, "wshard", axis=0, tiled=True),
    )
    full_gain_one, full_qkv, full_out, full_gain_two, full_up, full_down = gathered
    gain_first = full_gain_one.astype(jnp.float32)
    gain_second = full_gain_two.astype(jnp.float32)
    cycle_size = lax.axis_size("ctx")
    cycle_place = lax.axis_index("ctx")
    micro_count = tokens.shape[0]
    local_len = tokens.shape[2]
    scaling = HEAD_DIM ** (-0.5)
    query_pos = cycle_place * local_len + jnp.arange(local_len, dtype=jnp.int32)
    sum_gain_one = jnp.zeros((D,), jnp.float32)
    sum_gain_two = jnp.zeros((D,), jnp.float32)
    sum_qkv = jnp.zeros(full_qkv.shape, jnp.float32)
    sum_out = jnp.zeros(full_out.shape, jnp.float32)
    sum_up = jnp.zeros(full_up.shape, jnp.float32)
    sum_down = jnp.zeros(full_down.shape, jnp.float32)
    results = []
    grad_list = []
    for micro_index in range(micro_count):
        inputs = tokens[micro_index, 0].astype(jnp.float32)
        normed_f, norm_back = jax.vjp(layer_norm, inputs, gain_first)
        normed = normed_f.astype(jnp.bfloat16)
        mixed_all = jnp.dot(normed, full_qkv, preferred_element_type=jnp.float32).astype(
            jnp.bfloat16
        )
        keys_flat = mixed_all[:, D : 2 * D]
        values_flat = mixed_all[:, 2 * D :]
        query_h = mixed_all[:, :D].reshape(local_len, HEADS, HEAD_DIM)
        key_h = keys_flat.reshape(local_len, HEADS, HEAD_DIM)
        value_h = values_flat.reshape(local_len, HEADS, HEAD_DIM)
        start_state = (
            jnp.zeros((HEADS, local_len, HEAD_DIM), jnp.float32),
            jnp.ones((HEADS, local_len), jnp.float32),
            jnp.zeros((HEADS, local_len), jnp.float32),
        )
        shard_piece = (
            lax.all_gather(keys_flat, "ctx", axis=0, tiled=True),
            lax.all_gather(values_flat, "ctx", axis=0, tiled=True),
        )

        def compute(loop_state):
            accumulated, top_value, totals = loop_state
            key_piece = shard_piece[0].reshape(-1, HEADS, HEAD_DIM)
            value_piece = shard_piece[1].reshape(-1, HEADS, HEAD_DIM)
            key_pos = jnp.arange(key_piece.shape[0], dtype=jnp.int32)
            scores = (
                jnp.einsum("qhe,khe->hqk", query_h, key_piece, preferred_element_type=jnp.float32)
                * scaling
            )
            visible = key_pos[None, None, :] <= query_pos[None, :, None]
            magnitude = jnp.sqrt(scores * scores + 1.0)
            new_top = jnp.maximum(top_value, jnp.max(jnp.where(visible, magnitude, 0.0), axis=-1))
            weighted = jnp.exp(jnp.where(visible, magnitude - new_top[:, :, None], -1e30))
            signed = (scores / magnitude * weighted).astype(jnp.bfloat16)
            accumulated = jnp.einsum(
                "hqk,khe->hqe", signed, value_piece, preferred_element_type=jnp.float32
            )
            totals = jnp.sum(weighted, axis=-1)
            return (accumulated, new_top, totals)

        accumulated, top_value, totals = lax.cond(
            jnp.int32(0) <= query_pos[-1], compute, keep_state, start_state
        )
        attended_h = accumulated / totals[:, :, None]
        log_total = top_value + jnp.log(totals)
        attended = jnp.transpose(attended_h, (1, 0, 2)).reshape(local_len, D)
        attended_low = attended.astype(jnp.bfloat16)
        hidden = inputs + jnp.dot(attended_low, full_out, preferred_element_type=jnp.float32)
        normed_two_f, norm_two_back = jax.vjp(layer_norm, hidden, gain_second)
        normed_two = normed_two_f.astype(jnp.bfloat16)
        upward = jnp.dot(normed_two, full_up, preferred_element_type=jnp.float32)
        active_f, gelu_back = jax.vjp(gelu_smooth, upward)
        active = active_f.astype(jnp.bfloat16)
        result_rows = hidden + jnp.dot(active, full_down, preferred_element_type=jnp.float32)
        results.append(result_rows.astype(jnp.bfloat16))
        d_result = cotangent[micro_index, 0]
        sum_down = sum_down + contract_rows(active, d_result)
        d_active = times_rows(d_result, full_down)
        d_upward = gelu_back(d_active)[0].astype(jnp.bfloat16)
        sum_up = sum_up + contract_rows(normed_two, d_upward)
        d_normed_two = times_rows(d_upward, full_up)
        d_hidden_norm, d_gain_two = norm_two_back(d_normed_two)
        sum_gain_two = sum_gain_two + d_gain_two
        d_hidden = d_result.astype(jnp.float32) + d_hidden_norm
        d_branch = d_hidden.astype(jnp.bfloat16)
        sum_out = sum_out + contract_rows(attended_low, d_branch)
        d_attended = times_rows(d_branch, full_out).astype(jnp.bfloat16)
        dout_h = d_attended.reshape(local_len, HEADS, HEAD_DIM)
        row_delta = jnp.einsum("qhe,hqe->hq", dout_h.astype(jnp.float32), attended_h)
        zero_block = jnp.zeros((local_len, HEADS, HEAD_DIM), jnp.float32)

        def turn_keys(turn_index, loop_state):
            key_b, value_b, d_key_b, d_value_b, d_query = loop_state
            owner_index = (cycle_place + turn_index) % cycle_size
            key_pos = owner_index * local_len + jnp.arange(local_len, dtype=jnp.int32)

            def work(partial_sums):
                contrib = pair_grads(
                    query_h, dout_h, log_total, row_delta, query_pos, key_b, value_b, key_pos
                )
                return (
                    partial_sums[0] + contrib[0],
                    partial_sums[1] + contrib[1],
                    partial_sums[2] + contrib[2],
                )

            needed = (turn_index == 0) | (cycle_place + turn_index >= cycle_size)
            d_query, d_key_b, d_value_b = lax.cond(
                needed, work, keep_state, (d_query, d_key_b, d_value_b)
            )
            key_b, value_b = passed_along((key_b, value_b), "ctx", -1)
            d_key_b, d_value_b = (
                passed_along(d_key_b.astype(jnp.bfloat16), "ctx", -1).astype(d_key_b.dtype),
                passed_along(d_value_b.astype(jnp.bfloat16), "ctx", -1).astype(d_value_b.dtype),
            )
            return (key_b, value_b, d_key_b, d_value_b, d_query)

        final_state = lax.fori_loop(
            0, cycle_size, turn_keys, (key_h, value_h, zero_block, zero_block, zero_block)
        )
        d_key = final_state[2]
        d_value = final_state[3]
        d_query = final_state[4]
        d_mixed = jnp.concatenate(
            [
                d_query.reshape(local_len, D),
                d_key.reshape(local_len, D),
                d_value.reshape(local_len, D),
            ],
            axis=1,
        ).astype(jnp.bfloat16)
        sum_qkv = sum_qkv + contract_rows(normed, d_mixed)
        d_normed = times_rows(d_mixed, full_qkv)
        d_inputs_norm, d_gain_one = norm_back(d_normed)
        sum_gain_one = sum_gain_one + d_gain_one
        grad_list.append(d_hidden + d_inputs_norm)
    shares = (
        lax.psum_scatter(
            sum_gain_one.astype(jnp.bfloat16), "wshard", scatter_dimension=0, tiled=True
        ).astype(jnp.float32),
        lax.psum_scatter(
            sum_qkv.astype(jnp.bfloat16), "wshard", scatter_dimension=0, tiled=True
        ).astype(jnp.float32),
        lax.psum_scatter(
            sum_out.astype(jnp.bfloat16), "wshard", scatter_dimension=0, tiled=True
        ).astype(jnp.float32),
        lax.psum_scatter(
            sum_gain_two.astype(jnp.bfloat16), "wshard", scatter_dimension=0, tiled=True
        ).astype(jnp.float32),
        lax.psum_scatter(
            sum_up.astype(jnp.bfloat16), "wshard", scatter_dimension=0, tiled=True
        ).astype(jnp.float32),
        lax.psum_scatter(
            sum_down.astype(jnp.bfloat16), "wshard", scatter_dimension=0, tiled=True
        ).astype(jnp.float32),
    )
    summed = (
        lax.psum(shares[0].astype(jnp.bfloat16), "ctx").astype(jnp.float32),
        lax.psum(shares[1].astype(jnp.bfloat16), "ctx").astype(jnp.float32),
        lax.psum(shares[2].astype(jnp.bfloat16), "ctx").astype(jnp.float32),
        lax.psum(shares[3].astype(jnp.bfloat16), "ctx").astype(jnp.float32),
        lax.psum(shares[4].astype(jnp.bfloat16), "ctx").astype(jnp.float32),
        lax.psum(shares[5].astype(jnp.bfloat16), "ctx").astype(jnp.float32),
    )
    result_out = jnp.stack(results)[:, None]
    grad_out_tokens = jnp.stack(grad_list)[:, None]
    return (
        result_out,
        grad_out_tokens,
        summed[0],
        summed[1],
        summed[2],
        summed[3],
        summed[4],
        summed[5],
    )


BF = jnp.bfloat16
F32 = jnp.float32
TILE = 256
VMEM_LIMIT = 56 * 1024 * 1024


def nn(a, b):
    return lax.dot_general(a, b, (((1,), (0,)), ((), ())), preferred_element_type=F32)


def nt(a, b):
    return lax.dot_general(a, b, (((1,), (1,)), ((), ())), preferred_element_type=F32)


def tn(a, b):
    return lax.dot_general(a, b, (((0,), (0,)), ((), ())), preferred_element_type=F32)


def normalised(x):
    centred = x - jnp.mean(x, axis=-1, keepdims=True)
    variance = jnp.mean(centred * centred, axis=-1, keepdims=True)
    inverse = lax.rsqrt(variance + EPSILON)
    return centred * inverse, inverse


def norm_back(xhat, inverse, gain, dy):
    g = dy * gain
    mean_g = jnp.mean(g, axis=-1, keepdims=True)
    mean_gx = jnp.mean(g * xhat, axis=-1, keepdims=True)
    return (g - mean_g - xhat * mean_gx) * inverse


def causal_tile():
    rows = lax.broadcasted_iota(jnp.int32, (TILE, TILE), 0)
    cols = lax.broadcasted_iota(jnp.int32, (TILE, TILE), 1)
    return rows <= cols


def attend_kernel(x_ref, gain_ref, w_ref, normed_ref, kv_ref, mixt_ref, att_ref, low_ref, lse_ref, s_ref):
    length = x_ref.shape[0]

    @pl.when(pl.program_id(0) == 0)
    def _():
        for row in range(0, length, TILE):
            xhat, _ = normalised(x_ref[row : row + TILE, :].astype(F32))
            normed_ref[row : row + TILE, :] = (xhat * gain_ref[...]).astype(BF)

    mix = nn(normed_ref[...], w_ref[0]).astype(BF)
    kv_ref[0] = mix[:, HEAD_DIM:]
    mixt_ref[0] = mix.T
    keys = mix[:, HEAD_DIM : 2 * HEAD_DIM]
    for block in range(length // TILE):
        here = slice(block * TILE, (block + 1) * TILE)
        queries = mixt_ref[0, 0:HEAD_DIM, here] * BF(HEAD_DIM**-0.5)
        top = jnp.zeros((1, TILE), F32)
        for other in range(block + 1):
            there = slice(other * TILE, (other + 1) * TILE)
            s = nn(keys[there, :], queries)
            s_ref[there, :] = s
            size = jnp.abs(s)
            if other == block:
                size = jnp.where(causal_tile(), size, 0.0)
            top = jnp.maximum(top, jnp.max(size, axis=0, keepdims=True))
        top = jnp.sqrt(top * top + 1.0)
        total = jnp.zeros((1, TILE), F32)
        acc = jnp.zeros((HEAD_DIM, TILE), F32)
        for other in range(block + 1):
            there = slice(other * TILE, (other + 1) * TILE)
            s = s_ref[there, :]
            square = s * s + 1.0
            r = lax.rsqrt(square)
            p = jnp.exp(square * r - top)
            if other == block:
                p = jnp.where(causal_tile(), p, 0.0)
            total = total + jnp.sum(p, axis=0, keepdims=True)
            signed = (s * r * p).astype(BF)
            acc = acc + nn(mixt_ref[0, 2 * HEAD_DIM :, there], signed)
        att = acc / total
        att_ref[0, :, here] = att
        low_ref[0, :, here] = att.astype(BF)
        lse_ref[0, :, here] = top + jnp.log(total)


def attend(x, gain, w):
    length, heads = x.shape[0], w.shape[0]
    whole = lambda h: (0, 0)
    head = lambda h: (h, 0, 0)
    return pl.pallas_call(
        attend_kernel,
        grid=(heads,),
        in_specs=[
            pl.BlockSpec((length, D), whole),
            pl.BlockSpec((1, D), whole),
            pl.BlockSpec((1, D, 3 * HEAD_DIM), head),
        ],
        out_specs=[
            pl.BlockSpec((length, D), whole),
            pl.BlockSpec((1, length, 2 * HEAD_DIM), head),
            pl.BlockSpec((1, 3 * HEAD_DIM, length), head),
            pl.BlockSpec((1, HEAD_DIM, length), head),
            pl.BlockSpec((1, HEAD_DIM, length), head),
            pl.BlockSpec((1, 1, length), head),
        ],
        out_shape=[
            jax.ShapeDtypeStruct((length, D), BF),
            jax.ShapeDtypeStruct((heads, length, 2 * HEAD_DIM), BF),
            jax.ShapeDtypeStruct((heads, 3 * HEAD_DIM, length), BF),
            jax.ShapeDtypeStruct((heads, HEAD_DIM, length), F32),
            jax.ShapeDtypeStruct((heads, HEAD_DIM, length), BF),
            jax.ShapeDtypeStruct((heads, 1, length), F32),
        ],
        scratch_shapes=[pltpu.VMEM((length, TILE), F32)],
        compiler_params=pltpu.CompilerParams(vmem_limit_bytes=VMEM_LIMIT),
        cost_estimate=pl.CostEstimate(flops=3 * 10**9, bytes_accessed=6 * 10**6, transcendentals=4 * 10**6),
        name="attend",
    )(x, gain, w)


def attend_back_kernel(kv_ref, mixt_ref, att_ref, lse_ref, dout_ref, dmix_ref, dq_ref, dk_ref, dv_ref):
    length = kv_ref.shape[1]
    scale = BF(HEAD_DIM**-0.5)
    keys = kv_ref[0, :, :HEAD_DIM]
    values = kv_ref[0, :, HEAD_DIM:]
    for block in range(length // TILE):
        here = slice(block * TILE, (block + 1) * TILE)
        queries = mixt_ref[0, 0:HEAD_DIM, here] * scale
        dout = dout_ref[0, :, here]
        delta = jnp.sum(dout.astype(F32) * att_ref[0, :, here], axis=0, keepdims=True)
        lse = lse_ref[0, :, here]
        acc = jnp.zeros((HEAD_DIM, TILE), F32)
        for other in range(block + 1):
            there = slice(other * TILE, (other + 1) * TILE)
            s = nn(keys[there, :], queries)
            ds = nn(values[there, :], dout)
            square = s * s + 1.0
            r = lax.rsqrt(square)
            chance = jnp.exp(square * r - lse)
            if other == block:
                chance = jnp.where(causal_tile(), chance, 0.0)
            tilted = s * r
            signed = (tilted * chance).astype(BF)
            slope = r * r * r + tilted * tilted
            dsc = (chance * (ds * slope - tilted * delta)).astype(BF)
            acc = acc + nn(mixt_ref[0, HEAD_DIM : 2 * HEAD_DIM, there], dsc)
            dk = nt(dsc, queries)
            dv = nt(signed, dout)
            if other == block:
                dk_ref[there, :] = dk
                dv_ref[there, :] = dv
            else:
                dk_ref[there, :] += dk
                dv_ref[there, :] += dv
        dq_ref[:, here] = acc * HEAD_DIM**-0.5
    dmix_ref[0, :, 0:HEAD_DIM] = dq_ref[...].T.astype(BF)
    dmix_ref[0, :, HEAD_DIM : 2 * HEAD_DIM] = dk_ref[...].astype(BF)
    dmix_ref[0, :, 2 * HEAD_DIM :] = dv_ref[...].astype(BF)


def attend_back(kv, mixt, att, lse, dout):
    heads, length = kv.shape[0], kv.shape[1]
    head = lambda h: (h, 0, 0)
    return pl.pallas_call(
        attend_back_kernel,
        grid=(heads,),
        in_specs=[
            pl.BlockSpec((1, length, 2 * HEAD_DIM), head),
            pl.BlockSpec((1, 3 * HEAD_DIM, length), head),
            pl.BlockSpec((1, HEAD_DIM, length), head),
            pl.BlockSpec((1, 1, length), head),
            pl.BlockSpec((1, HEAD_DIM, length), head),
        ],
        out_specs=pl.BlockSpec((1, length, 3 * HEAD_DIM), head),
        out_shape=jax.ShapeDtypeStruct((heads, length, 3 * HEAD_DIM), BF),
        scratch_shapes=[
            pltpu.VMEM((HEAD_DIM, length), F32),
            pltpu.VMEM((length, HEAD_DIM), F32),
            pltpu.VMEM((length, HEAD_DIM), F32),
        ],
        compiler_params=pltpu.CompilerParams(vmem_limit_bytes=VMEM_LIMIT),
        cost_estimate=pl.CostEstimate(flops=3 * 10**9, bytes_accessed=6 * 10**6, transcendentals=4 * 10**6),
        name="attend_back",
    )(kv, mixt, att, lse, dout)


def pick(value, index, axis=0):
    return lax.dynamic_index_in_dim(value, index, axis, keepdims=False)


def across_w(value, flip):
    return lax.ppermute(value, "wshard", [(i, i ^ flip) for i in range(4)])


def across_core(value):
    return lax.ppermute(value, "ctx", [(i, i ^ 1) for i in range(8)])


def across_z(value, flip):
    return lax.ppermute(value, "ctx", [(i, i ^ (2 * flip)) for i in range(8)])


def along_z(value, by):
    return lax.ppermute(value, "ctx", [(i, i + 2 * by) for i in range(8) if 0 <= i + 2 * by < 8])


Z_GROUPS = [[0, 2, 4, 6], [1, 3, 5, 7]]


def gather_w(shard):
    place = lax.axis_index("wshard")
    half = shard.shape[0] // 2
    from_x = across_w(shard, 1)
    from_y = across_w(shard, 2)
    corner = jnp.concatenate([across_w(from_x[:half], 2), across_w(from_y[half:], 1)])
    stacked = jnp.stack([shard, from_x, from_y, corner])
    return jnp.stack([pick(stacked, place ^ j) for j in range(4)])


def gather_z(block):
    z = lax.axis_index("ctx") // 2
    up1, down1 = along_z(block, 1), along_z(block, -1)
    up2, down2 = along_z(up1, 1), along_z(down1, -1)
    up3, down3 = along_z(up2, 1), along_z(down2, -1)
    line = jnp.stack([up3, up2, up1, block, down1, down2, down3])
    return lax.dynamic_slice_in_dim(line, 3 - z, 4, 0)


def scatter_w(partial, x_first):
    place = lax.axis_index("wshard")
    y, x = place // 2, place % 2
    grid = partial.reshape((2, 2) + partial.shape[1:])
    if x_first:
        first = pick(grid, x, 1) + across_w(pick(grid, 1 - x, 1), 1)
        return pick(first, y) + across_w(pick(first, 1 - y), 2)
    first = pick(grid, y, 0) + across_w(pick(grid, 1 - y, 0), 2)
    return pick(first, x) + across_w(pick(first, 1 - x), 1)


def scatter_z(partial):
    z = lax.axis_index("ctx") // 2
    high, low = z // 2, z % 2
    grid = partial.reshape((2, 2) + partial.shape[1:])
    first = pick(grid, low, 1) + across_z(pick(grid, 1 - low, 1), 1)
    return pick(first, high) + across_z(pick(first, 1 - high), 2)


def unscatter_z(slot):
    z = lax.axis_index("ctx") // 2
    high, low = z // 2, z % 2
    other = across_z(slot, 2)
    pair = jnp.where(high == 0, jnp.stack([slot, other]), jnp.stack([other, slot]))
    far = across_z(pair, 1)
    return jnp.where(low == 0, jnp.stack([pair, far], 1), jnp.stack([far, pair], 1)).reshape((4,) + slot.shape)


def total_z(partial):
    rows = partial.shape[0] // 4
    return unscatter_z(scatter_z(partial.reshape((4, rows) + partial.shape[1:]))).reshape(partial.shape)


def local_grid(tokens, gain_one, w_qkv, w_out, gain_two, w_up, w_down, cotangent):
    core = lax.axis_index("ctx") % 2
    z = lax.axis_index("ctx") // 2
    block = tokens.shape[2]
    quarter = D // 4
    own_heads = HEADS // 4

    tok = tokens[:, 0]
    other_tok = across_core(pick(tok, 1 - core))
    own_tok = pick(tok, core)
    x_block = jnp.where(core == 0, jnp.concatenate([own_tok, other_tok]), jnp.concatenate([other_tok, own_tok]))
    x_all = gather_z(x_block).reshape(-1, D)

    shard_rows = w_qkv.shape[0]
    w_heads = pick(w_qkv.reshape(shard_rows, 3, 4, own_heads, HEAD_DIM), z, 2)
    w_heads = w_heads.transpose(2, 0, 1, 3).reshape(own_heads * shard_rows, 3 * HEAD_DIM)
    first = gather_w(jnp.concatenate([w_heads, gain_one[None], gain_two[None], jnp.zeros((14, quarter), BF)]))
    gains = first[:, own_heads * shard_rows :, :]
    gain_first = gains[:, 0].reshape(1, D).astype(F32)
    gain_second = gains[:, 1].reshape(1, D).astype(F32)
    w_heads = first[:, : own_heads * shard_rows].reshape(4, own_heads, shard_rows, 3 * HEAD_DIM)
    w_heads = w_heads.transpose(1, 0, 2, 3).reshape(own_heads, D, 3 * HEAD_DIM)

    full_out = gather_w(w_out).reshape(D, D)
    half = w_down.shape[0] // 2
    up_half = pick(w_up.reshape(shard_rows, 4, 2, half), core, 2).reshape(shard_rows, 4 * half)
    full_up = gather_w(up_half).reshape(D, 4 * half)
    full_down = gather_w(pick(w_down.reshape(2, half, D), core)).reshape(4 * half, D)

    cot = cotangent[:, 0]
    other_cot = across_core(cot)
    cots = jnp.where(core == 0, jnp.stack([cot, other_cot], 1), jnp.stack([other_cot, cot], 1))
    cots = cots.reshape(2, 2 * block, D)
    cot_mine = pick(cots, core)
    cot_both = jnp.concatenate([cot_mine, pick(cots, 1 - core)])

    normed_all, kv, mixt, att, att_low, lse = attend(x_all, gain_first, w_heads)
    att_home = lax.all_to_all(
        att_low.reshape(quarter, -1), "ctx", 1, 0, tiled=True, axis_index_groups=Z_GROUPS
    )

    x_own = x_block.astype(F32)
    hidden = x_own + tn(att_home, full_out)
    xhat_two, inverse_two = normalised(hidden)
    normed_two = (xhat_two * gain_second).astype(BF)
    normed_both = jnp.concatenate([normed_two, across_core(normed_two)])
    upward = nn(normed_both, full_up)
    active_f, gelu_back = jax.vjp(gelu_smooth, upward)
    active = active_f.astype(BF)
    down = nn(active, full_down)
    rows = 2 * block
    result = hidden + down[:rows] + across_core(down[rows:].astype(BF)).astype(F32)
    result = result.astype(BF)

    grad_down = tn(active, cot_both).astype(BF)
    d_upward = gelu_back(nt(cot_both, full_down))[0].astype(BF)
    d_normed = nt(d_upward, full_up)
    grad_up = tn(normed_both, d_upward).astype(BF)
    d_normed_two = d_normed[:rows] + across_core(d_normed[rows:].astype(BF)).astype(F32)
    d_gain_two = jnp.sum(d_normed_two * xhat_two, axis=0)
    d_hidden = cot_mine.astype(F32) + norm_back(xhat_two, inverse_two, gain_second, d_normed_two)
    d_branch = d_hidden.astype(BF)
    d_att = nt(full_out, d_branch).astype(BF)
    dout = lax.all_to_all(d_att, "ctx", 0, 1, tiled=True, axis_index_groups=Z_GROUPS)
    grad_out = nn(att_home, d_branch).astype(BF)

    d_mix = attend_back(kv, mixt, att, lse, dout.reshape(own_heads, HEAD_DIM, -1))
    d_first = sum(nt(d_mix[h], w_heads[h]) for h in range(own_heads))
    xhat_all, _ = normalised(x_all.astype(F32))
    d_gain_one = jnp.sum(d_first * xhat_all, axis=0)
    grad_heads = jnp.stack([tn(normed_all, d_mix[h]) for h in range(own_heads)]).astype(BF)
    d_first = scatter_z(d_first.astype(BF).reshape(4, rows, D)).astype(F32)
    xhat_one, inverse_one = normalised(x_own)
    grad_tok = d_hidden + norm_back(xhat_one, inverse_one, gain_first, d_first)

    sum_up = total_z(scatter_w(grad_up.reshape(4, shard_rows, 4 * half), True))
    sum_down = total_z(scatter_w(grad_down.reshape(4, half, D), False))
    other_up, other_down = across_core(sum_up), across_core(sum_down)
    pair_up = jnp.where(core == 0, jnp.stack([sum_up, other_up]), jnp.stack([other_up, sum_up]))
    out_up = pair_up.reshape(2, shard_rows, 4, half).transpose(1, 2, 0, 3).reshape(shard_rows, 8 * half).astype(F32)
    pair_down = jnp.where(core == 0, jnp.stack([sum_down, other_down]), jnp.stack([other_down, sum_down]))
    out_down = pair_down.reshape(2 * half, D).astype(F32)

    part = shard_rows // 2
    grid_out = grad_out.reshape(4, 2, part, D)
    sum_out = pick(grid_out, core, 1) + across_core(pick(grid_out, 1 - core, 1))
    sum_out = total_z(scatter_w(sum_out, True))
    other_out = across_core(sum_out)
    out_out = jnp.where(core == 0, jnp.concatenate([sum_out, other_out]), jnp.concatenate([other_out, sum_out]))
    out_out = out_out.astype(F32)

    grid_heads = grad_heads.reshape(own_heads, 4, 2, part, 3 * HEAD_DIM).transpose(1, 2, 0, 3, 4)
    grid_heads = grid_heads.reshape(4, 2, own_heads * part, 3 * HEAD_DIM)
    extra = jnp.stack([d_gain_one, d_gain_two]).astype(BF).reshape(2, 4, quarter).transpose(1, 0, 2)
    extra = jnp.stack([extra, jnp.zeros_like(extra)], 1)
    extra = jnp.pad(extra, ((0, 0), (0, 0), (0, 14), (0, 0)))
    both = jnp.concatenate([grid_heads, extra], 2)
    sum_heads = pick(both, core, 1) + across_core(pick(both, 1 - core, 1))
    sum_heads = gather_z(scatter_w(sum_heads, False))
    other_heads = across_core(sum_heads)
    pair = jnp.where(core == 0, jnp.stack([sum_heads, other_heads]), jnp.stack([other_heads, sum_heads]))
    pair = pair.astype(F32)
    out_gains = jnp.sum(pair[0, :, own_heads * part :], axis=0)
    heads_out = pair[:, :, : own_heads * part].reshape(2, 4, own_heads, part, 3, HEAD_DIM)
    out_qkv = heads_out.transpose(0, 3, 4, 1, 2, 5).reshape(shard_rows, 3 * D)

    result = result.reshape(2, block, D)
    grad_tok = grad_tok.reshape(2, block, D)
    result_kept, result_got = pick(result, core), across_core(pick(result, 1 - core))
    grad_kept, grad_got = pick(grad_tok, core), across_core(pick(grad_tok, 1 - core))
    out_result = jnp.where(core == 0, jnp.stack([result_kept, result_got]), jnp.stack([result_got, result_kept]))
    out_tokens = jnp.where(core == 0, jnp.stack([grad_kept, grad_got]), jnp.stack([grad_got, grad_kept]))
    return (
        out_result[:, None],
        out_tokens[:, None],
        out_gains[0],
        out_qkv,
        out_out,
        out_gains[1],
        out_up,
        out_down,
    )


def local(tokens, *rest):
    fits = (
        lax.axis_size("wshard") == 4
        and lax.axis_size("ctx") == 8
        and tokens.shape[:2] == (2, 1)
        and tokens.shape[2] % 128 == 0
    )
    return (local_grid if fits else local_any)(tokens, *rest)


def solution(mesh):
    placed = (
        P(None, "wshard", "ctx", None),
        P("wshard"),
        P("wshard", None),
        P("wshard", None),
        P("wshard"),
        P("wshard", None),
        P("wshard", None),
        P(None, "wshard", "ctx", None),
    )
    return jax.shard_map(
        local,
        mesh=mesh,
        in_specs=placed,
        out_specs=(
            P(None, "wshard", "ctx", None),
            P(None, "wshard", "ctx", None),
            P("wshard"),
            P("wshard", None),
            P("wshard", None),
            P("wshard"),
            P("wshard", None),
            P("wshard", None),
        ),
        check_vma=False,
    )
```

```python
import jax
import jax.numpy as jnp
from jax import lax
from jax.experimental import pallas as pl
from jax.experimental.pallas import tpu as pltpu
from jax.sharding import PartitionSpec as P

D = 768
HEADS = 12
HEAD_DIM = 64


EPSILON = 1e-05


def passed_along(value, axis, by):
    count = lax.axis_size(axis)
    return lax.ppermute(value, axis, [(i, (i + by) % count) for i in range(count)])


def layer_norm(inputs, scaling):
    centred = inputs - jnp.mean(inputs, axis=-1, keepdims=True)
    variance = jnp.mean(centred * centred, axis=-1, keepdims=True)
    return centred * lax.rsqrt(variance + EPSILON) * scaling


def gelu_smooth(values_in):
    return jax.nn.gelu(values_in, approximate=True)


def contract_rows(left_side, right_side):
    return lax.dot_general(
        left_side, right_side, (((0,), (0,)), ((), ())), preferred_element_type=jnp.float32
    )


def times_rows(left_side, right_side):
    return lax.dot_general(
        left_side, right_side, (((1,), (1,)), ((), ())), preferred_element_type=jnp.float32
    )


def pair_grads(query_h, dout_h, log_total, row_delta, query_pos, key_h, value_h, key_pos):
    scaling = HEAD_DIM ** (-0.5)
    scores = (
        jnp.einsum("qhe,khe->hqk", query_h, key_h, preferred_element_type=jnp.float32) * scaling
    )
    visible = key_pos[None, None, :] <= query_pos[None, :, None]
    magnitude = jnp.sqrt(scores * scores + 1.0)
    tilted = scores / magnitude
    chance = jnp.exp(jnp.where(visible, magnitude - log_total[:, :, None], -1e30))
    signed = (tilted * chance).astype(jnp.bfloat16)
    d_signed = jnp.einsum("qhe,khe->hqk", dout_h, value_h, preferred_element_type=jnp.float32)
    slope = 1.0 / (magnitude * magnitude * magnitude) + tilted * tilted
    d_scores = (chance * (d_signed * slope - tilted * row_delta[:, :, None])).astype(jnp.bfloat16)
    d_query = (
        jnp.einsum("hqk,khe->qhe", d_scores, key_h, preferred_element_type=jnp.float32) * scaling
    )
    d_key = (
        jnp.einsum("hqk,qhe->khe", d_scores, query_h, preferred_element_type=jnp.float32) * scaling
    )
    d_value = jnp.einsum("hqk,qhe->khe", signed, dout_h, preferred_element_type=jnp.float32)
    return (d_query, d_key, d_value)


def keep_state(loop_state):
    return loop_state


def local_any(tokens, gain_one, w_qkv, w_out, gain_two, w_up, w_down, cotangent):
    gathered = (
        lax.all_gather(gain_one, "wshard", axis=0, tiled=True),
        lax.all_gather(w_qkv, "wshard", axis=0, tiled=True),
        lax.all_gather(w_out, "wshard", axis=0, tiled=True),
        lax.all_gather(gain_two, "wshard", axis=0, tiled=True),
        lax.all_gather(w_up, "wshard", axis=0, tiled=True),
        lax.all_gather(w_down, "wshard", axis=0, tiled=True),
    )
    full_gain_one, full_qkv, full_out, full_gain_two, full_up, full_down = gathered
    gain_first = full_gain_one.astype(jnp.float32)
    gain_second = full_gain_two.astype(jnp.float32)
    cycle_size = lax.axis_size("ctx")
    cycle_place = lax.axis_index("ctx")
    micro_count = tokens.shape[0]
    local_len = tokens.shape[2]
    scaling = HEAD_DIM ** (-0.5)
    query_pos = cycle_place * local_len + jnp.arange(local_len, dtype=jnp.int32)
    sum_gain_one = jnp.zeros((D,), jnp.float32)
    sum_gain_two = jnp.zeros((D,), jnp.float32)
    sum_qkv = jnp.zeros(full_qkv.shape, jnp.float32)
    sum_out = jnp.zeros(full_out.shape, jnp.float32)
    sum_up = jnp.zeros(full_up.shape, jnp.float32)
    sum_down = jnp.zeros(full_down.shape, jnp.float32)
    results = []
    grad_list = []
    for micro_index in range(micro_count):
        inputs = tokens[micro_index, 0].astype(jnp.float32)
        normed_f, norm_back = jax.vjp(layer_norm, inputs, gain_first)
        normed = normed_f.astype(jnp.bfloat16)
        mixed_all = jnp.dot(normed, full_qkv, preferred_element_type=jnp.float32).astype(
            jnp.bfloat16
        )
        keys_flat = mixed_all[:, D : 2 * D]
        values_flat = mixed_all[:, 2 * D :]
        query_h = mixed_all[:, :D].reshape(local_len, HEADS, HEAD_DIM)
        key_h = keys_flat.reshape(local_len, HEADS, HEAD_DIM)
        value_h = values_flat.reshape(local_len, HEADS, HEAD_DIM)
        start_state = (
            jnp.zeros((HEADS, local_len, HEAD_DIM), jnp.float32),
            jnp.ones((HEADS, local_len), jnp.float32),
            jnp.zeros((HEADS, local_len), jnp.float32),
        )
        shard_piece = (
            lax.all_gather(keys_flat, "ctx", axis=0, tiled=True),
            lax.all_gather(values_flat, "ctx", axis=0, tiled=True),
        )

        def compute(loop_state):
            accumulated, top_value, totals = loop_state
            key_piece = shard_piece[0].reshape(-1, HEADS, HEAD_DIM)
            value_piece = shard_piece[1].reshape(-1, HEADS, HEAD_DIM)
            key_pos = jnp.arange(key_piece.shape[0], dtype=jnp.int32)
            scores = (
                jnp.einsum("qhe,khe->hqk", query_h, key_piece, preferred_element_type=jnp.float32)
                * scaling
            )
            visible = key_pos[None, None, :] <= query_pos[None, :, None]
            magnitude = jnp.sqrt(scores * scores + 1.0)
            new_top = jnp.maximum(top_value, jnp.max(jnp.where(visible, magnitude, 0.0), axis=-1))
            weighted = jnp.exp(jnp.where(visible, magnitude - new_top[:, :, None], -1e30))
            signed = (scores / magnitude * weighted).astype(jnp.bfloat16)
            accumulated = jnp.einsum(
                "hqk,khe->hqe", signed, value_piece, preferred_element_type=jnp.float32
            )
            totals = jnp.sum(weighted, axis=-1)
            return (accumulated, new_top, totals)

        accumulated, top_value, totals = lax.cond(
            jnp.int32(0) <= query_pos[-1], compute, keep_state, start_state
        )
        attended_h = accumulated / totals[:, :, None]
        log_total = top_value + jnp.log(totals)
        attended = jnp.transpose(attended_h, (1, 0, 2)).reshape(local_len, D)
        attended_low = attended.astype(jnp.bfloat16)
        hidden = inputs + jnp.dot(attended_low, full_out, preferred_element_type=jnp.float32)
        normed_two_f, norm_two_back = jax.vjp(layer_norm, hidden, gain_second)
        normed_two = normed_two_f.astype(jnp.bfloat16)
        upward = jnp.dot(normed_two, full_up, preferred_element_type=jnp.float32)
        active_f, gelu_back = jax.vjp(gelu_smooth, upward)
        active = active_f.astype(jnp.bfloat16)
        result_rows = hidden + jnp.dot(active, full_down, preferred_element_type=jnp.float32)
        results.append(result_rows.astype(jnp.bfloat16))
        d_result = cotangent[micro_index, 0]
        sum_down = sum_down + contract_rows(active, d_result)
        d_active = times_rows(d_result, full_down)
        d_upward = gelu_back(d_active)[0].astype(jnp.bfloat16)
        sum_up = sum_up + contract_rows(normed_two, d_upward)
        d_normed_two = times_rows(d_upward, full_up)
        d_hidden_norm, d_gain_two = norm_two_back(d_normed_two)
        sum_gain_two = sum_gain_two + d_gain_two
        d_hidden = d_result.astype(jnp.float32) + d_hidden_norm
        d_branch = d_hidden.astype(jnp.bfloat16)
        sum_out = sum_out + contract_rows(attended_low, d_branch)
        d_attended = times_rows(d_branch, full_out).astype(jnp.bfloat16)
        dout_h = d_attended.reshape(local_len, HEADS, HEAD_DIM)
        row_delta = jnp.einsum("qhe,hqe->hq", dout_h.astype(jnp.float32), attended_h)
        zero_block = jnp.zeros((local_len, HEADS, HEAD_DIM), jnp.float32)

        def turn_keys(turn_index, loop_state):
            key_b, value_b, d_key_b, d_value_b, d_query = loop_state
            owner_index = (cycle_place + turn_index) % cycle_size
            key_pos = owner_index * local_len + jnp.arange(local_len, dtype=jnp.int32)

            def work(partial_sums):
                contrib = pair_grads(
                    query_h, dout_h, log_total, row_delta, query_pos, key_b, value_b, key_pos
                )
                return (
                    partial_sums[0] + contrib[0],
                    partial_sums[1] + contrib[1],
                    partial_sums[2] + contrib[2],
                )

            needed = (turn_index == 0) | (cycle_place + turn_index >= cycle_size)
            d_query, d_key_b, d_value_b = lax.cond(
                needed, work, keep_state, (d_query, d_key_b, d_value_b)
            )
            key_b, value_b = passed_along((key_b, value_b), "ctx", -1)
            d_key_b, d_value_b = (
                passed_along(d_key_b.astype(jnp.bfloat16), "ctx", -1).astype(d_key_b.dtype),
                passed_along(d_value_b.astype(jnp.bfloat16), "ctx", -1).astype(d_value_b.dtype),
            )
            return (key_b, value_b, d_key_b, d_value_b, d_query)

        final_state = lax.fori_loop(
            0, cycle_size, turn_keys, (key_h, value_h, zero_block, zero_block, zero_block)
        )
        d_key = final_state[2]
        d_value = final_state[3]
        d_query = final_state[4]
        d_mixed = jnp.concatenate(
            [
                d_query.reshape(local_len, D),
                d_key.reshape(local_len, D),
                d_value.reshape(local_len, D),
            ],
            axis=1,
        ).astype(jnp.bfloat16)
        sum_qkv = sum_qkv + contract_rows(normed, d_mixed)
        d_normed = times_rows(d_mixed, full_qkv)
        d_inputs_norm, d_gain_one = norm_back(d_normed)
        sum_gain_one = sum_gain_one + d_gain_one
        grad_list.append(d_hidden + d_inputs_norm)
    shares = (
        lax.psum_scatter(
            sum_gain_one.astype(jnp.bfloat16), "wshard", scatter_dimension=0, tiled=True
        ).astype(jnp.float32),
        lax.psum_scatter(
            sum_qkv.astype(jnp.bfloat16), "wshard", scatter_dimension=0, tiled=True
        ).astype(jnp.float32),
        lax.psum_scatter(
            sum_out.astype(jnp.bfloat16), "wshard", scatter_dimension=0, tiled=True
        ).astype(jnp.float32),
        lax.psum_scatter(
            sum_gain_two.astype(jnp.bfloat16), "wshard", scatter_dimension=0, tiled=True
        ).astype(jnp.float32),
        lax.psum_scatter(
            sum_up.astype(jnp.bfloat16), "wshard", scatter_dimension=0, tiled=True
        ).astype(jnp.float32),
        lax.psum_scatter(
            sum_down.astype(jnp.bfloat16), "wshard", scatter_dimension=0, tiled=True
        ).astype(jnp.float32),
    )
    summed = (
        lax.psum(shares[0].astype(jnp.bfloat16), "ctx").astype(jnp.float32),
        lax.psum(shares[1].astype(jnp.bfloat16), "ctx").astype(jnp.float32),
        lax.psum(shares[2].astype(jnp.bfloat16), "ctx").astype(jnp.float32),
        lax.psum(shares[3].astype(jnp.bfloat16), "ctx").astype(jnp.float32),
        lax.psum(shares[4].astype(jnp.bfloat16), "ctx").astype(jnp.float32),
        lax.psum(shares[5].astype(jnp.bfloat16), "ctx").astype(jnp.float32),
    )
    result_out = jnp.stack(results)[:, None]
    grad_out_tokens = jnp.stack(grad_list)[:, None]
    return (
        result_out,
        grad_out_tokens,
        summed[0],
        summed[1],
        summed[2],
        summed[3],
        summed[4],
        summed[5],
    )


BF = jnp.bfloat16
F32 = jnp.float32
TILE = 256
SHARD = D // 4
OWN_HEADS = HEADS // 4
OWN = OWN_HEADS * HEAD_DIM
MIX = 3 * OWN
HEAD_ROWS = 160
PART = SHARD // 2
QUART = SHARD // 4
HALF = D // 2
VMEM_LIMIT = 56 * 1024 * 1024
WHOLE = pl.BlockSpec(memory_space=pltpu.VMEM)
ANYWHERE = pl.BlockSpec(memory_space=pl.ANY)


def nn(a, b):
    return lax.dot_general(a, b, (((1,), (0,)), ((), ())), preferred_element_type=F32)


def nt(a, b):
    return lax.dot_general(a, b, (((1,), (1,)), ((), ())), preferred_element_type=F32)


def normalised(x):
    centred = x - jnp.mean(x, axis=-1, keepdims=True)
    variance = jnp.mean(centred * centred, axis=-1, keepdims=True)
    inverse = lax.rsqrt(variance + EPSILON)
    return centred * inverse, inverse


def norm_back(xhat, inverse, gain, dy):
    g = dy * gain
    mean_g = jnp.mean(g, axis=-1, keepdims=True)
    mean_gx = jnp.mean(g * xhat, axis=-1, keepdims=True)
    return (g - mean_g - xhat * mean_gx) * inverse


def causal_tile():
    rows = lax.broadcasted_iota(jnp.int32, (TILE, TILE), 0)
    cols = lax.broadcasted_iota(jnp.int32, (TILE, TILE), 1)
    return rows <= cols


def call(kernel, name, ins, outs, scratch, flops, args, out_specs=None):
    moved = sum(a.size * a.dtype.itemsize for a in args)
    return pl.pallas_call(
        kernel,
        in_specs=ins,
        out_specs=out_specs or [WHOLE] * len(outs),
        out_shape=[jax.ShapeDtypeStruct(shape, kind) for shape, kind in outs],
        scratch_shapes=scratch,
        compiler_params=pltpu.CompilerParams(vmem_limit_bytes=VMEM_LIMIT),
        cost_estimate=pl.CostEstimate(flops=1000, bytes_accessed=1000, transcendentals=0),
        name=name,
    )(*args)


def shard_rows_of(pieces, which, first, count):
    if which < 3:
        return pieces[which].at[pl.ds(first, count)]
    half = pieces[3].shape[0]
    if first < half:
        return pieces[3].at[pl.ds(first, count)]
    return pieces[4].at[pl.ds(first - half, count)]


def run_copies(pairs, sems):
    copies = [pltpu.make_async_copy(src, dst, sems.at[i]) for i, (src, dst) in enumerate(pairs)]
    for copy in copies:
        copy.start()
    for copy in copies:
        copy.wait()


def attend_kernel(own, pair, near, far, mid_near, mid_far, w0, w1, w2, w3, w4, gain_ref,
                  normed_ref, kv_ref, mixt_ref, att_ref, low_ref, lse_ref, wfull_ref, x_ref, s_ref, sems, wsems):
    z = lax.axis_index("ctx") // 2
    place = lax.axis_index("wshard")
    end = (z == 0) | (z == 3)
    near_slot = jnp.where(z < 2, 2, 1)
    far_slot = jnp.where(z < 2, 3, 0)

    def line_copies(do):
        do(pltpu.make_async_copy(own, x_ref.at[z], sems.at[0]))
        do(pltpu.make_async_copy(pair, x_ref.at[jnp.bitwise_xor(z, 1)], sems.at[1]))

        @pl.when(end)
        def _():
            do(pltpu.make_async_copy(near, x_ref.at[near_slot], sems.at[2]))
            do(pltpu.make_async_copy(far, x_ref.at[far_slot], sems.at[3]))

        @pl.when(jnp.logical_not(end))
        def _():
            do(pltpu.make_async_copy(mid_near, x_ref.at[near_slot], sems.at[2]))
            do(pltpu.make_async_copy(mid_far, x_ref.at[far_slot], sems.at[3]))

    line_copies(lambda copy: copy.start())
    pieces = (w0, w1, w2, w3, w4)
    half = w3.shape[0]
    pairs = []
    for k in range(4):
        to = pl.multiple_of(jnp.bitwise_xor(place, k) * SHARD, SHARD)
        if k < 3:
            pairs.append((shard_rows_of(pieces, k, 0, SHARD), wfull_ref.at[pl.ds(to, SHARD)]))
        else:
            pairs.append((w3, wfull_ref.at[pl.ds(to, half)]))
            pairs.append((w4.at[pl.ds(0, SHARD - half)], wfull_ref.at[pl.ds(to + half, SHARD - half)]))
    run_copies(pairs, wsems)
    line_copies(lambda copy: copy.wait())
    for row in range(4):
        here = slice(row * TILE, (row + 1) * TILE)
        xhat, _ = normalised(x_ref[row].astype(F32))
        normed = (xhat * gain_ref[...]).astype(BF)
        normed_ref[here, :] = normed
        mix = nn(normed, wfull_ref[...]).astype(BF)
        mixt_ref[:, here] = mix.T
        for h in range(OWN_HEADS):
            kv_ref[h, here, 0:HEAD_DIM] = mix[:, OWN + h * HEAD_DIM : OWN + (h + 1) * HEAD_DIM]
            kv_ref[h, here, HEAD_DIM:] = mix[:, 2 * OWN + h * HEAD_DIM : 2 * OWN + (h + 1) * HEAD_DIM]

    @pl.loop(0, OWN_HEADS)
    def _(h):
        base = pl.multiple_of(h * HEAD_DIM, HEAD_DIM)
        for block in range(4):
            here = slice(block * TILE, (block + 1) * TILE)
            queries = mixt_ref[pl.ds(base, HEAD_DIM), here] * BF(HEAD_DIM**-0.5)
            top = jnp.zeros((1, TILE), F32)
            for other in range(block + 1):
                there = slice(other * TILE, (other + 1) * TILE)
                s = nn(kv_ref[h, there, 0:HEAD_DIM], queries)
                s_ref[there, :] = s
                size = jnp.abs(s)
                if other == block:
                    size = jnp.where(causal_tile(), size, 0.0)
                top = jnp.maximum(top, jnp.max(size, axis=0, keepdims=True))
            top = jnp.sqrt(top * top + 1.0)
            total = jnp.zeros((1, TILE), F32)
            acc = jnp.zeros((HEAD_DIM, TILE), F32)
            for other in range(block + 1):
                there = slice(other * TILE, (other + 1) * TILE)
                s = s_ref[there, :]
                square = s * s + 1.0
                r = lax.rsqrt(square)
                p = jnp.exp(square * r - top)
                if other == block:
                    p = jnp.where(causal_tile(), p, 0.0)
                total = total + jnp.sum(p, axis=0, keepdims=True)
                signed = (s * r * p).astype(BF)
                acc = acc + nn(mixt_ref[pl.ds(2 * OWN + base, HEAD_DIM), there], signed)
            att = acc / total
            att_ref[pl.ds(base, HEAD_DIM), here] = att
            low_ref[block, pl.ds(base, HEAD_DIM), :] = att.astype(BF)
            lse_ref[pl.ds(h, 1), here] = top + jnp.log(total)


def attend(line, pieces, gain):
    length = 4 * TILE
    return call(
        attend_kernel,
        "attend",
        [ANYWHERE] * 11 + [WHOLE],
        [
            ((length, D), BF),
            ((OWN_HEADS, length, 2 * HEAD_DIM), BF),
            ((MIX, length), BF),
            ((OWN, length), F32),
            ((4, OWN, TILE), BF),
            ((8, length), F32),
            ((D, MIX), BF),
        ],
        [
            pltpu.VMEM((4, TILE, D), BF),
            pltpu.VMEM((length, TILE), F32),
            pltpu.SemaphoreType.DMA((4,)),
            pltpu.SemaphoreType.DMA((5,)),
        ],
        3 * 10**9,
        (*line, *pieces, gain),
    )


def project_kernel(att_ref, x_ref, gain_ref, b0, b1, b2, b3, hidden_ref, normed_ref, wout_ref, sems):
    place = lax.axis_index("wshard")
    pairs = []
    for k, (ref, first) in enumerate(((b0, TILE), (b1, TILE), (b2, TILE), (b3, b3.shape[0] - SHARD))):
        to = pl.multiple_of(jnp.bitwise_xor(place, k) * SHARD, SHARD)
        pairs.append((ref.at[pl.ds(first, SHARD)], wout_ref.at[pl.ds(to, SHARD)]))
    run_copies(pairs, sems)
    hidden = x_ref[...].astype(F32) + nn(att_ref[...].T, wout_ref[...])
    hidden_ref[...] = hidden
    xhat, _ = normalised(hidden)
    normed_ref[...] = (xhat * gain_ref[...]).astype(BF)


def project(att_home, x_block, gain, shared):
    rows = x_block.shape[0]
    own, from_x, from_y, _, low = shared
    return call(
        project_kernel,
        "project",
        [WHOLE] * 3 + [ANYWHERE] * 4,
        [((rows, D), F32), ((rows, D), BF), ((D, D), BF)],
        [pltpu.SemaphoreType.DMA((4,))],
        3 * 10**8,
        (att_home, x_block, gain, own, from_x, from_y, low),
    )


SLOPE = (2.0 / 3.141592653589793) ** 0.5


def feed_rows(n, cot, up_ref, down_ref, active_ref, dup_ref, here):
    for first in range(0, D, TILE):
        cols = slice(first, first + TILE)
        u = nn(n, up_ref[:, cols])
        square = u * u
        t = jnp.tanh(SLOPE * (u + 0.044715 * (square * u)))
        side = 0.5 + 0.5 * t
        active_ref[here, cols] = (u * side).astype(BF)
        grad = side + (0.5 * SLOPE) * u * (1.0 - t * t) * (1.0 + 0.134145 * square)
        dup_ref[here, cols] = (grad * nt(cot, down_ref[cols, :])).astype(BF)
    return nn(active_ref[here, :], down_ref[...]), nt(dup_ref[here, :], up_ref[...])


def feed_own_kernel(n_ref, cot_ref, up_ref, down_ref, active_ref, dup_ref, out_ref, dout_ref):
    out_ref[...], dout_ref[...] = feed_rows(
        n_ref[...], cot_ref[0:TILE, :], up_ref, down_ref, active_ref, dup_ref, slice(0, TILE)
    )


def feed_own(n, shared, up, down):
    return call(
        feed_own_kernel,
        "feed_own",
        [WHOLE] * 4,
        [((TILE, D), BF), ((TILE, D), BF), ((TILE, D), F32), ((TILE, D), F32)],
        [],
        2 * 10**9,
        (n, shared[0], up, down),
    )


def feed_near_kernel(nx_ref, ny_ref, cx_ref, cy_ref, up_ref, down_ref, active_ref, dup_ref, out_ref, dout_ref):
    for k, (n_ref, cot_ref) in enumerate(((nx_ref, cx_ref), (ny_ref, cy_ref))):
        here = slice(k * TILE, (k + 1) * TILE)
        out, dout = feed_rows(n_ref[...], cot_ref[0:TILE, :], up_ref, down_ref, active_ref, dup_ref, here)
        out_ref[here, :], dout_ref[here, :] = out.astype(BF), dout.astype(BF)


def feed_near(nx, ny, shared, up, down):
    return call(
        feed_near_kernel,
        "feed_near",
        [WHOLE] * 6,
        [((2 * TILE, D), BF)] * 4,
        [],
        4 * 10**9,
        (nx, ny, shared[1], shared[2], up, down),
    )


def feed_far_kernel(na_ref, nb_ref, ca_ref, cb_ref, out_ref, dout_ref, up_ref, down_ref,
                    active_ref, dup_ref, oa_ref, oaf_ref, ob_ref, obf_ref, da_ref, daf_ref, db_ref, dbf_ref):
    n = jnp.concatenate([na_ref[...], nb_ref[...]])
    first = ca_ref.shape[0]
    cot = jnp.concatenate([ca_ref[...], cb_ref[0 : TILE - first, :]])
    half = TILE // 2
    out, dout = feed_rows(n, cot, up_ref, down_ref, active_ref, dup_ref, slice(0, TILE))
    for far, near, a, af, b, bf in (
        (out, out_ref, oa_ref, oaf_ref, ob_ref, obf_ref),
        (dout, dout_ref, da_ref, daf_ref, db_ref, dbf_ref),
    ):
        far = far.astype(BF)
        a[0], a[1] = near[0:half, :], far[0:half]
        b[0], b[1] = near[TILE + half :, :], far[half:]
        af[...] = near[TILE : TILE + half, :]
        bf[...] = near[half:TILE, :]


def feed_far(na, nb, shared, out, dout, up, down):
    half = TILE // 2
    return call(
        feed_far_kernel,
        "feed_far",
        [WHOLE] * 8,
        [((TILE, D), BF)] * 2 + [((2, half, D), BF), ((half, D), BF)] * 4,
        [],
        2 * 10**9,
        (na, nb, shared[3], shared[4], out, dout, up, down),
    )


def feed_grads_kernel(n0, n1, n2, n3, n4, c0, c1, c2, c3, c4, a0, a1, a2, d0, d1, d2,
                      shares_ref, nt_ref, cot_ref, at_ref, dup_ref):
    first = c3.shape[0]
    for k, piece in enumerate((n0, n1, n2)):
        nt_ref[:, k * TILE : (k + 1) * TILE] = piece[...].T
    nt_ref[:, 3 * TILE :] = jnp.concatenate([n3[...], n4[...]]).T
    for k, piece in enumerate((c0, c1, c2)):
        cot_ref[k * TILE : (k + 1) * TILE] = piece[0:TILE, :]
    cot_ref[3 * TILE : 3 * TILE + first] = c3[...]
    cot_ref[3 * TILE + first :] = c4[0 : TILE - first, :]
    at_ref[:, 0:TILE] = a0[...].T
    at_ref[:, TILE : 3 * TILE] = a1[...].T
    at_ref[:, 3 * TILE :] = a2[...].T
    dup_ref[0:TILE] = d0[...]
    dup_ref[TILE : 3 * TILE] = d1[...]
    dup_ref[3 * TILE :] = d2[...]
    rows = D // 8
    for k in range(8):
        g = nn(at_ref[k * rows : (k + 1) * rows, :], cot_ref[...]).astype(BF)
        for side in range(2):
            shares_ref[k, SHARD + side * rows : SHARD + (side + 1) * rows] = g[:, side * HALF : (side + 1) * HALF]
    for to in range(4):
        g = nn(nt_ref[to * SHARD : (to + 1) * SHARD, :], dup_ref[...]).astype(BF)
        for k in range(8):
            r, c = (k // 2) * QUART, (k % 2) * HALF
            shares_ref[k, to * QUART : (to + 1) * QUART] = g[r : r + QUART, c : c + HALF]


def feed_grads(ns, shared, actives, dups):
    length = 4 * TILE
    return call(
        feed_grads_kernel,
        "feed_grads",
        [WHOLE] * 16,
        [((8, 2 * SHARD, HALF), BF)],
        [
            pltpu.VMEM((D, length), BF),
            pltpu.VMEM((length, D), BF),
            pltpu.VMEM((D, length), BF),
            pltpu.VMEM((length, D), BF),
        ],
        3 * 10**9,
        (*ns, *shared, *actives, *dups),
    )[0]


def summed(keep_ref, a_ref, a_more_ref, b_ref, b_more_ref):
    first = a_ref[0].astype(F32) + a_more_ref[...].astype(F32)
    second = b_ref[0].astype(F32) + b_more_ref[...].astype(F32)
    return keep_ref[...] + jnp.concatenate([first, second])


def give_kernel(hidden_ref, keep_ref, a_ref, a_more_ref, b_ref, b_more_ref, rkeep_ref, rsend_ref, result_ref, sems):
    core = lax.axis_index("ctx") % 2
    result = (hidden_ref[...] + summed(keep_ref, a_ref, a_more_ref, b_ref, b_more_ref)).astype(BF)
    half = TILE // 2
    result_ref[0], result_ref[1] = result[:half], result[half:]
    run_copies(((result_ref.at[1 - core], rsend_ref), (result_ref.at[core], rkeep_ref)), sems)


def give(hidden, keep, parts):
    half = TILE // 2
    return call(
        give_kernel,
        "give",
        [WHOLE] * 6,
        [((half, D), BF)] * 2,
        [pltpu.VMEM((2, half, D), BF), pltpu.SemaphoreType.DMA((2,))],
        10**6,
        (hidden, keep, *parts),
        [ANYWHERE] * 2,
    )


def turn_kernel(hidden_ref, gain_ref, dkeep_ref, a_ref, a_more_ref, b_ref, b_more_ref, cot_ref, wout_ref,
                dhidden_ref, datt_ref, dbranch_ref, dgain_ref):
    gain = gain_ref[...]
    xhat, inverse = normalised(hidden_ref[...])
    dy = summed(dkeep_ref, a_ref, a_more_ref, b_ref, b_more_ref)
    dgain_ref[...] = jnp.sum(dy * xhat, axis=0, keepdims=True)
    d_hidden = cot_ref[...].astype(F32) + norm_back(xhat, inverse, gain, dy)
    dhidden_ref[...] = d_hidden
    d_branch = d_hidden.astype(BF)
    dbranch_ref[...] = d_branch
    d_att = nt(wout_ref[...], d_branch).astype(BF)
    for k in range(4):
        datt_ref[k] = d_att[k * OWN : (k + 1) * OWN]


def turn(hidden, gain, dkeep, parts, cot, w_out):
    rows = hidden.shape[0]
    return call(
        turn_kernel,
        "turn",
        [WHOLE] * 9,
        [((rows, D), F32), ((4, OWN, rows), BF), ((rows, D), BF), ((1, D), F32)],
        [],
        6 * 10**8,
        (hidden, gain, dkeep, *parts, cot, w_out),
    )


def out_grad_kernel(att_ref, dbranch_ref, own_ref, far_ref, send_ref, grad_ref, sems):
    place = lax.axis_index("wshard")
    x, y = jnp.bitwise_and(place, 1), place // 2
    for to in range(4):
        g = nn(att_ref[to * SHARD : (to + 1) * SHARD, :], dbranch_ref[...])
        grad_ref[to % 2, to // 2] = g.astype(BF)
    pairs = (
        (grad_ref.at[1 - x, y], send_ref.at[0]),
        (grad_ref.at[1 - x, 1 - y], send_ref.at[1]),
        (grad_ref.at[x, 1 - y], far_ref),
        (grad_ref.at[x, y], own_ref),
    )
    run_copies(pairs, sems)


def out_grad(att_home, d_branch):
    return call(
        out_grad_kernel,
        "out_grad",
        [WHOLE] * 2,
        [((SHARD, D), BF), ((SHARD, D), BF), ((2, SHARD, D), BF)],
        [pltpu.VMEM((2, 2, SHARD, D), BF), pltpu.SemaphoreType.DMA((4,))],
        3 * 10**8,
        (att_home, d_branch),
        [ANYWHERE] * 3,
    )


def attend_back_kernel(kv_ref, mixt_ref, att_ref, lse_ref, dout_ref, normed_ref, w_ref, gain_ref, dgain_ref,
                       f0_ref, f1_ref, f2_ref, f3_ref, gkeep_ref, gsend_ref,
                       dq_ref, dk_ref, dv_ref, dm_ref, mix_ref, total_ref, first_ref, head_ref, sems):
    length = normed_ref.shape[0]
    scale = BF(HEAD_DIM**-0.5)
    core = lax.axis_index("ctx") % 2
    z = lax.axis_index("ctx") // 2
    place = lax.axis_index("wshard")

    @pl.loop(0, OWN_HEADS)
    def _(h):
        base = pl.multiple_of(h * HEAD_DIM, HEAD_DIM)
        for block in range(4):
            here = slice(block * TILE, (block + 1) * TILE)
            queries = mixt_ref[pl.ds(base, HEAD_DIM), here] * scale
            dout = dout_ref[block, pl.ds(base, HEAD_DIM), :]
            delta = jnp.sum(dout.astype(F32) * att_ref[pl.ds(base, HEAD_DIM), here], axis=0, keepdims=True)
            lse = lse_ref[pl.ds(h, 1), here]
            acc = jnp.zeros((HEAD_DIM, TILE), F32)
            for other in range(block + 1):
                there = slice(other * TILE, (other + 1) * TILE)
                s = nn(kv_ref[h, there, 0:HEAD_DIM], queries)
                ds = nn(kv_ref[h, there, HEAD_DIM:], dout)
                square = s * s + 1.0
                r = lax.rsqrt(square)
                chance = jnp.exp(square * r - lse)
                if other == block:
                    chance = jnp.where(causal_tile(), chance, 0.0)
                tilted = s * r
                signed = (tilted * chance).astype(BF)
                slope = r * r * r + tilted * tilted
                dsc = (chance * (ds * slope - tilted * delta)).astype(BF)
                acc = acc + nn(mixt_ref[pl.ds(OWN + base, HEAD_DIM), there], dsc)
                dk = nt(dsc, queries)
                dv = nt(signed, dout)
                if other == block:
                    dk_ref[there, :] = dk
                    dv_ref[there, :] = dv
                else:
                    dk_ref[there, :] += dk
                    dv_ref[there, :] += dv
            dq_ref[:, here] = acc * HEAD_DIM**-0.5
        dm_ref[h, :, 0:HEAD_DIM] = dq_ref[...].T.astype(BF)
        dm_ref[h, :, HEAD_DIM : 2 * HEAD_DIM] = dk_ref[...].astype(BF)
        dm_ref[h, :, 2 * HEAD_DIM :] = dv_ref[...].astype(BF)

    for h in range(OWN_HEADS):
        for kind in range(3):
            to = kind * OWN + h * HEAD_DIM
            mix_ref[:, to : to + HEAD_DIM] = dm_ref[h, :, kind * HEAD_DIM : (kind + 1) * HEAD_DIM]
    total_ref[...] = jnp.zeros_like(total_ref)
    for block in range(4):
        here = slice(block * TILE, (block + 1) * TILE)
        first = nt(mix_ref[here, :], w_ref[...])
        first_ref[block] = first.astype(BF)
        total_ref[...] += jnp.sum(first * normed_ref[here, :].astype(F32), axis=0, keepdims=True)
    outs = (f3_ref, f2_ref, f1_ref, f0_ref)
    copies = [
        pltpu.make_async_copy(first_ref.at[jnp.bitwise_xor(z, 3 - k)], ref, sems.at[k]) for k, ref in enumerate(outs)
    ]
    for copy in copies:
        copy.start()
    gain_one = total_ref[...] / gain_ref[...]
    gain_two = dgain_ref[...]
    for to in range(4):
        e = jnp.bitwise_xor(place, to)
        e_x, e_y = jnp.bitwise_and(e, 1), e // 2
        g = nn(normed_ref[:, to * SHARD : (to + 1) * SHARD].T, mix_ref[...]).astype(BF)
        span = slice(to * SHARD, (to + 1) * SHARD)
        gains = jnp.concatenate([gain_one[:, span], gain_two[:, span], jnp.zeros((14, SHARD), F32)], axis=0)
        gains = jnp.concatenate([gains, jnp.zeros((16, HALF - SHARD), F32)], axis=1).astype(BF)
        for side in range(2):
            at = side * PART
            head_ref[side, e_y, e_x, 0:PART] = g[at : at + PART, 0:HALF]
            head_ref[side, e_y, e_x, PART : PART + QUART, 0:OWN] = g[at : at + QUART, HALF:]
            head_ref[side, e_y, e_x, PART : PART + QUART, OWN:] = g[at + QUART : at + PART, HALF:]
            head_ref[side, e_y, e_x, PART + QUART :] = gains if side == 0 else jnp.zeros_like(gains)
    more = [
        pltpu.make_async_copy(head_ref.at[1 - core], gsend_ref, sems.at[4]),
        pltpu.make_async_copy(head_ref.at[core], gkeep_ref, sems.at[5]),
    ]
    for copy in more:
        copy.start()
    for copy in copies + more:
        copy.wait()


def attend_back(kv, mixt, att, lse, dout, normed, w, gain, dgain):
    length = normed.shape[0]
    return call(
        attend_back_kernel,
        "attend_back",
        [WHOLE] * 9,
        [((TILE, D), BF)] * 4 + [((2, 2, HEAD_ROWS, HALF), BF)] * 2,
        [
            pltpu.VMEM((HEAD_DIM, length), F32),
            pltpu.VMEM((length, HEAD_DIM), F32),
            pltpu.VMEM((length, HEAD_DIM), F32),
            pltpu.VMEM((OWN_HEADS, length, 3 * HEAD_DIM), BF),
            pltpu.VMEM((length, MIX), BF),
            pltpu.VMEM((1, D), F32),
            pltpu.VMEM((4, TILE, D), BF),
            pltpu.VMEM((2, 2, 2, HEAD_ROWS, HALF), BF),
            pltpu.SemaphoreType.DMA((6,)),
        ],
        5 * 10**9,
        (kv, mixt, att, lse, dout, normed, w, gain, dgain),
        [ANYWHERE] * 6,
    )


def is_inner():
    z = lax.axis_index("ctx") // 2
    return (z == 1) | (z == 2)


def last_kernel(first_ref, pair_ref, middle_ref, x_ref, gain_ref, dhidden_ref, keep_ref, send_ref, grad_ref, sems):
    core = lax.axis_index("ctx") % 2
    rows = x_ref.shape[0] // 2
    dy = first_ref[...].astype(F32) + pair_ref[...].astype(F32)
    dy = dy + jnp.where(is_inner(), middle_ref[...].astype(F32), 0.0)
    xhat, inverse = normalised(x_ref[...].astype(F32))
    grad = dhidden_ref[...] + norm_back(xhat, inverse, gain_ref[...], dy)
    grad_ref[0], grad_ref[1] = grad[:rows], grad[rows:]
    run_copies(((grad_ref.at[1 - core], send_ref), (grad_ref.at[core], keep_ref)), sems)


def last(*args):
    rows = TILE // 2
    return call(
        last_kernel,
        "last",
        [WHOLE] * 6,
        [((rows, D), F32), ((rows, D), F32)],
        [pltpu.VMEM((2, rows, D), F32), pltpu.SemaphoreType.DMA((2,))],
        10**7,
        args,
        [ANYWHERE] * 2,
    )


def finish_kernel(*refs):
    mine, theirs, (gup_ref, gdown_ref, gqkv_ref, gains_ref) = refs[:4], refs[4:8], refs[8:]
    core = lax.axis_index("ctx") % 2
    z = lax.axis_index("ctx") // 2
    rows = D // 8
    slots = (z, jnp.bitwise_xor(z, 1), jnp.where(z < 2, 2, 1), jnp.where(z < 2, 3, 0))
    for group, side in ((mine, core), (theirs, 1 - core)):
        for ref, slot in zip(group, slots):
            at = pl.multiple_of(slot * QUART, 16)
            for j in range(4):
                to = pl.multiple_of(j * D + side * HALF, 128)
                gup_ref[pl.ds(at, QUART), pl.ds(to, HALF)] = ref[j * QUART : (j + 1) * QUART].astype(F32)
            at = pl.multiple_of((2 * slot + side) * rows, 32)
            for half in range(2):
                share = ref[SHARD + half * rows : SHARD + (half + 1) * rows]
                gdown_ref[pl.ds(at, rows), half * HALF : (half + 1) * HALF] = share.astype(F32)
    first = core == 0
    mine, theirs = [[ref[2 * SHARD :].astype(F32) for ref in group] for group in (mine, theirs)]
    low = [jnp.where(first, a, b) for a, b in zip(mine, theirs)]
    high = [jnp.where(first, b, a) for a, b in zip(mine, theirs)]
    gains_ref[...] = sum(block[PART + QUART :, 0:SHARD] for block in low)
    for slot in range(4):
        for side, group in enumerate((low, high)):
            block = jnp.where(
                slot == z, group[0], jnp.where(slot == slots[1], group[1], jnp.where(slot == slots[2], group[2], group[3]))
            )
            at, to = side * PART, slot * OWN
            gqkv_ref[at : at + PART, to : to + OWN] = block[0:PART, 0:OWN]
            gqkv_ref[at : at + PART, D + to : D + to + OWN] = block[0:PART, OWN:]
            gqkv_ref[at : at + QUART, 2 * D + to : 2 * D + to + OWN] = block[PART : PART + QUART, 0:OWN]
            gqkv_ref[at + QUART : at + PART, 2 * D + to : 2 * D + to + OWN] = block[PART : PART + QUART, OWN:]


def finish(*args):
    return call(
        finish_kernel,
        "finish",
        [WHOLE] * 8,
        [((SHARD, 4 * D), F32), ((D, D), F32), ((SHARD, 3 * D), F32), ((16, SHARD), F32)],
        [],
        10**7,
        args,
    )


def pick(value, index, axis=0):
    return lax.dynamic_index_in_dim(value, index, axis, keepdims=False)


def across_w(value, flip):
    return lax.ppermute(value, "wshard", [(i, i ^ flip) for i in range(4)])


def across_core(value):
    return lax.ppermute(value, "ctx", [(i, i ^ 1) for i in range(8)])


def between_z(value, pairs):
    return lax.ppermute(value, "ctx", [(2 * a + c, 2 * b + c) for a, b in pairs for c in range(2)])


Z_GROUPS = [[0, 2, 4, 6], [1, 3, 5, 7]]


def after(value, *others):
    return lax.optimization_barrier((value, *others))[0]


PAIRS = [(0, 1), (1, 0), (2, 3), (3, 2)]
MIDDLE = [(1, 2), (2, 1), (0, 0), (3, 3)]


def line_z(block):
    pair = between_z(block, PAIRS)
    mid_near = between_z(block, MIDDLE)
    near = between_z(mid_near, PAIRS)
    mid_far = between_z(pair, MIDDLE)
    far = between_z(mid_far, PAIRS)
    return block, pair, near, far, mid_near, mid_far


TO_MIDDLE = [(0, 1), (3, 2)]
TO_ENDS = [(1, 0), (2, 3)]
ACROSS = [(1, 2), (2, 1)]


def own_slot(slots, x_first):
    one, two = (1, 2) if x_first else (2, 1)
    got = across_w(slots[1], one)
    far = slots[0, 1] + got[1]
    return (slots[0, 0] + got[0]) + across_w(far, two)


def gather_plane(block, *others):
    half = block.shape[0] // 2
    from_x, from_y = across_w(block, 1), across_w(block, 2)
    first, second = from_x[:half], from_y[half:]
    if others:
        first, second, *_ = tied(first, second, *others)
    return block, from_x, from_y, across_w(first, 2), across_w(second, 1)


def tied(*values):
    return lax.optimization_barrier(values)


def local_grid(tokens, gain_one, w_qkv, w_out, gain_two, w_up, w_down, cotangent):
    core = lax.axis_index("ctx") % 2
    z = lax.axis_index("ctx") // 2
    place = lax.axis_index("wshard")
    inner = (z == 1) | (z == 2)

    def both_micros(kept, got):
        return jnp.where(core == 0, jnp.stack([kept, got]), jnp.stack([got, kept]))[:, None]

    tok, cot = tokens[:, 0], cotangent[:, 0]
    kept = jnp.concatenate([pick(tok, core), pick(cot, core)])
    got = across_core(jnp.concatenate([pick(tok, 1 - core), pick(cot, 1 - core)]))
    half = TILE // 2
    own = [jnp.where(core == 0, a, b) for a, b in ((kept, got), (got, kept))]
    x_block = jnp.concatenate([own[0][:half], own[1][:half]])
    cot = jnp.concatenate([own[0][half:], own[1][half:]])

    w_heads = pick(w_qkv.reshape(SHARD, 3, 4, OWN), z, 2).reshape(SHARD, MIX)
    gains = jnp.pad(jnp.stack([gain_one, gain_two]), ((0, 30), (0, MIX - SHARD)))
    w_heads = after(jnp.concatenate([w_heads, gains]), x_block)
    pair, mid_near = between_z(x_block, PAIRS), between_z(x_block, MIDDLE)
    heads_x, heads_y = across_w(w_heads, 1), across_w(w_heads, 2)
    pair, mid_near, heads_x, heads_y = tied(pair, mid_near, heads_x, heads_y)
    near, mid_far = between_z(mid_near, PAIRS), between_z(pair, MIDDLE)
    middle = w_heads.shape[0] // 2
    heads = w_heads, heads_x, heads_y, across_w(heads_x[:middle], 2), across_w(heads_y[middle:], 1)
    far = between_z(mid_far, PAIRS)
    shared, *heads = tied(jnp.concatenate([cot, w_out]), *heads)
    shared_x, shared_y = across_w(shared, 1), across_w(shared, 2)
    line = x_block, pair, near, far, mid_near, mid_far
    up, *line = tied(w_up.reshape(SHARD, 4, D).transpose(1, 0, 2), *line)
    up = lax.all_to_all(up, "wshard", 0, 0, tiled=True).reshape(D, D)
    at = SHARD - heads[3].shape[0]
    gains = jnp.stack([heads[k][SHARD : SHARD + 2] for k in range(3)] + [heads[4][at : at + 2]])
    gains = gains[:, :, :SHARD].astype(F32)
    gains = jnp.concatenate([pick(gains, place ^ j) for j in range(4)], axis=1)
    gain_first, gain_second = gains[0:1], gains[1:2]

    normed_all, kv, mixt, att, att_low, lse, w_full = attend(line, heads, gain_first)
    att_low, up, shared_x, shared_y = tied(att_low, up, shared_x, shared_y)
    middle = shared.shape[0] // 2
    shared = shared, shared_x, shared_y, across_w(shared_x[:middle], 2), across_w(shared_y[middle:], 1)
    att_home = lax.all_to_all(att_low, "ctx", 0, 0, tiled=True, axis_index_groups=Z_GROUPS).reshape(D, -1)
    hidden, normed_two, wout_full = project(att_home, x_block, gain_second, shared)

    active0, dup0, out0, dout0 = feed_own(normed_two, shared, up, w_down)
    ns = gather_plane(normed_two, active0)
    active1, dup1, out1, dout1 = feed_near(ns[1], ns[2], shared, up, w_down)
    active2, dup2, *parts = feed_far(ns[3], ns[4], shared, out1, dout1, up, w_down)
    parts, (a, a_far, b, b_far) = parts[:4], parts[4:]
    got_a, got_b = across_w(a, 1), across_w(b, 2)
    shares = feed_grads(ns, shared, (active0, active1, active2), (dup0, dup1, dup2))
    shares, got_a, got_b = tied(shares, got_a, got_b)
    shares = lax.psum_scatter(shares, "ctx", scatter_dimension=0)
    more_a, more_b = across_w(a_far + got_a[1], 2), across_w(b_far + got_b[1], 1)
    d_hidden, d_att, d_branch, d_gain_two = turn(
        hidden, gain_second, dout0, (got_a, more_a, got_b, more_b), cot, wout_full
    )
    d_out = lax.all_to_all(d_att, "ctx", 0, 0, tiled=True, axis_index_groups=Z_GROUPS)
    out_own, out_far, out_send = out_grad(att_home, d_branch)
    d_out, out_send = tied(d_out, out_send)
    out_got = across_w(out_send, 1)
    *firsts, head_keep, head_send = attend_back(
        kv, mixt, att, lse, d_out, normed_all, w_full, gain_first, d_gain_two
    )
    *firsts, head_keep, head_send, out_got = tied(*firsts, head_keep, head_send, out_got)

    got = between_z(firsts[3], TO_MIDDLE)
    sum_head = head_keep + across_core(head_send)
    head_got = across_w(sum_head[1], 2)
    out_far = across_w(out_far + out_got[1], 2)
    up_share = lax.all_to_all(shares[:SHARD].reshape(4, QUART, HALF), "wshard", 0, 0, tiled=True)
    got, head_got, out_far, up_share, *parts = tied(got, head_got, out_far, up_share, *parts)

    both = firsts[2] + jnp.where(inner, got, BF(0))
    outer, middle = between_z(both, TO_MIDDLE), between_z(both, ACROSS)
    head_far = across_w(sum_head[0, 1] + head_got[1], 1)
    head = (sum_head[0, 0] + head_got[0]) + head_far
    share = jnp.concatenate([up_share.reshape(SHARD, HALF), shares[SHARD:], head])
    share_pair, share_mid = between_z(share, PAIRS), between_z(share, ACROSS)
    sum_out = ((out_own + out_got[0]) + out_far).reshape(2, PART, D)
    sum_out = pick(sum_out, core) + across_core(pick(sum_out, 1 - core))
    outer, middle, share_pair, share_mid, sum_out, *parts = tied(outer, middle, share_pair, share_mid, sum_out, *parts)

    pair = between_z(firsts[1] + jnp.where(inner, middle, BF(0)), PAIRS)
    middle = between_z(firsts[3] + outer, ACROSS)
    share_near, share_far = between_z(share_mid, PAIRS), between_z(share_pair, ACROSS)
    a, a_far, b, b_far = parts
    got_a, got_b = across_w(a, 1), across_w(b, 2)
    sum_out = sum_out + between_z(sum_out, TO_MIDDLE)
    pair, middle, share_near, share_far, sum_out, got_a, got_b = tied(
        pair, middle, share_near, share_far, sum_out, got_a, got_b
    )

    share_last = between_z(share_far, PAIRS)
    sum_out = sum_out + between_z(sum_out, ACROSS)
    grad_keep, grad_send = last(firsts[0], pair, middle, x_block, gain_first, d_hidden)
    more_a, more_b = across_w(a_far + got_a[1], 2), across_w(b_far + got_b[1], 1)
    shares = share, share_pair, jnp.where(inner, share_mid, share_near), jnp.where(inner, share_far, share_last)
    result_keep, result_send = give(hidden, out0, (got_a, more_a, got_b, more_b))
    out_result = both_micros(result_keep, across_core(result_send))
    out_tokens = both_micros(grad_keep, across_core(grad_send))
    sum_out = jnp.where(inner, sum_out, between_z(sum_out, TO_ENDS))
    grad_out = both_micros(sum_out, across_core(sum_out)).reshape(SHARD, D).astype(F32)
    grad_up, grad_down, grad_qkv, out_gains = finish(*shares, *(across_core(block) for block in shares))
    return (
        out_result,
        out_tokens,
        out_gains[0],
        grad_qkv,
        grad_out,
        out_gains[1],
        grad_up,
        grad_down,
    )


def local(tokens, *rest):
    fits = (
        lax.axis_size("wshard") == 4
        and lax.axis_size("ctx") == 8
        and tokens.shape[:2] == (2, 1)
        and 2 * tokens.shape[2] == TILE
    )
    return (local_grid if fits else local_any)(tokens, *rest)


def solution(mesh):
    placed = (
        P(None, "wshard", "ctx", None),
        P("wshard"),
        P("wshard", None),
        P("wshard", None),
        P("wshard"),
        P("wshard", None),
        P("wshard", None),
        P(None, "wshard", "ctx", None),
    )
    return jax.shard_map(
        local,
        mesh=mesh,
        in_specs=placed,
        out_specs=(
            P(None, "wshard", "ctx", None),
            P(None, "wshard", "ctx", None),
            P("wshard"),
            P("wshard", None),
            P("wshard", None),
            P("wshard"),
            P("wshard", None),
            P("wshard", None),
        ),
        check_vma=False,
    )
```

```python
import jax
import jax.numpy as jnp
from jax import lax
from jax.experimental import pallas as pl
from jax.experimental.pallas import tpu as pltpu
from jax.sharding import PartitionSpec as P

D = 768
HEADS = 12
HEAD_DIM = 64


EPSILON = 1e-05


def passed_along(value, axis, by):
    count = lax.axis_size(axis)
    return lax.ppermute(value, axis, [(i, (i + by) % count) for i in range(count)])


def layer_norm(inputs, scaling):
    centred = inputs - jnp.mean(inputs, axis=-1, keepdims=True)
    variance = jnp.mean(centred * centred, axis=-1, keepdims=True)
    return centred * lax.rsqrt(variance + EPSILON) * scaling


def gelu_smooth(values_in):
    return jax.nn.gelu(values_in, approximate=True)


def contract_rows(left_side, right_side):
    return lax.dot_general(
        left_side, right_side, (((0,), (0,)), ((), ())), preferred_element_type=jnp.float32
    )


def times_rows(left_side, right_side):
    return lax.dot_general(
        left_side, right_side, (((1,), (1,)), ((), ())), preferred_element_type=jnp.float32
    )


def pair_grads(query_h, dout_h, log_total, row_delta, query_pos, key_h, value_h, key_pos):
    scaling = HEAD_DIM ** (-0.5)
    scores = (
        jnp.einsum("qhe,khe->hqk", query_h, key_h, preferred_element_type=jnp.float32) * scaling
    )
    visible = key_pos[None, None, :] <= query_pos[None, :, None]
    magnitude = jnp.sqrt(scores * scores + 1.0)
    tilted = scores / magnitude
    chance = jnp.exp(jnp.where(visible, magnitude - log_total[:, :, None], -1e30))
    signed = (tilted * chance).astype(jnp.bfloat16)
    d_signed = jnp.einsum("qhe,khe->hqk", dout_h, value_h, preferred_element_type=jnp.float32)
    slope = 1.0 / (magnitude * magnitude * magnitude) + tilted * tilted
    d_scores = (chance * (d_signed * slope - tilted * row_delta[:, :, None])).astype(jnp.bfloat16)
    d_query = (
        jnp.einsum("hqk,khe->qhe", d_scores, key_h, preferred_element_type=jnp.float32) * scaling
    )
    d_key = (
        jnp.einsum("hqk,qhe->khe", d_scores, query_h, preferred_element_type=jnp.float32) * scaling
    )
    d_value = jnp.einsum("hqk,qhe->khe", signed, dout_h, preferred_element_type=jnp.float32)
    return (d_query, d_key, d_value)


def keep_state(loop_state):
    return loop_state


def local_any(tokens, gain_one, w_qkv, w_out, gain_two, w_up, w_down, cotangent):
    gathered = (
        lax.all_gather(gain_one, "wshard", axis=0, tiled=True),
        lax.all_gather(w_qkv, "wshard", axis=0, tiled=True),
        lax.all_gather(w_out, "wshard", axis=0, tiled=True),
        lax.all_gather(gain_two, "wshard", axis=0, tiled=True),
        lax.all_gather(w_up, "wshard", axis=0, tiled=True),
        lax.all_gather(w_down, "wshard", axis=0, tiled=True),
    )
    full_gain_one, full_qkv, full_out, full_gain_two, full_up, full_down = gathered
    gain_first = full_gain_one.astype(jnp.float32)
    gain_second = full_gain_two.astype(jnp.float32)
    cycle_size = lax.axis_size("ctx")
    cycle_place = lax.axis_index("ctx")
    micro_count = tokens.shape[0]
    local_len = tokens.shape[2]
    scaling = HEAD_DIM ** (-0.5)
    query_pos = cycle_place * local_len + jnp.arange(local_len, dtype=jnp.int32)
    sum_gain_one = jnp.zeros((D,), jnp.float32)
    sum_gain_two = jnp.zeros((D,), jnp.float32)
    sum_qkv = jnp.zeros(full_qkv.shape, jnp.float32)
    sum_out = jnp.zeros(full_out.shape, jnp.float32)
    sum_up = jnp.zeros(full_up.shape, jnp.float32)
    sum_down = jnp.zeros(full_down.shape, jnp.float32)
    results = []
    grad_list = []
    for micro_index in range(micro_count):
        inputs = tokens[micro_index, 0].astype(jnp.float32)
        normed_f, norm_back = jax.vjp(layer_norm, inputs, gain_first)
        normed = normed_f.astype(jnp.bfloat16)
        mixed_all = jnp.dot(normed, full_qkv, preferred_element_type=jnp.float32).astype(
            jnp.bfloat16
        )
        keys_flat = mixed_all[:, D : 2 * D]
        values_flat = mixed_all[:, 2 * D :]
        query_h = mixed_all[:, :D].reshape(local_len, HEADS, HEAD_DIM)
        key_h = keys_flat.reshape(local_len, HEADS, HEAD_DIM)
        value_h = values_flat.reshape(local_len, HEADS, HEAD_DIM)
        start_state = (
            jnp.zeros((HEADS, local_len, HEAD_DIM), jnp.float32),
            jnp.ones((HEADS, local_len), jnp.float32),
            jnp.zeros((HEADS, local_len), jnp.float32),
        )
        shard_piece = (
            lax.all_gather(keys_flat, "ctx", axis=0, tiled=True),
            lax.all_gather(values_flat, "ctx", axis=0, tiled=True),
        )

        def compute(loop_state):
            accumulated, top_value, totals = loop_state
            key_piece = shard_piece[0].reshape(-1, HEADS, HEAD_DIM)
            value_piece = shard_piece[1].reshape(-1, HEADS, HEAD_DIM)
            key_pos = jnp.arange(key_piece.shape[0], dtype=jnp.int32)
            scores = (
                jnp.einsum("qhe,khe->hqk", query_h, key_piece, preferred_element_type=jnp.float32)
                * scaling
            )
            visible = key_pos[None, None, :] <= query_pos[None, :, None]
            magnitude = jnp.sqrt(scores * scores + 1.0)
            new_top = jnp.maximum(top_value, jnp.max(jnp.where(visible, magnitude, 0.0), axis=-1))
            weighted = jnp.exp(jnp.where(visible, magnitude - new_top[:, :, None], -1e30))
            signed = (scores / magnitude * weighted).astype(jnp.bfloat16)
            accumulated = jnp.einsum(
                "hqk,khe->hqe", signed, value_piece, preferred_element_type=jnp.float32
            )
            totals = jnp.sum(weighted, axis=-1)
            return (accumulated, new_top, totals)

        accumulated, top_value, totals = lax.cond(
            jnp.int32(0) <= query_pos[-1], compute, keep_state, start_state
        )
        attended_h = accumulated / totals[:, :, None]
        log_total = top_value + jnp.log(totals)
        attended = jnp.transpose(attended_h, (1, 0, 2)).reshape(local_len, D)
        attended_low = attended.astype(jnp.bfloat16)
        hidden = inputs + jnp.dot(attended_low, full_out, preferred_element_type=jnp.float32)
        normed_two_f, norm_two_back = jax.vjp(layer_norm, hidden, gain_second)
        normed_two = normed_two_f.astype(jnp.bfloat16)
        upward = jnp.dot(normed_two, full_up, preferred_element_type=jnp.float32)
        active_f, gelu_back = jax.vjp(gelu_smooth, upward)
        active = active_f.astype(jnp.bfloat16)
        result_rows = hidden + jnp.dot(active, full_down, preferred_element_type=jnp.float32)
        results.append(result_rows.astype(jnp.bfloat16))
        d_result = cotangent[micro_index, 0]
        sum_down = sum_down + contract_rows(active, d_result)
        d_active = times_rows(d_result, full_down)
        d_upward = gelu_back(d_active)[0].astype(jnp.bfloat16)
        sum_up = sum_up + contract_rows(normed_two, d_upward)
        d_normed_two = times_rows(d_upward, full_up)
        d_hidden_norm, d_gain_two = norm_two_back(d_normed_two)
        sum_gain_two = sum_gain_two + d_gain_two
        d_hidden = d_result.astype(jnp.float32) + d_hidden_norm
        d_branch = d_hidden.astype(jnp.bfloat16)
        sum_out = sum_out + contract_rows(attended_low, d_branch)
        d_attended = times_rows(d_branch, full_out).astype(jnp.bfloat16)
        dout_h = d_attended.reshape(local_len, HEADS, HEAD_DIM)
        row_delta = jnp.einsum("qhe,hqe->hq", dout_h.astype(jnp.float32), attended_h)
        zero_block = jnp.zeros((local_len, HEADS, HEAD_DIM), jnp.float32)

        def turn_keys(turn_index, loop_state):
            key_b, value_b, d_key_b, d_value_b, d_query = loop_state
            owner_index = (cycle_place + turn_index) % cycle_size
            key_pos = owner_index * local_len + jnp.arange(local_len, dtype=jnp.int32)

            def work(partial_sums):
                contrib = pair_grads(
                    query_h, dout_h, log_total, row_delta, query_pos, key_b, value_b, key_pos
                )
                return (
                    partial_sums[0] + contrib[0],
                    partial_sums[1] + contrib[1],
                    partial_sums[2] + contrib[2],
                )

            needed = (turn_index == 0) | (cycle_place + turn_index >= cycle_size)
            d_query, d_key_b, d_value_b = lax.cond(
                needed, work, keep_state, (d_query, d_key_b, d_value_b)
            )
            key_b, value_b = passed_along((key_b, value_b), "ctx", -1)
            d_key_b, d_value_b = (
                passed_along(d_key_b.astype(jnp.bfloat16), "ctx", -1).astype(d_key_b.dtype),
                passed_along(d_value_b.astype(jnp.bfloat16), "ctx", -1).astype(d_value_b.dtype),
            )
            return (key_b, value_b, d_key_b, d_value_b, d_query)

        final_state = lax.fori_loop(
            0, cycle_size, turn_keys, (key_h, value_h, zero_block, zero_block, zero_block)
        )
        d_key = final_state[2]
        d_value = final_state[3]
        d_query = final_state[4]
        d_mixed = jnp.concatenate(
            [
                d_query.reshape(local_len, D),
                d_key.reshape(local_len, D),
                d_value.reshape(local_len, D),
            ],
            axis=1,
        ).astype(jnp.bfloat16)
        sum_qkv = sum_qkv + contract_rows(normed, d_mixed)
        d_normed = times_rows(d_mixed, full_qkv)
        d_inputs_norm, d_gain_one = norm_back(d_normed)
        sum_gain_one = sum_gain_one + d_gain_one
        grad_list.append(d_hidden + d_inputs_norm)
    shares = (
        lax.psum_scatter(
            sum_gain_one.astype(jnp.bfloat16), "wshard", scatter_dimension=0, tiled=True
        ).astype(jnp.float32),
        lax.psum_scatter(
            sum_qkv.astype(jnp.bfloat16), "wshard", scatter_dimension=0, tiled=True
        ).astype(jnp.float32),
        lax.psum_scatter(
            sum_out.astype(jnp.bfloat16), "wshard", scatter_dimension=0, tiled=True
        ).astype(jnp.float32),
        lax.psum_scatter(
            sum_gain_two.astype(jnp.bfloat16), "wshard", scatter_dimension=0, tiled=True
        ).astype(jnp.float32),
        lax.psum_scatter(
            sum_up.astype(jnp.bfloat16), "wshard", scatter_dimension=0, tiled=True
        ).astype(jnp.float32),
        lax.psum_scatter(
            sum_down.astype(jnp.bfloat16), "wshard", scatter_dimension=0, tiled=True
        ).astype(jnp.float32),
    )
    summed = (
        lax.psum(shares[0].astype(jnp.bfloat16), "ctx").astype(jnp.float32),
        lax.psum(shares[1].astype(jnp.bfloat16), "ctx").astype(jnp.float32),
        lax.psum(shares[2].astype(jnp.bfloat16), "ctx").astype(jnp.float32),
        lax.psum(shares[3].astype(jnp.bfloat16), "ctx").astype(jnp.float32),
        lax.psum(shares[4].astype(jnp.bfloat16), "ctx").astype(jnp.float32),
        lax.psum(shares[5].astype(jnp.bfloat16), "ctx").astype(jnp.float32),
    )
    result_out = jnp.stack(results)[:, None]
    grad_out_tokens = jnp.stack(grad_list)[:, None]
    return (
        result_out,
        grad_out_tokens,
        summed[0],
        summed[1],
        summed[2],
        summed[3],
        summed[4],
        summed[5],
    )


BF = jnp.bfloat16
F32 = jnp.float32
TILE = 256
SHARD = D // 4
OWN_HEADS = HEADS // 4
OWN = OWN_HEADS * HEAD_DIM
MIX = 3 * OWN
HEAD_ROWS = 160
PART = SHARD // 2
QUART = SHARD // 4
HALF = D // 2
MIDDLE_ROW = 224
VMEM_LIMIT = 56 * 1024 * 1024
WHOLE = pl.BlockSpec(memory_space=pltpu.VMEM)
ANYWHERE = pl.BlockSpec(memory_space=pl.ANY)


def nn(a, b):
    return lax.dot_general(a, b, (((1,), (0,)), ((), ())), preferred_element_type=F32)


def nt(a, b):
    return lax.dot_general(a, b, (((1,), (1,)), ((), ())), preferred_element_type=F32)


def normalised(x):
    centred = x - jnp.mean(x, axis=-1, keepdims=True)
    variance = jnp.mean(centred * centred, axis=-1, keepdims=True)
    inverse = lax.rsqrt(variance + EPSILON)
    return centred * inverse, inverse


def norm_back(xhat, inverse, gain, dy):
    g = dy * gain
    mean_g = jnp.mean(g, axis=-1, keepdims=True)
    mean_gx = jnp.mean(g * xhat, axis=-1, keepdims=True)
    return (g - mean_g - xhat * mean_gx) * inverse


def causal_tile():
    rows = lax.broadcasted_iota(jnp.int32, (TILE, TILE), 0)
    cols = lax.broadcasted_iota(jnp.int32, (TILE, TILE), 1)
    return rows <= cols


def call(kernel, name, ins, outs, scratch, flops, args, out_specs=None):
    moved = sum(a.size * a.dtype.itemsize for a in args)
    return pl.pallas_call(
        kernel,
        in_specs=ins,
        out_specs=out_specs or [WHOLE] * len(outs),
        out_shape=[jax.ShapeDtypeStruct(shape, kind) for shape, kind in outs],
        scratch_shapes=scratch,
        compiler_params=pltpu.CompilerParams(vmem_limit_bytes=VMEM_LIMIT),
        cost_estimate=pl.CostEstimate(flops=1000, bytes_accessed=1000, transcendentals=0),
        name=name,
    )(*args)


def shard_rows_of(pieces, which, first, count):
    if which < 3:
        return pieces[which].at[pl.ds(first, count)]
    half = pieces[3].shape[0]
    if first < half:
        return pieces[3].at[pl.ds(first, count)]
    return pieces[4].at[pl.ds(first - half, count)]


def run_copies(pairs, sems):
    copies = [pltpu.make_async_copy(src, dst, sems.at[i]) for i, (src, dst) in enumerate(pairs)]
    for copy in copies:
        copy.start()
    for copy in copies:
        copy.wait()


def attend_kernel(x_ref, w0, w1, w2, w3, w4,
                  normed_ref, kv_ref, mixt_ref, att_ref, low_ref, lse_ref, wfull_ref, gains_ref, s_ref, g_ref, wsems):
    place = lax.axis_index("wshard")
    pieces = (w0, w1, w2, w3, w4)
    half = w3.shape[0]
    pairs = []
    for k in range(4):
        to = pl.multiple_of(jnp.bitwise_xor(place, k) * SHARD, SHARD)
        if k < 3:
            pairs.append((shard_rows_of(pieces, k, 0, SHARD), wfull_ref.at[pl.ds(to, SHARD)]))
        else:
            pairs.append((w3, wfull_ref.at[pl.ds(to, half)]))
            pairs.append((w4.at[pl.ds(0, SHARD - half)], wfull_ref.at[pl.ds(to + half, SHARD - half)]))
        source = w4.at[pl.ds(SHARD - half, 16)] if k == 3 else pieces[k].at[pl.ds(SHARD, 16)]
        pairs.append((source, g_ref.at[k]))
    run_copies(pairs, wsems)
    gains = jnp.concatenate([g_ref[jnp.bitwise_xor(place, j)][0:8, 0:SHARD].astype(F32) for j in range(4)], axis=1)
    gains_ref[...] = gains
    for row in range(4):
        here = slice(row * TILE, (row + 1) * TILE)
        xhat, _ = normalised(x_ref[row].astype(F32))
        normed = (xhat * gains[0:1]).astype(BF)
        normed_ref[here, :] = normed
        mix = nn(normed, wfull_ref[...]).astype(BF)
        mixt_ref[:, here] = mix.T
        for h in range(OWN_HEADS):
            kv_ref[h, here, 0:HEAD_DIM] = mix[:, OWN + h * HEAD_DIM : OWN + (h + 1) * HEAD_DIM]
            kv_ref[h, here, HEAD_DIM:] = mix[:, 2 * OWN + h * HEAD_DIM : 2 * OWN + (h + 1) * HEAD_DIM]

    @pl.loop(0, OWN_HEADS)
    def _(h):
        base = pl.multiple_of(h * HEAD_DIM, HEAD_DIM)
        for block in range(4):
            here = slice(block * TILE, (block + 1) * TILE)
            queries = mixt_ref[pl.ds(base, HEAD_DIM), here] * BF(HEAD_DIM**-0.5)
            top = jnp.zeros((1, TILE), F32)
            for other in range(block + 1):
                there = slice(other * TILE, (other + 1) * TILE)
                s = nn(kv_ref[h, there, 0:HEAD_DIM], queries)
                s_ref[there, :] = s
                size = jnp.abs(s)
                if other == block:
                    size = jnp.where(causal_tile(), size, 0.0)
                top = jnp.maximum(top, jnp.max(size, axis=0, keepdims=True))
            top = jnp.sqrt(top * top + 1.0)
            total = jnp.zeros((1, TILE), F32)
            acc = jnp.zeros((HEAD_DIM, TILE), F32)
            for other in range(block + 1):
                there = slice(other * TILE, (other + 1) * TILE)
                s = s_ref[there, :]
                square = s * s + 1.0
                r = lax.rsqrt(square)
                p = jnp.exp(square * r - top)
                if other == block:
                    p = jnp.where(causal_tile(), p, 0.0)
                total = total + jnp.sum(p, axis=0, keepdims=True)
                signed = (s * r * p).astype(BF)
                acc = acc + nn(mixt_ref[pl.ds(2 * OWN + base, HEAD_DIM), there], signed)
            att = acc / total
            att_ref[pl.ds(base, HEAD_DIM), here] = att
            low_ref[block, pl.ds(base, HEAD_DIM), :] = att.astype(BF)
            lse_ref[pl.ds(h, 1), here] = top + jnp.log(total)


def attend(x_all, pieces):
    length = 4 * TILE
    return call(
        attend_kernel,
        "attend",
        [WHOLE] + [ANYWHERE] * 5,
        [
            ((length, D), BF),
            ((OWN_HEADS, length, 2 * HEAD_DIM), BF),
            ((MIX, length), BF),
            ((OWN, length), F32),
            ((4, OWN, TILE), BF),
            ((8, length), F32),
            ((D, MIX), BF),
            ((8, D), F32),
        ],
        [
            pltpu.VMEM((length, TILE), F32),
            pltpu.VMEM((4, 16, MIX), BF),
            pltpu.SemaphoreType.DMA((9,)),
        ],
        3 * 10**9,
        (x_all, *pieces),
    )


def parcel_kernel(cot_ref, wout_ref, wup_ref, x_on_ref, x_ref, y_on_ref, y_ref, sems):
    place = lax.axis_index("wshard")

    def columns(k, first, count):
        at = pl.multiple_of(jnp.bitwise_xor(place, k) * D, D)
        return wup_ref.at[pl.ds(first, count), pl.ds(at, D)]

    low, high = cot_ref.at[pl.ds(0, MIDDLE_ROW)], cot_ref.at[pl.ds(MIDDLE_ROW, 32)]
    pairs = (
        (low, x_on_ref.at[pl.ds(0, MIDDLE_ROW)]),
        (columns(3, 0, PART), x_on_ref.at[pl.ds(MIDDLE_ROW, PART)]),
        (high, y_on_ref.at[pl.ds(0, 32)]),
        (wout_ref, y_on_ref.at[pl.ds(32, SHARD)]),
        (columns(3, PART, PART), y_on_ref.at[pl.ds(MIDDLE_ROW, PART)]),
        (columns(1, 0, SHARD), x_ref.at[pl.ds(0, SHARD)]),
        (high, x_ref.at[pl.ds(SHARD, 32)]),
        (wout_ref, x_ref.at[pl.ds(SHARD + 32, SHARD)]),
        (columns(2, 0, SHARD), y_ref.at[pl.ds(0, SHARD)]),
        (low, y_ref.at[pl.ds(SHARD, MIDDLE_ROW)]),
    )
    run_copies(pairs, sems)


def parcels(cot, w_out, w_up):
    on, rest = MIDDLE_ROW + PART, SHARD + MIDDLE_ROW
    return call(
        parcel_kernel,
        "parcels",
        [ANYWHERE] * 3,
        [((on, D), BF), ((rest, D), BF)] * 2,
        [pltpu.SemaphoreType.DMA((10,))],
        10**6,
        (cot, w_out, w_up),
    )


def assemble_kernel(cot_ref, own_ref, wup_ref, x_on, x_rest, y_on, y_rest, corner_a, corner_b,
                    wout_ref, up_ref, cots_ref, sems):
    place = lax.axis_index("wshard")
    at = [pl.multiple_of(jnp.bitwise_xor(place, k) * SHARD, SHARD) for k in range(4)]
    half = PART
    mine = pl.multiple_of(place * D, D)
    pairs = (
        (own_ref, wout_ref.at[pl.ds(at[0], SHARD)]),
        (x_rest.at[pl.ds(SHARD + 32, SHARD)], wout_ref.at[pl.ds(at[1], SHARD)]),
        (y_on.at[pl.ds(32, SHARD)], wout_ref.at[pl.ds(at[2], SHARD)]),
        (corner_b.at[pl.ds(32, SHARD)], wout_ref.at[pl.ds(at[3], SHARD)]),
        (wup_ref.at[:, pl.ds(mine, D)], up_ref.at[pl.ds(at[0], SHARD)]),
        (x_rest.at[pl.ds(0, SHARD)], up_ref.at[pl.ds(at[1], SHARD)]),
        (y_rest.at[pl.ds(0, SHARD)], up_ref.at[pl.ds(at[2], SHARD)]),
        (corner_a.at[pl.ds(MIDDLE_ROW, half)], up_ref.at[pl.ds(at[3], half)]),
        (corner_b.at[pl.ds(MIDDLE_ROW, half)], up_ref.at[pl.ds(at[3] + half, half)]),
        (cot_ref, cots_ref.at[pl.ds(0, TILE)]),
        (x_on.at[pl.ds(0, MIDDLE_ROW)], cots_ref.at[pl.ds(TILE, MIDDLE_ROW)]),
        (x_rest.at[pl.ds(SHARD, 32)], cots_ref.at[pl.ds(TILE + MIDDLE_ROW, 32)]),
        (y_rest.at[pl.ds(SHARD, MIDDLE_ROW)], cots_ref.at[pl.ds(2 * TILE, MIDDLE_ROW)]),
        (y_on.at[pl.ds(0, 32)], cots_ref.at[pl.ds(2 * TILE + MIDDLE_ROW, 32)]),
        (corner_a.at[pl.ds(0, MIDDLE_ROW)], cots_ref.at[pl.ds(3 * TILE, MIDDLE_ROW)]),
        (corner_b.at[pl.ds(0, 32)], cots_ref.at[pl.ds(3 * TILE + MIDDLE_ROW, 32)]),
    )
    run_copies(pairs, sems)


def assemble(cot, w_out, w_up, shared):
    return call(
        assemble_kernel,
        "assemble",
        [ANYWHERE] * 9,
        [((D, D), BF), ((D, D), BF), ((4 * TILE, D), BF)],
        [pltpu.SemaphoreType.DMA((16,))],
        10**6,
        (cot, w_out, w_up, *shared),
    )


def project_kernel(att_ref, x_ref, gain_ref, wout_ref, hidden_ref, normed_ref):
    hidden = x_ref[...].astype(F32) + nn(att_ref[...].T, wout_ref[...])
    hidden_ref[...] = hidden
    xhat, _ = normalised(hidden)
    normed_ref[...] = (xhat * gain_ref[1:2]).astype(BF)


def project(att_home, x_block, gain, w_out):
    rows = x_block.shape[0]
    return call(
        project_kernel,
        "project",
        [WHOLE] * 4,
        [((rows, D), F32), ((rows, D), BF)],
        [],
        3 * 10**8,
        (att_home, x_block, gain, w_out),
    )


SLOPE = (2.0 / 3.141592653589793) ** 0.5


def feed_rows(n, cot, up_ref, down_ref, active_ref, dup_ref, here):
    for first in range(0, D, TILE):
        cols = slice(first, first + TILE)
        u = nn(n, up_ref[:, cols])
        square = u * u
        t = jnp.tanh(SLOPE * (u + 0.044715 * (square * u)))
        side = 0.5 + 0.5 * t
        active_ref[here, cols] = (u * side).astype(BF)
        grad = side + (0.5 * SLOPE) * u * (1.0 - t * t) * (1.0 + 0.134145 * square)
        dup_ref[here, cols] = (grad * nt(cot, down_ref[cols, :])).astype(BF)
    return nn(active_ref[here, :], down_ref[...]), nt(dup_ref[here, :], up_ref[...])


def feed_own_kernel(n_ref, cot_ref, up_ref, down_ref, active_ref, dup_ref, out_ref, dout_ref):
    out_ref[...], dout_ref[...] = feed_rows(
        n_ref[...], cot_ref[0:TILE, :], up_ref, down_ref, active_ref, dup_ref, slice(0, TILE)
    )


def feed_own(n, cots, up, down):
    return call(
        feed_own_kernel,
        "feed_own",
        [WHOLE] * 4,
        [((TILE, D), BF), ((TILE, D), BF), ((TILE, D), F32), ((TILE, D), F32)],
        [],
        2 * 10**9,
        (n, cots, up, down),
    )


def feed_near_kernel(nx_ref, ny_ref, cot_ref, up_ref, down_ref, active_ref, dup_ref, out_ref, dout_ref):
    for k, n_ref in enumerate((nx_ref, ny_ref)):
        here = slice(k * TILE, (k + 1) * TILE)
        out, dout = feed_rows(n_ref[...], cot_ref[(k + 1) * TILE : (k + 2) * TILE, :], up_ref, down_ref, active_ref, dup_ref, here)
        out_ref[here, :], dout_ref[here, :] = out.astype(BF), dout.astype(BF)


def feed_near(nx, ny, cots, up, down):
    return call(
        feed_near_kernel,
        "feed_near",
        [WHOLE] * 5,
        [((2 * TILE, D), BF)] * 4,
        [],
        4 * 10**9,
        (nx, ny, cots, up, down),
    )


def feed_far_kernel(na_ref, nb_ref, cot_ref, out_ref, dout_ref, up_ref, down_ref,
                    active_ref, dup_ref, oa_ref, oaf_ref, ob_ref, obf_ref, da_ref, daf_ref, db_ref, dbf_ref):
    n = jnp.concatenate([na_ref[...], nb_ref[...]])
    cot = cot_ref[3 * TILE :, :]
    half = TILE // 2
    out, dout = feed_rows(n, cot, up_ref, down_ref, active_ref, dup_ref, slice(0, TILE))
    for far, near, a, af, b, bf in (
        (out, out_ref, oa_ref, oaf_ref, ob_ref, obf_ref),
        (dout, dout_ref, da_ref, daf_ref, db_ref, dbf_ref),
    ):
        far = far.astype(BF)
        a[0], a[1] = near[0:half, :], far[0:half]
        b[0], b[1] = near[TILE + half :, :], far[half:]
        af[...] = near[TILE : TILE + half, :]
        bf[...] = near[half:TILE, :]


def feed_far(na, nb, cots, out, dout, up, down):
    half = TILE // 2
    return call(
        feed_far_kernel,
        "feed_far",
        [WHOLE] * 7,
        [((TILE, D), BF)] * 2 + [((2, half, D), BF), ((half, D), BF)] * 4,
        [],
        2 * 10**9,
        (na, nb, cots, out, dout, up, down),
    )


def feed_grads_kernel(n0, n1, n2, n3, n4, cot_ref, a0, a1, a2, d0, d1, d2,
                      shares_ref, nt_ref, at_ref, dup_ref):
    for k, piece in enumerate((n0, n1, n2)):
        nt_ref[:, k * TILE : (k + 1) * TILE] = piece[...].T
    nt_ref[:, 3 * TILE :] = jnp.concatenate([n3[...], n4[...]]).T
    at_ref[:, 0:TILE] = a0[...].T
    at_ref[:, TILE : 3 * TILE] = a1[...].T
    at_ref[:, 3 * TILE :] = a2[...].T
    dup_ref[0:TILE] = d0[...]
    dup_ref[TILE : 3 * TILE] = d1[...]
    dup_ref[3 * TILE :] = d2[...]
    rows = D // 8
    for k in range(8):
        g = nn(at_ref[k * rows : (k + 1) * rows, :], cot_ref[...]).astype(BF)
        for side in range(2):
            for part in range(2):
                piece = g[part * QUART : (part + 1) * QUART, side * HALF : (side + 1) * HALF]
                shares_ref[k, 4 + 2 * side + part] = piece
    for to in range(4):
        g = nn(nt_ref[to * SHARD : (to + 1) * SHARD, :], dup_ref[...]).astype(BF)
        slot = jnp.bitwise_xor(lax.axis_index("wshard"), to)
        for k in range(8):
            r, c = (k // 2) * QUART, (k % 2) * HALF
            shares_ref[k, slot] = g[r : r + QUART, c : c + HALF]


def feed_grads(ns, cots, actives, dups):
    length = 4 * TILE
    return call(
        feed_grads_kernel,
        "feed_grads",
        [WHOLE] * 12,
        [((8, 8, QUART, HALF), BF)],
        [
            pltpu.VMEM((D, length), BF),
            pltpu.VMEM((D, length), BF),
            pltpu.VMEM((length, D), BF),
        ],
        3 * 10**9,
        (*ns, cots, *actives, *dups),
    )[0]


def summed(keep_ref, a_ref, a_more_ref, b_ref, b_more_ref):
    first = a_ref[0].astype(F32) + a_more_ref[...].astype(F32)
    second = b_ref[0].astype(F32) + b_more_ref[...].astype(F32)
    return keep_ref[...] + jnp.concatenate([first, second])


def give_kernel(hidden_ref, keep_ref, a_ref, a_more_ref, b_ref, b_more_ref, rkeep_ref, rsend_ref, result_ref, sems):
    core = lax.axis_index("ctx") % 2
    result = (hidden_ref[...] + summed(keep_ref, a_ref, a_more_ref, b_ref, b_more_ref)).astype(BF)
    half = TILE // 2
    result_ref[0], result_ref[1] = result[:half], result[half:]
    run_copies(((result_ref.at[1 - core], rsend_ref), (result_ref.at[core], rkeep_ref)), sems)


def give(hidden, keep, parts):
    half = TILE // 2
    return call(
        give_kernel,
        "give",
        [WHOLE] * 6,
        [((half, D), BF)] * 2,
        [pltpu.VMEM((2, half, D), BF), pltpu.SemaphoreType.DMA((2,))],
        10**6,
        (hidden, keep, *parts),
        [ANYWHERE] * 2,
    )


def turn_kernel(hidden_ref, gain_ref, dkeep_ref, a_ref, a_more_ref, b_ref, b_more_ref, cot_ref, wout_ref,
                dhidden_ref, datt_ref, dbranch_ref, dgain_ref):
    gain = gain_ref[1:2]
    xhat, inverse = normalised(hidden_ref[...])
    dy = summed(dkeep_ref, a_ref, a_more_ref, b_ref, b_more_ref)
    dgain_ref[...] = jnp.sum(dy * xhat, axis=0, keepdims=True)
    d_hidden = cot_ref[...].astype(F32) + norm_back(xhat, inverse, gain, dy)
    dhidden_ref[...] = d_hidden
    d_branch = d_hidden.astype(BF)
    dbranch_ref[...] = d_branch
    d_att = nt(wout_ref[...], d_branch).astype(BF)
    for k in range(4):
        datt_ref[k] = d_att[k * OWN : (k + 1) * OWN]


def turn(hidden, gain, dkeep, parts, cot, w_out):
    rows = hidden.shape[0]
    return call(
        turn_kernel,
        "turn",
        [WHOLE] * 9,
        [((rows, D), F32), ((4, OWN, rows), BF), ((rows, D), BF), ((1, D), F32)],
        [],
        6 * 10**8,
        (hidden, gain, dkeep, *parts, cot, w_out),
    )


def out_grad_kernel(att_ref, dbranch_ref, keep_ref, send_ref, grad_ref, sems):
    core = lax.axis_index("ctx") % 2
    place = lax.axis_index("wshard")
    for to in range(4):
        e = jnp.bitwise_xor(place, to)
        e_x, e_y = jnp.bitwise_and(e, 1), e // 2
        g = nn(att_ref[to * SHARD : (to + 1) * SHARD, :], dbranch_ref[...]).astype(BF)
        for side in range(2):
            for half in range(2):
                piece = g[side * PART : (side + 1) * PART, half * HALF : (half + 1) * HALF]
                grad_ref[side, e_y, e_x, half * PART : (half + 1) * PART] = piece
    rows = pl.ds(HEAD_ROWS, SHARD)
    pairs = ((grad_ref.at[1 - core], send_ref.at[:, :, rows]), (grad_ref.at[core], keep_ref.at[:, :, rows]))
    run_copies(pairs, sems)


def out_grad(att_home, d_branch):
    return call(
        out_grad_kernel,
        "out_grad",
        [WHOLE] * 2,
        [((2, 2, HEAD_ROWS + SHARD, HALF), BF)] * 2,
        [pltpu.VMEM((2, 2, 2, SHARD, HALF), BF), pltpu.SemaphoreType.DMA((2,))],
        3 * 10**8,
        (att_home, d_branch),
        [ANYWHERE] * 2,
    )


def attend_back_kernel(kv_ref, mixt_ref, att_ref, lse_ref, dout_ref, normed_ref, w_ref, gain_ref, dgain_ref, _, __,
                       f0_ref, f1_ref, f2_ref, f3_ref, gkeep_ref, gsend_ref,
                       dq_ref, dk_ref, dv_ref, dm_ref, mix_ref, total_ref, first_ref, head_ref, sems):
    length = normed_ref.shape[0]
    scale = BF(HEAD_DIM**-0.5)
    core = lax.axis_index("ctx") % 2
    z = lax.axis_index("ctx") // 2
    place = lax.axis_index("wshard")

    @pl.loop(0, OWN_HEADS)
    def _(h):
        base = pl.multiple_of(h * HEAD_DIM, HEAD_DIM)
        for block in range(4):
            here = slice(block * TILE, (block + 1) * TILE)
            queries = mixt_ref[pl.ds(base, HEAD_DIM), here] * scale
            dout = dout_ref[block, pl.ds(base, HEAD_DIM), :]
            delta = jnp.sum(dout.astype(F32) * att_ref[pl.ds(base, HEAD_DIM), here], axis=0, keepdims=True)
            lse = lse_ref[pl.ds(h, 1), here]
            acc = jnp.zeros((HEAD_DIM, TILE), F32)
            for other in range(block + 1):
                there = slice(other * TILE, (other + 1) * TILE)
                s = nn(kv_ref[h, there, 0:HEAD_DIM], queries)
                ds = nn(kv_ref[h, there, HEAD_DIM:], dout)
                square = s * s + 1.0
                r = lax.rsqrt(square)
                chance = jnp.exp(square * r - lse)
                if other == block:
                    chance = jnp.where(causal_tile(), chance, 0.0)
                tilted = s * r
                signed = (tilted * chance).astype(BF)
                slope = r * r * r + tilted * tilted
                dsc = (chance * (ds * slope - tilted * delta)).astype(BF)
                acc = acc + nn(mixt_ref[pl.ds(OWN + base, HEAD_DIM), there], dsc)
                dk = nt(dsc, queries)
                dv = nt(signed, dout)
                if other == block:
                    dk_ref[there, :] = dk
                    dv_ref[there, :] = dv
                else:
                    dk_ref[there, :] += dk
                    dv_ref[there, :] += dv
            dq_ref[:, here] = acc * HEAD_DIM**-0.5
        dm_ref[h, :, 0:HEAD_DIM] = dq_ref[...].T.astype(BF)
        dm_ref[h, :, HEAD_DIM : 2 * HEAD_DIM] = dk_ref[...].astype(BF)
        dm_ref[h, :, 2 * HEAD_DIM :] = dv_ref[...].astype(BF)

    for h in range(OWN_HEADS):
        for kind in range(3):
            to = kind * OWN + h * HEAD_DIM
            mix_ref[:, to : to + HEAD_DIM] = dm_ref[h, :, kind * HEAD_DIM : (kind + 1) * HEAD_DIM]
    total_ref[...] = jnp.zeros_like(total_ref)
    for block in range(4):
        here = slice(block * TILE, (block + 1) * TILE)
        first = nt(mix_ref[here, :], w_ref[...])
        first_ref[block] = first.astype(BF)
        total_ref[...] += jnp.sum(first * normed_ref[here, :].astype(F32), axis=0, keepdims=True)
    outs = (f3_ref, f2_ref, f1_ref, f0_ref)
    copies = [
        pltpu.make_async_copy(first_ref.at[jnp.bitwise_xor(z, 3 - k)], ref, sems.at[k]) for k, ref in enumerate(outs)
    ]
    for copy in copies:
        copy.start()
    gain_one = total_ref[...] / gain_ref[0:1]
    gain_two = dgain_ref[...]
    for to in range(4):
        e = jnp.bitwise_xor(place, to)
        e_x, e_y = jnp.bitwise_and(e, 1), e // 2
        g = nn(normed_ref[:, to * SHARD : (to + 1) * SHARD].T, mix_ref[...]).astype(BF)
        span = slice(to * SHARD, (to + 1) * SHARD)
        gains = jnp.concatenate([gain_one[:, span], gain_two[:, span], jnp.zeros((14, SHARD), F32)], axis=0)
        gains = jnp.concatenate([gains, jnp.zeros((16, HALF - SHARD), F32)], axis=1).astype(BF)
        for side in range(2):
            at = side * PART
            head_ref[side, e_y, e_x, 0:PART] = g[at : at + PART, 0:HALF]
            head_ref[side, e_y, e_x, PART : PART + QUART, 0:OWN] = g[at : at + QUART, HALF:]
            head_ref[side, e_y, e_x, PART : PART + QUART, OWN:] = g[at + QUART : at + PART, HALF:]
            head_ref[side, e_y, e_x, PART + QUART :] = gains if side == 0 else jnp.zeros_like(gains)
    more = [
        pltpu.make_async_copy(head_ref.at[1 - core], gsend_ref.at[:, :, pl.ds(0, HEAD_ROWS)], sems.at[4]),
        pltpu.make_async_copy(head_ref.at[core], gkeep_ref.at[:, :, pl.ds(0, HEAD_ROWS)], sems.at[5]),
    ]
    for copy in more:
        copy.start()
    for copy in copies + more:
        copy.wait()


def attend_back(kv, mixt, att, lse, dout, normed, w, gain, dgain, keep, send):
    length = normed.shape[0]
    return pl.pallas_call(
        attend_back_kernel,
        in_specs=[WHOLE] * 9 + [ANYWHERE] * 2,
        out_specs=[ANYWHERE] * 6,
        out_shape=[jax.ShapeDtypeStruct((TILE, D), BF)] * 4 + [jax.ShapeDtypeStruct(keep.shape, BF)] * 2,
        input_output_aliases={9: 4, 10: 5},
        scratch_shapes=[
            pltpu.VMEM((HEAD_DIM, length), F32),
            pltpu.VMEM((length, HEAD_DIM), F32),
            pltpu.VMEM((length, HEAD_DIM), F32),
            pltpu.VMEM((OWN_HEADS, length, 3 * HEAD_DIM), BF),
            pltpu.VMEM((length, MIX), BF),
            pltpu.VMEM((1, D), F32),
            pltpu.VMEM((4, TILE, D), BF),
            pltpu.VMEM((2, 2, 2, HEAD_ROWS, HALF), BF),
            pltpu.SemaphoreType.DMA((6,)),
        ],
        compiler_params=pltpu.CompilerParams(vmem_limit_bytes=VMEM_LIMIT),
        cost_estimate=pl.CostEstimate(flops=1000, bytes_accessed=1000, transcendentals=0),
        name="attend_back",
    )(kv, mixt, att, lse, dout, normed, w, gain, dgain, keep, send)


def is_inner():
    z = lax.axis_index("ctx") // 2
    return (z == 1) | (z == 2)


def last_kernel(first_ref, pair_ref, middle_ref, x_ref, gain_ref, dhidden_ref, keep_ref, send_ref, grad_ref, sems):
    core = lax.axis_index("ctx") % 2
    rows = x_ref.shape[0] // 2
    dy = first_ref[...].astype(F32) + pair_ref[...].astype(F32)
    dy = dy + jnp.where(is_inner(), middle_ref[...].astype(F32), 0.0)
    xhat, inverse = normalised(x_ref[...].astype(F32))
    grad = dhidden_ref[...] + norm_back(xhat, inverse, gain_ref[0:1], dy)
    grad_ref[0], grad_ref[1] = grad[:rows], grad[rows:]
    run_copies(((grad_ref.at[1 - core], send_ref), (grad_ref.at[core], keep_ref)), sems)


def last(*args):
    rows = TILE // 2
    return call(
        last_kernel,
        "last",
        [WHOLE] * 6,
        [((rows, D), F32), ((rows, D), F32)],
        [pltpu.VMEM((2, rows, D), F32), pltpu.SemaphoreType.DMA((2,))],
        10**7,
        args,
        [ANYWHERE] * 2,
    )


def line_slots():
    z = lax.axis_index("ctx") // 2
    return z, jnp.bitwise_xor(z, 1), jnp.where(z < 2, 2, 1), jnp.where(z < 2, 3, 0)


def finish_feed_kernel(*refs):
    mine, theirs, (gup_ref, gdown_ref) = refs[:4], refs[4:8], refs[8:]
    core = lax.axis_index("ctx") % 2
    place = lax.axis_index("wshard")
    rows = D // 8
    for group, side in ((mine, core), (theirs, 1 - core)):
        for ref, slot in zip(group, line_slots()):
            at = pl.multiple_of(slot * QUART, 16)
            for k in range(4):
                to = pl.multiple_of(jnp.bitwise_xor(place, k) * D + side * HALF, 128)
                gup_ref[pl.ds(at, QUART), pl.ds(to, HALF)] = ref[k * QUART : (k + 1) * QUART].astype(F32)
            at = pl.multiple_of((2 * slot + side) * rows, 32)
            for half in range(2):
                share = ref[SHARD + half * rows : SHARD + (half + 1) * rows]
                gdown_ref[pl.ds(at, rows), half * HALF : (half + 1) * HALF] = share.astype(F32)


def finish_feed(*args):
    return call(
        finish_feed_kernel, "finish_feed", [WHOLE] * 8, [((SHARD, 4 * D), F32), ((D, D), F32)], [], 10**7, args
    )


def finish_heads_kernel(*refs):
    mine, theirs, outs, (gout_ref, gqkv_ref, gains_ref) = refs[:4], refs[4:8], refs[8:10], refs[10:]
    slots = line_slots()
    first = lax.axis_index("ctx") % 2 == 0
    out, other_out = [ref[...].astype(F32) for ref in outs]
    for half in range(2):
        here, cols = slice(half * PART, (half + 1) * PART), slice(half * HALF, (half + 1) * HALF)
        gout_ref[0:PART, cols] = jnp.where(first, out[here], other_out[here])
        gout_ref[PART:, cols] = jnp.where(first, other_out[here], out[here])
    mine, theirs = [[ref[...].astype(F32) for ref in group] for group in (mine, theirs)]
    low = [jnp.where(first, a, b) for a, b in zip(mine, theirs)]
    high = [jnp.where(first, b, a) for a, b in zip(mine, theirs)]
    gains_ref[...] = sum(block[PART + QUART :, 0:SHARD] for block in low)
    for slot in range(4):
        for side, group in enumerate((low, high)):
            block = jnp.where(
                slot == slots[0],
                group[0],
                jnp.where(slot == slots[1], group[1], jnp.where(slot == slots[2], group[2], group[3])),
            )
            at, to = side * PART, slot * OWN
            gqkv_ref[at : at + PART, to : to + OWN] = block[0:PART, 0:OWN]
            gqkv_ref[at : at + PART, D + to : D + to + OWN] = block[0:PART, OWN:]
            gqkv_ref[at : at + QUART, 2 * D + to : 2 * D + to + OWN] = block[PART : PART + QUART, 0:OWN]
            gqkv_ref[at + QUART : at + PART, 2 * D + to : 2 * D + to + OWN] = block[PART : PART + QUART, OWN:]


def finish_heads(*args):
    return call(
        finish_heads_kernel,
        "finish_heads",
        [WHOLE] * 10,
        [((SHARD, D), F32), ((SHARD, 3 * D), F32), ((16, SHARD), F32)],
        [],
        10**7,
        args,
    )


def pick(value, index, axis=0):
    return lax.dynamic_index_in_dim(value, index, axis, keepdims=False)


def across_w(value, flip):
    return lax.ppermute(value, "wshard", [(i, i ^ flip) for i in range(4)])


def across_core(value):
    return lax.ppermute(value, "ctx", [(i, i ^ 1) for i in range(8)])


def between_z(value, pairs):
    return lax.ppermute(value, "ctx", [(2 * a + c, 2 * b + c) for a, b in pairs for c in range(2)])


Z_GROUPS = [[0, 2, 4, 6], [1, 3, 5, 7]]


def after(value, *others):
    return lax.optimization_barrier((value, *others))[0]


PAIRS = [(0, 1), (1, 0), (2, 3), (3, 2)]
MIDDLE = [(1, 2), (2, 1), (0, 0), (3, 3)]


def line_z(block):
    pair = between_z(block, PAIRS)
    mid_near = between_z(block, MIDDLE)
    near = between_z(mid_near, PAIRS)
    mid_far = between_z(pair, MIDDLE)
    far = between_z(mid_far, PAIRS)
    return block, pair, near, far, mid_near, mid_far


TO_MIDDLE = [(0, 1), (3, 2)]
TO_ENDS = [(1, 0), (2, 3)]
ACROSS = [(1, 2), (2, 1)]


def own_slot(slots, x_first):
    one, two = (1, 2) if x_first else (2, 1)
    got = across_w(slots[1], one)
    far = slots[0, 1] + got[1]
    return (slots[0, 0] + got[0]) + across_w(far, two)


def gather_plane(block, *others):
    half = block.shape[0] // 2
    from_x, from_y = across_w(block, 1), across_w(block, 2)
    first, second = from_x[:half], from_y[half:]
    if others:
        first, second, *_ = tied(first, second, *others)
    return block, from_x, from_y, across_w(first, 2), across_w(second, 1)


def tied(*values):
    return lax.optimization_barrier(values)


def local_grid(tokens, gain_one, w_qkv, w_out, gain_two, w_up, w_down, cotangent):
    core = lax.axis_index("ctx") % 2
    z = lax.axis_index("ctx") // 2
    place = lax.axis_index("wshard")
    inner = (z == 1) | (z == 2)

    def both_micros(kept, got):
        return jnp.where(core == 0, jnp.stack([kept, got]), jnp.stack([got, kept]))[:, None]

    tok, cot = tokens[:, 0], cotangent[:, 0]
    kept = jnp.concatenate([pick(tok, core), pick(cot, core)])
    got = across_core(jnp.concatenate([pick(tok, 1 - core), pick(cot, 1 - core)]))
    half = TILE // 2
    own = [jnp.where(core == 0, a, b) for a, b in ((kept, got), (got, kept))]
    x_block = jnp.concatenate([own[0][:half], own[1][:half]])
    cot = jnp.concatenate([own[0][half:], own[1][half:]])

    w_heads = pick(w_qkv.reshape(SHARD, 3, 4, OWN), z, 2).reshape(SHARD, MIX)
    gains = jnp.pad(jnp.stack([gain_one, gain_two]), ((0, 30), (0, MIX - SHARD)))
    x_all = lax.all_to_all(
        jnp.broadcast_to(x_block, (4,) + x_block.shape), "ctx", 0, 0, tiled=True, axis_index_groups=Z_GROUPS
    )
    x_on, x_rest, y_on, y_rest = parcels(cot, w_out, w_up)
    x_on, y_on = across_w(x_on, 1), across_w(y_on, 2)
    x_on, y_on, w_heads = tied(x_on, y_on, jnp.concatenate([w_heads, gains]))
    heads = gather_plane(w_heads)
    corner_a, corner_b = across_w(x_on, 2), across_w(y_on, 1)
    x_rest, y_rest, *heads = tied(x_rest, y_rest, *heads)
    x_rest, y_rest = across_w(x_rest, 1), across_w(y_rest, 2)
    normed_all, kv, mixt, att, att_low, lse, w_full, gains = attend(x_all, heads)
    shared = x_on, x_rest, y_on, y_rest, corner_a, corner_b
    att_low, *shared = tied(att_low, *shared)
    att_home = lax.all_to_all(att_low, "ctx", 0, 0, tiled=True, axis_index_groups=Z_GROUPS).reshape(D, -1)
    wout_full, up, cots = assemble(cot, w_out, w_up, shared)
    hidden, normed_two = project(att_home, x_block, gains, wout_full)

    active0, dup0, out0, dout0 = feed_own(normed_two, cots, up, w_down)
    ns = gather_plane(normed_two, active0)
    active1, dup1, out1, dout1 = feed_near(ns[1], ns[2], cots, up, w_down)
    active2, dup2, *parts = feed_far(ns[3], ns[4], cots, out1, dout1, up, w_down)
    parts, (a, a_far, b, b_far) = parts[:4], parts[4:]
    got_a, got_b = across_w(a, 1), across_w(b, 2)
    shares = feed_grads(ns, cots, (active0, active1, active2), (dup0, dup1, dup2))
    shares, got_a, got_b = tied(shares, got_a, got_b)
    shares = lax.psum_scatter(shares, "ctx", scatter_dimension=0)
    more_a, more_b = across_w(a_far + got_a[1], 2), across_w(b_far + got_b[1], 1)
    d_hidden, d_att, d_branch, d_gain_two = turn(
        hidden, gains, dout0, (got_a, more_a, got_b, more_b), cot, wout_full
    )
    d_out = lax.all_to_all(d_att, "ctx", 0, 0, tiled=True, axis_index_groups=Z_GROUPS)
    keep, send = out_grad(att_home, d_branch)
    d_out, keep, send = tied(d_out, keep, send)
    a, a_far, b, b_far = parts
    got_a, got_b = across_w(a, 1), across_w(b, 2)
    *firsts, keep, send = attend_back(
        kv, mixt, att, lse, d_out, normed_all, w_full, gains, d_gain_two, keep, send
    )
    *firsts, keep, send, shares, got_a, got_b = tied(*firsts, keep, send, shares, got_a, got_b)

    got = between_z(firsts[3], TO_MIDDLE)
    both = firsts[2] + jnp.where(inner, got, BF(0))
    outer, middle = between_z(both, TO_MIDDLE), between_z(both, ACROSS)
    pair = between_z(firsts[1] + jnp.where(inner, middle, BF(0)), PAIRS)
    middle = between_z(firsts[3] + outer, ACROSS)

    ups = [shares[0]] + [across_w(shares[e], e) for e in (1, 2, 3)]
    share = jnp.concatenate(ups + [shares[4:].reshape(SHARD, HALF)])
    share_pair, share_mid = between_z(share, PAIRS), between_z(share, ACROSS)
    share_near, share_mid_far = between_z(share_mid, TO_ENDS), between_z(share_pair, ACROSS)
    share_far = between_z(share_mid_far, TO_ENDS)
    blocks = share, share_pair, jnp.where(inner, share_mid, share_near), jnp.where(inner, share_mid_far, share_far)
    grad_up, grad_down = finish_feed(*blocks, *(across_core(block) for block in blocks))

    sums, a_far, b_far = tied(keep + across_core(send), a_far, b_far)
    sums_got = across_w(sums[1], 2)
    sums_far = across_w(sums[0, 1] + sums_got[1], 1)
    sums, a_far, b_far = tied((sums[0, 0] + sums_got[0]) + sums_far, a_far, b_far)
    more_a, more_b = across_w(a_far + got_a[1], 2), across_w(b_far + got_b[1], 1)
    result_keep, result_send = give(hidden, out0, (got_a, more_a, got_b, more_b))
    out_result = both_micros(result_keep, across_core(result_send))
    sums_pair, head_mid = between_z(sums, PAIRS), between_z(sums[:HEAD_ROWS], ACROSS)
    out = sums[HEAD_ROWS:] + sums_pair[HEAD_ROWS:]
    head_near = between_z(head_mid, TO_ENDS)
    sums_far = between_z(jnp.concatenate([sums_pair[:HEAD_ROWS], out]), ACROSS)
    pair, middle, out_result, sums_far, head_near = tied(pair, middle, out_result, sums_far, head_near)
    sums_far = jnp.concatenate([sums_far[:HEAD_ROWS], out + sums_far[HEAD_ROWS:]])
    sums_last = between_z(sums_far, TO_ENDS)
    grad_keep, grad_send = last(firsts[0], pair, middle, x_block, gains, d_hidden)
    out_tokens = both_micros(grad_keep, across_core(grad_send))
    sums_last = jnp.where(inner, sums_far, sums_last)
    head_near = jnp.where(inner, head_mid, head_near)
    blocks = sums[:HEAD_ROWS], sums_pair[:HEAD_ROWS], head_near, sums_last[:HEAD_ROWS]
    others = [across_core(block) for block in (*blocks[:3], sums_last)]
    grad_out, grad_qkv, out_gains = finish_heads(
        *blocks, *others[:3], others[3][:HEAD_ROWS], sums_last[HEAD_ROWS:], others[3][HEAD_ROWS:]
    )
    return (
        out_result,
        out_tokens,
        out_gains[0],
        grad_qkv,
        grad_out,
        out_gains[1],
        grad_up,
        grad_down,
    )


def local(tokens, *rest):
    fits = (
        lax.axis_size("wshard") == 4
        and lax.axis_size("ctx") == 8
        and tokens.shape[:2] == (2, 1)
        and 2 * tokens.shape[2] == TILE
    )
    return (local_grid if fits else local_any)(tokens, *rest)


def solution(mesh):
    placed = (
        P(None, "wshard", "ctx", None),
        P("wshard"),
        P("wshard", None),
        P("wshard", None),
        P("wshard"),
        P("wshard", None),
        P("wshard", None),
        P(None, "wshard", "ctx", None),
    )
    return jax.shard_map(
        local,
        mesh=mesh,
        in_specs=placed,
        out_specs=(
            P(None, "wshard", "ctx", None),
            P(None, "wshard", "ctx", None),
            P("wshard"),
            P("wshard", None),
            P("wshard", None),
            P("wshard"),
            P("wshard", None),
            P("wshard", None),
        ),
        check_vma=False,
    )
```

```python
import jax
import jax.numpy as jnp
from jax import lax
from jax.experimental import pallas as pl
from jax.experimental.pallas import tpu as pltpu
from jax.sharding import PartitionSpec as P

D = 768
HEADS = 12
HEAD_DIM = 64


EPSILON = 1e-05


def passed_along(value, axis, by):
    count = lax.axis_size(axis)
    return lax.ppermute(value, axis, [(i, (i + by) % count) for i in range(count)])


def layer_norm(inputs, scaling):
    centred = inputs - jnp.mean(inputs, axis=-1, keepdims=True)
    variance = jnp.mean(centred * centred, axis=-1, keepdims=True)
    return centred * lax.rsqrt(variance + EPSILON) * scaling


def gelu_smooth(values_in):
    return jax.nn.gelu(values_in, approximate=True)


def contract_rows(left_side, right_side):
    return lax.dot_general(
        left_side, right_side, (((0,), (0,)), ((), ())), preferred_element_type=jnp.float32
    )


def times_rows(left_side, right_side):
    return lax.dot_general(
        left_side, right_side, (((1,), (1,)), ((), ())), preferred_element_type=jnp.float32
    )


def pair_grads(query_h, dout_h, log_total, row_delta, query_pos, key_h, value_h, key_pos):
    scaling = HEAD_DIM ** (-0.5)
    scores = (
        jnp.einsum("qhe,khe->hqk", query_h, key_h, preferred_element_type=jnp.float32) * scaling
    )
    visible = key_pos[None, None, :] <= query_pos[None, :, None]
    magnitude = jnp.sqrt(scores * scores + 1.0)
    tilted = scores / magnitude
    chance = jnp.exp(jnp.where(visible, magnitude - log_total[:, :, None], -1e30))
    signed = (tilted * chance).astype(jnp.bfloat16)
    d_signed = jnp.einsum("qhe,khe->hqk", dout_h, value_h, preferred_element_type=jnp.float32)
    slope = 1.0 / (magnitude * magnitude * magnitude) + tilted * tilted
    d_scores = (chance * (d_signed * slope - tilted * row_delta[:, :, None])).astype(jnp.bfloat16)
    d_query = (
        jnp.einsum("hqk,khe->qhe", d_scores, key_h, preferred_element_type=jnp.float32) * scaling
    )
    d_key = (
        jnp.einsum("hqk,qhe->khe", d_scores, query_h, preferred_element_type=jnp.float32) * scaling
    )
    d_value = jnp.einsum("hqk,qhe->khe", signed, dout_h, preferred_element_type=jnp.float32)
    return (d_query, d_key, d_value)


def keep_state(loop_state):
    return loop_state


def local_any(tokens, gain_one, w_qkv, w_out, gain_two, w_up, w_down, cotangent):
    gathered = (
        lax.all_gather(gain_one, "wshard", axis=0, tiled=True),
        lax.all_gather(w_qkv, "wshard", axis=0, tiled=True),
        lax.all_gather(w_out, "wshard", axis=0, tiled=True),
        lax.all_gather(gain_two, "wshard", axis=0, tiled=True),
        lax.all_gather(w_up, "wshard", axis=0, tiled=True),
        lax.all_gather(w_down, "wshard", axis=0, tiled=True),
    )
    full_gain_one, full_qkv, full_out, full_gain_two, full_up, full_down = gathered
    gain_first = full_gain_one.astype(jnp.float32)
    gain_second = full_gain_two.astype(jnp.float32)
    cycle_size = lax.axis_size("ctx")
    cycle_place = lax.axis_index("ctx")
    micro_count = tokens.shape[0]
    local_len = tokens.shape[2]
    scaling = HEAD_DIM ** (-0.5)
    query_pos = cycle_place * local_len + jnp.arange(local_len, dtype=jnp.int32)
    sum_gain_one = jnp.zeros((D,), jnp.float32)
    sum_gain_two = jnp.zeros((D,), jnp.float32)
    sum_qkv = jnp.zeros(full_qkv.shape, jnp.float32)
    sum_out = jnp.zeros(full_out.shape, jnp.float32)
    sum_up = jnp.zeros(full_up.shape, jnp.float32)
    sum_down = jnp.zeros(full_down.shape, jnp.float32)
    results = []
    grad_list = []
    for micro_index in range(micro_count):
        inputs = tokens[micro_index, 0].astype(jnp.float32)
        normed_f, norm_back = jax.vjp(layer_norm, inputs, gain_first)
        normed = normed_f.astype(jnp.bfloat16)
        mixed_all = jnp.dot(normed, full_qkv, preferred_element_type=jnp.float32).astype(
            jnp.bfloat16
        )
        keys_flat = mixed_all[:, D : 2 * D]
        values_flat = mixed_all[:, 2 * D :]
        query_h = mixed_all[:, :D].reshape(local_len, HEADS, HEAD_DIM)
        key_h = keys_flat.reshape(local_len, HEADS, HEAD_DIM)
        value_h = values_flat.reshape(local_len, HEADS, HEAD_DIM)
        start_state = (
            jnp.zeros((HEADS, local_len, HEAD_DIM), jnp.float32),
            jnp.ones((HEADS, local_len), jnp.float32),
            jnp.zeros((HEADS, local_len), jnp.float32),
        )
        shard_piece = (
            lax.all_gather(keys_flat, "ctx", axis=0, tiled=True),
            lax.all_gather(values_flat, "ctx", axis=0, tiled=True),
        )

        def compute(loop_state):
            accumulated, top_value, totals = loop_state
            key_piece = shard_piece[0].reshape(-1, HEADS, HEAD_DIM)
            value_piece = shard_piece[1].reshape(-1, HEADS, HEAD_DIM)
            key_pos = jnp.arange(key_piece.shape[0], dtype=jnp.int32)
            scores = (
                jnp.einsum("qhe,khe->hqk", query_h, key_piece, preferred_element_type=jnp.float32)
                * scaling
            )
            visible = key_pos[None, None, :] <= query_pos[None, :, None]
            magnitude = jnp.sqrt(scores * scores + 1.0)
            new_top = jnp.maximum(top_value, jnp.max(jnp.where(visible, magnitude, 0.0), axis=-1))
            weighted = jnp.exp(jnp.where(visible, magnitude - new_top[:, :, None], -1e30))
            signed = (scores / magnitude * weighted).astype(jnp.bfloat16)
            accumulated = jnp.einsum(
                "hqk,khe->hqe", signed, value_piece, preferred_element_type=jnp.float32
            )
            totals = jnp.sum(weighted, axis=-1)
            return (accumulated, new_top, totals)

        accumulated, top_value, totals = lax.cond(
            jnp.int32(0) <= query_pos[-1], compute, keep_state, start_state
        )
        attended_h = accumulated / totals[:, :, None]
        log_total = top_value + jnp.log(totals)
        attended = jnp.transpose(attended_h, (1, 0, 2)).reshape(local_len, D)
        attended_low = attended.astype(jnp.bfloat16)
        hidden = inputs + jnp.dot(attended_low, full_out, preferred_element_type=jnp.float32)
        normed_two_f, norm_two_back = jax.vjp(layer_norm, hidden, gain_second)
        normed_two = normed_two_f.astype(jnp.bfloat16)
        upward = jnp.dot(normed_two, full_up, preferred_element_type=jnp.float32)
        active_f, gelu_back = jax.vjp(gelu_smooth, upward)
        active = active_f.astype(jnp.bfloat16)
        result_rows = hidden + jnp.dot(active, full_down, preferred_element_type=jnp.float32)
        results.append(result_rows.astype(jnp.bfloat16))
        d_result = cotangent[micro_index, 0]
        sum_down = sum_down + contract_rows(active, d_result)
        d_active = times_rows(d_result, full_down)
        d_upward = gelu_back(d_active)[0].astype(jnp.bfloat16)
        sum_up = sum_up + contract_rows(normed_two, d_upward)
        d_normed_two = times_rows(d_upward, full_up)
        d_hidden_norm, d_gain_two = norm_two_back(d_normed_two)
        sum_gain_two = sum_gain_two + d_gain_two
        d_hidden = d_result.astype(jnp.float32) + d_hidden_norm
        d_branch = d_hidden.astype(jnp.bfloat16)
        sum_out = sum_out + contract_rows(attended_low, d_branch)
        d_attended = times_rows(d_branch, full_out).astype(jnp.bfloat16)
        dout_h = d_attended.reshape(local_len, HEADS, HEAD_DIM)
        row_delta = jnp.einsum("qhe,hqe->hq", dout_h.astype(jnp.float32), attended_h)
        zero_block = jnp.zeros((local_len, HEADS, HEAD_DIM), jnp.float32)

        def turn_keys(turn_index, loop_state):
            key_b, value_b, d_key_b, d_value_b, d_query = loop_state
            owner_index = (cycle_place + turn_index) % cycle_size
            key_pos = owner_index * local_len + jnp.arange(local_len, dtype=jnp.int32)

            def work(partial_sums):
                contrib = pair_grads(
                    query_h, dout_h, log_total, row_delta, query_pos, key_b, value_b, key_pos
                )
                return (
                    partial_sums[0] + contrib[0],
                    partial_sums[1] + contrib[1],
                    partial_sums[2] + contrib[2],
                )

            needed = (turn_index == 0) | (cycle_place + turn_index >= cycle_size)
            d_query, d_key_b, d_value_b = lax.cond(
                needed, work, keep_state, (d_query, d_key_b, d_value_b)
            )
            key_b, value_b = passed_along((key_b, value_b), "ctx", -1)
            d_key_b, d_value_b = (
                passed_along(d_key_b.astype(jnp.bfloat16), "ctx", -1).astype(d_key_b.dtype),
                passed_along(d_value_b.astype(jnp.bfloat16), "ctx", -1).astype(d_value_b.dtype),
            )
            return (key_b, value_b, d_key_b, d_value_b, d_query)

        final_state = lax.fori_loop(
            0, cycle_size, turn_keys, (key_h, value_h, zero_block, zero_block, zero_block)
        )
        d_key = final_state[2]
        d_value = final_state[3]
        d_query = final_state[4]
        d_mixed = jnp.concatenate(
            [
                d_query.reshape(local_len, D),
                d_key.reshape(local_len, D),
                d_value.reshape(local_len, D),
            ],
            axis=1,
        ).astype(jnp.bfloat16)
        sum_qkv = sum_qkv + contract_rows(normed, d_mixed)
        d_normed = times_rows(d_mixed, full_qkv)
        d_inputs_norm, d_gain_one = norm_back(d_normed)
        sum_gain_one = sum_gain_one + d_gain_one
        grad_list.append(d_hidden + d_inputs_norm)
    shares = (
        lax.psum_scatter(
            sum_gain_one.astype(jnp.bfloat16), "wshard", scatter_dimension=0, tiled=True
        ).astype(jnp.float32),
        lax.psum_scatter(
            sum_qkv.astype(jnp.bfloat16), "wshard", scatter_dimension=0, tiled=True
        ).astype(jnp.float32),
        lax.psum_scatter(
            sum_out.astype(jnp.bfloat16), "wshard", scatter_dimension=0, tiled=True
        ).astype(jnp.float32),
        lax.psum_scatter(
            sum_gain_two.astype(jnp.bfloat16), "wshard", scatter_dimension=0, tiled=True
        ).astype(jnp.float32),
        lax.psum_scatter(
            sum_up.astype(jnp.bfloat16), "wshard", scatter_dimension=0, tiled=True
        ).astype(jnp.float32),
        lax.psum_scatter(
            sum_down.astype(jnp.bfloat16), "wshard", scatter_dimension=0, tiled=True
        ).astype(jnp.float32),
    )
    summed = (
        lax.psum(shares[0].astype(jnp.bfloat16), "ctx").astype(jnp.float32),
        lax.psum(shares[1].astype(jnp.bfloat16), "ctx").astype(jnp.float32),
        lax.psum(shares[2].astype(jnp.bfloat16), "ctx").astype(jnp.float32),
        lax.psum(shares[3].astype(jnp.bfloat16), "ctx").astype(jnp.float32),
        lax.psum(shares[4].astype(jnp.bfloat16), "ctx").astype(jnp.float32),
        lax.psum(shares[5].astype(jnp.bfloat16), "ctx").astype(jnp.float32),
    )
    result_out = jnp.stack(results)[:, None]
    grad_out_tokens = jnp.stack(grad_list)[:, None]
    return (
        result_out,
        grad_out_tokens,
        summed[0],
        summed[1],
        summed[2],
        summed[3],
        summed[4],
        summed[5],
    )


BF = jnp.bfloat16
F32 = jnp.float32
TILE = 256
SHARD = D // 4
OWN_HEADS = HEADS // 4
OWN = OWN_HEADS * HEAD_DIM
MIX = 3 * OWN
HEAD_ROWS = 160
PART = SHARD // 2
QUART = SHARD // 4
HALF = D // 2
MIDDLE_ROW = 224
VMEM_LIMIT = 56 * 1024 * 1024
WHOLE = pl.BlockSpec(memory_space=pltpu.VMEM)
ANYWHERE = pl.BlockSpec(memory_space=pl.ANY)


def nn(a, b):
    return lax.dot_general(a, b, (((1,), (0,)), ((), ())), preferred_element_type=F32)


def nt(a, b):
    return lax.dot_general(a, b, (((1,), (1,)), ((), ())), preferred_element_type=F32)


def normalised(x):
    centred = x - jnp.mean(x, axis=-1, keepdims=True)
    variance = jnp.mean(centred * centred, axis=-1, keepdims=True)
    inverse = lax.rsqrt(variance + EPSILON)
    return centred * inverse, inverse


def norm_back(xhat, inverse, gain, dy):
    g = dy * gain
    mean_g = jnp.mean(g, axis=-1, keepdims=True)
    mean_gx = jnp.mean(g * xhat, axis=-1, keepdims=True)
    return (g - mean_g - xhat * mean_gx) * inverse


def causal_tile():
    rows = lax.broadcasted_iota(jnp.int32, (TILE, TILE), 0)
    cols = lax.broadcasted_iota(jnp.int32, (TILE, TILE), 1)
    return rows <= cols


def call(kernel, name, ins, outs, scratch, flops, args, out_specs=None):
    moved = sum(a.size * a.dtype.itemsize for a in args)
    return pl.pallas_call(
        kernel,
        in_specs=ins,
        out_specs=out_specs or [WHOLE] * len(outs),
        out_shape=[jax.ShapeDtypeStruct(shape, kind) for shape, kind in outs],
        scratch_shapes=scratch,
        compiler_params=pltpu.CompilerParams(vmem_limit_bytes=VMEM_LIMIT),
        cost_estimate=pl.CostEstimate(flops=1000, bytes_accessed=1000, transcendentals=0),
        name=name,
    )(*args)


def shard_rows_of(pieces, which, first, count):
    if which < 3:
        return pieces[which].at[pl.ds(first, count)]
    half = pieces[3].shape[0]
    if first < half:
        return pieces[3].at[pl.ds(first, count)]
    return pieces[4].at[pl.ds(first - half, count)]


def run_copies(pairs, sems):
    copies = [pltpu.make_async_copy(src, dst, sems.at[i]) for i, (src, dst) in enumerate(pairs)]
    for copy in copies:
        copy.start()
    for copy in copies:
        copy.wait()


def attend_kernel(x_ref, w0, w1, w2, w3, w4,
                  normed_out, kv_out, mixt_out, att_ref, low_ref, lse_ref, wfull_out, gains_ref,
                  normed_ref, kv_ref, mixt_ref, wfull_ref, s_ref, g_ref, wsems, sems):
    place = lax.axis_index("wshard")
    pieces = (w0, w1, w2, w3, w4)
    half = w3.shape[0]
    pairs = []
    for k in range(4):
        to = pl.multiple_of(jnp.bitwise_xor(place, k) * SHARD, SHARD)
        if k < 3:
            pairs.append((shard_rows_of(pieces, k, 0, SHARD), wfull_ref.at[pl.ds(to, SHARD)]))
        else:
            pairs.append((w3, wfull_ref.at[pl.ds(to, half)]))
            pairs.append((w4.at[pl.ds(0, SHARD - half)], wfull_ref.at[pl.ds(to + half, SHARD - half)]))
        source = w4.at[pl.ds(SHARD - half, 16)] if k == 3 else pieces[k].at[pl.ds(SHARD, 16)]
        pairs.append((source, g_ref.at[k]))
    run_copies(pairs, wsems)
    gains = jnp.concatenate([g_ref[jnp.bitwise_xor(place, j)][0:8, 0:SHARD].astype(F32) for j in range(4)], axis=1)
    gains_ref[...] = gains
    for row in range(4):
        here = slice(row * TILE, (row + 1) * TILE)
        xhat, _ = normalised(x_ref[row].astype(F32))
        normed = (xhat * gains[0:1]).astype(BF)
        normed_ref[here, :] = normed
        mix = nn(normed, wfull_ref[...]).astype(BF)
        mixt_ref[:, here] = mix.T
        for h in range(OWN_HEADS):
            kv_ref[h, here, 0:HEAD_DIM] = mix[:, OWN + h * HEAD_DIM : OWN + (h + 1) * HEAD_DIM]
            kv_ref[h, here, HEAD_DIM:] = mix[:, 2 * OWN + h * HEAD_DIM : 2 * OWN + (h + 1) * HEAD_DIM]

    pairs = ((normed_ref, normed_out), (kv_ref, kv_out), (mixt_ref, mixt_out), (wfull_ref, wfull_out))
    copies = [pltpu.make_async_copy(src, dst, sems.at[k]) for k, (src, dst) in enumerate(pairs)]
    for copy in copies:
        copy.start()

    @pl.loop(0, OWN_HEADS)
    def _(h):
        base = pl.multiple_of(h * HEAD_DIM, HEAD_DIM)
        for block in range(4):
            here = slice(block * TILE, (block + 1) * TILE)
            queries = mixt_ref[pl.ds(base, HEAD_DIM), here] * BF(HEAD_DIM**-0.5)
            top = jnp.zeros((1, TILE), F32)
            for other in range(block + 1):
                there = slice(other * TILE, (other + 1) * TILE)
                s = nn(kv_ref[h, there, 0:HEAD_DIM], queries)
                s_ref[there, :] = s
                size = jnp.abs(s)
                if other == block:
                    size = jnp.where(causal_tile(), size, 0.0)
                top = jnp.maximum(top, jnp.max(size, axis=0, keepdims=True))
            top = jnp.sqrt(top * top + 1.0)
            total = jnp.zeros((1, TILE), F32)
            acc = jnp.zeros((HEAD_DIM, TILE), F32)
            for other in range(block + 1):
                there = slice(other * TILE, (other + 1) * TILE)
                s = s_ref[there, :]
                square = s * s + 1.0
                r = lax.rsqrt(square)
                p = jnp.exp(square * r - top)
                if other == block:
                    p = jnp.where(causal_tile(), p, 0.0)
                total = total + jnp.sum(p, axis=0, keepdims=True)
                signed = (s * r * p).astype(BF)
                acc = acc + nn(mixt_ref[pl.ds(2 * OWN + base, HEAD_DIM), there], signed)
            att = acc / total
            att_ref[pl.ds(base, HEAD_DIM), here] = att
            low_ref[block, pl.ds(base, HEAD_DIM), :] = att.astype(BF)
            lse_ref[pl.ds(h, 1), here] = top + jnp.log(total)

    for copy in copies:
        copy.wait()


def attend(x_all, pieces):
    length = 4 * TILE
    return call(
        attend_kernel,
        "attend",
        [WHOLE] + [ANYWHERE] * 5,
        [
            ((length, D), BF),
            ((OWN_HEADS, length, 2 * HEAD_DIM), BF),
            ((MIX, length), BF),
            ((OWN, length), F32),
            ((4, OWN, TILE), BF),
            ((8, length), F32),
            ((D, MIX), BF),
            ((8, D), F32),
        ],
        [
            pltpu.VMEM((length, D), BF),
            pltpu.VMEM((OWN_HEADS, length, 2 * HEAD_DIM), BF),
            pltpu.VMEM((MIX, length), BF),
            pltpu.VMEM((D, MIX), BF),
            pltpu.VMEM((length, TILE), F32),
            pltpu.VMEM((4, 16, MIX), BF),
            pltpu.SemaphoreType.DMA((9,)),
            pltpu.SemaphoreType.DMA((4,)),
        ],
        3 * 10**9,
        (x_all, *pieces),
        [ANYWHERE] * 3 + [WHOLE] * 3 + [ANYWHERE, WHOLE],
    )


def parcel_kernel(cot_ref, wout_ref, wup_ref, x_on_ref, x_ref, y_on_ref, y_ref, sems):
    place = lax.axis_index("wshard")

    def columns(k, first, count):
        at = pl.multiple_of(jnp.bitwise_xor(place, k) * D, D)
        return wup_ref.at[pl.ds(first, count), pl.ds(at, D)]

    low, high = cot_ref.at[pl.ds(0, MIDDLE_ROW)], cot_ref.at[pl.ds(MIDDLE_ROW, 32)]
    pairs = (
        (low, x_on_ref.at[pl.ds(0, MIDDLE_ROW)]),
        (columns(3, 0, PART), x_on_ref.at[pl.ds(MIDDLE_ROW, PART)]),
        (high, y_on_ref.at[pl.ds(0, 32)]),
        (wout_ref, y_on_ref.at[pl.ds(32, SHARD)]),
        (columns(3, PART, PART), y_on_ref.at[pl.ds(MIDDLE_ROW, PART)]),
        (columns(1, 0, SHARD), x_ref.at[pl.ds(0, SHARD)]),
        (high, x_ref.at[pl.ds(SHARD, 32)]),
        (wout_ref, x_ref.at[pl.ds(SHARD + 32, SHARD)]),
        (columns(2, 0, SHARD), y_ref.at[pl.ds(0, SHARD)]),
        (low, y_ref.at[pl.ds(SHARD, MIDDLE_ROW)]),
    )
    run_copies(pairs, sems)


def parcels(cot, w_out, w_up):
    on, rest = MIDDLE_ROW + PART, SHARD + MIDDLE_ROW
    return call(
        parcel_kernel,
        "parcels",
        [ANYWHERE] * 3,
        [((on, D), BF), ((rest, D), BF)] * 2,
        [pltpu.SemaphoreType.DMA((10,))],
        10**6,
        (cot, w_out, w_up),
    )


def assemble_kernel(cot_ref, own_ref, wup_ref, x_on, x_rest, y_on, y_rest, corner_a, corner_b,
                    wout_ref, up_ref, cots_ref, sems):
    place = lax.axis_index("wshard")
    at = [pl.multiple_of(jnp.bitwise_xor(place, k) * SHARD, SHARD) for k in range(4)]
    half = PART
    mine = pl.multiple_of(place * D, D)
    pairs = (
        (own_ref, wout_ref.at[pl.ds(at[0], SHARD)]),
        (x_rest.at[pl.ds(SHARD + 32, SHARD)], wout_ref.at[pl.ds(at[1], SHARD)]),
        (y_on.at[pl.ds(32, SHARD)], wout_ref.at[pl.ds(at[2], SHARD)]),
        (corner_b.at[pl.ds(32, SHARD)], wout_ref.at[pl.ds(at[3], SHARD)]),
        (wup_ref.at[:, pl.ds(mine, D)], up_ref.at[pl.ds(at[0], SHARD)]),
        (x_rest.at[pl.ds(0, SHARD)], up_ref.at[pl.ds(at[1], SHARD)]),
        (y_rest.at[pl.ds(0, SHARD)], up_ref.at[pl.ds(at[2], SHARD)]),
        (corner_a.at[pl.ds(MIDDLE_ROW, half)], up_ref.at[pl.ds(at[3], half)]),
        (corner_b.at[pl.ds(MIDDLE_ROW, half)], up_ref.at[pl.ds(at[3] + half, half)]),
        (cot_ref, cots_ref.at[pl.ds(0, TILE)]),
        (x_on.at[pl.ds(0, MIDDLE_ROW)], cots_ref.at[pl.ds(TILE, MIDDLE_ROW)]),
        (x_rest.at[pl.ds(SHARD, 32)], cots_ref.at[pl.ds(TILE + MIDDLE_ROW, 32)]),
        (y_rest.at[pl.ds(SHARD, MIDDLE_ROW)], cots_ref.at[pl.ds(2 * TILE, MIDDLE_ROW)]),
        (y_on.at[pl.ds(0, 32)], cots_ref.at[pl.ds(2 * TILE + MIDDLE_ROW, 32)]),
        (corner_a.at[pl.ds(0, MIDDLE_ROW)], cots_ref.at[pl.ds(3 * TILE, MIDDLE_ROW)]),
        (corner_b.at[pl.ds(0, 32)], cots_ref.at[pl.ds(3 * TILE + MIDDLE_ROW, 32)]),
    )
    run_copies(pairs, sems)


def assemble(cot, w_out, w_up, shared):
    return call(
        assemble_kernel,
        "assemble",
        [ANYWHERE] * 9,
        [((D, D), BF), ((D, D), BF), ((4 * TILE, D), BF)],
        [pltpu.SemaphoreType.DMA((16,))],
        10**6,
        (cot, w_out, w_up, *shared),
    )


def project_kernel(att_ref, x_ref, gain_ref, wout_ref, hidden_ref, normed_ref):
    hidden = x_ref[...].astype(F32) + nn(att_ref[...].T, wout_ref[...])
    hidden_ref[...] = hidden
    xhat, _ = normalised(hidden)
    normed_ref[...] = (xhat * gain_ref[1:2]).astype(BF)


def project(att_home, x_block, gain, w_out):
    rows = x_block.shape[0]
    return call(
        project_kernel,
        "project",
        [WHOLE] * 4,
        [((rows, D), F32), ((rows, D), BF)],
        [],
        3 * 10**8,
        (att_home, x_block, gain, w_out),
    )


SLOPE = (2.0 / 3.141592653589793) ** 0.5


def feed_rows(n, cot, up_ref, down_ref, active_ref, dup_ref, here):
    for first in range(0, D, TILE):
        cols = slice(first, first + TILE)
        u = nn(n, up_ref[:, cols])
        square = u * u
        t = jnp.tanh(SLOPE * (u + 0.044715 * (square * u)))
        side = 0.5 + 0.5 * t
        active_ref[here, cols] = (u * side).astype(BF)
        grad = side + (0.5 * SLOPE) * u * (1.0 - t * t) * (1.0 + 0.134145 * square)
        dup_ref[here, cols] = (grad * nt(cot, down_ref[cols, :])).astype(BF)
    return nn(active_ref[here, :], down_ref[...]), nt(dup_ref[here, :], up_ref[...])


def feed_own_kernel(n_ref, cot_ref, up_ref, down_ref, active_ref, dup_ref, out_ref, dout_ref):
    out_ref[...], dout_ref[...] = feed_rows(
        n_ref[...], cot_ref[0:TILE, :], up_ref, down_ref, active_ref, dup_ref, slice(0, TILE)
    )


def feed_own(n, cots, up, down):
    return call(
        feed_own_kernel,
        "feed_own",
        [WHOLE] * 4,
        [((TILE, D), BF), ((TILE, D), BF), ((TILE, D), F32), ((TILE, D), F32)],
        [],
        2 * 10**9,
        (n, cots, up, down),
    )


def feed_near_kernel(nx_ref, ny_ref, cot_ref, up_ref, down_ref, active_ref, dup_ref, out_ref, dout_ref):
    for k, n_ref in enumerate((nx_ref, ny_ref)):
        here = slice(k * TILE, (k + 1) * TILE)
        out, dout = feed_rows(n_ref[...], cot_ref[(k + 1) * TILE : (k + 2) * TILE, :], up_ref, down_ref, active_ref, dup_ref, here)
        out_ref[here, :], dout_ref[here, :] = out.astype(BF), dout.astype(BF)


def feed_near(nx, ny, cots, up, down):
    return call(
        feed_near_kernel,
        "feed_near",
        [WHOLE] * 5,
        [((2 * TILE, D), BF)] * 4,
        [],
        4 * 10**9,
        (nx, ny, cots, up, down),
    )


def feed_far_kernel(na_ref, nb_ref, cot_ref, out_ref, dout_ref, up_ref, down_ref,
                    active_ref, dup_ref, oa_ref, oaf_ref, ob_ref, obf_ref, da_ref, daf_ref, db_ref, dbf_ref):
    n = jnp.concatenate([na_ref[...], nb_ref[...]])
    cot = cot_ref[3 * TILE :, :]
    half = TILE // 2
    out, dout = feed_rows(n, cot, up_ref, down_ref, active_ref, dup_ref, slice(0, TILE))
    for far, near, a, af, b, bf in (
        (out, out_ref, oa_ref, oaf_ref, ob_ref, obf_ref),
        (dout, dout_ref, da_ref, daf_ref, db_ref, dbf_ref),
    ):
        far = far.astype(BF)
        a[0], a[1] = near[0:half, :], far[0:half]
        b[0], b[1] = near[TILE + half :, :], far[half:]
        af[...] = near[TILE : TILE + half, :]
        bf[...] = near[half:TILE, :]


def feed_far(na, nb, cots, out, dout, up, down):
    half = TILE // 2
    return call(
        feed_far_kernel,
        "feed_far",
        [WHOLE] * 7,
        [((TILE, D), BF)] * 2 + [((2, half, D), BF), ((half, D), BF)] * 4,
        [],
        2 * 10**9,
        (na, nb, cots, out, dout, up, down),
    )


def feed_grads_kernel(n0, n1, n2, n3, n4, cot_ref, a0, a1, a2, d0, d1, d2,
                      shares_ref, nt_ref, at_ref, dup_ref):
    for k, piece in enumerate((n0, n1, n2)):
        nt_ref[:, k * TILE : (k + 1) * TILE] = piece[...].T
    nt_ref[:, 3 * TILE :] = jnp.concatenate([n3[...], n4[...]]).T
    at_ref[:, 0:TILE] = a0[...].T
    at_ref[:, TILE : 3 * TILE] = a1[...].T
    at_ref[:, 3 * TILE :] = a2[...].T
    dup_ref[0:TILE] = d0[...]
    dup_ref[TILE : 3 * TILE] = d1[...]
    dup_ref[3 * TILE :] = d2[...]
    rows = D // 8
    for k in range(8):
        g = nn(at_ref[k * rows : (k + 1) * rows, :], cot_ref[...]).astype(BF)
        for side in range(2):
            for part in range(2):
                piece = g[part * QUART : (part + 1) * QUART, side * HALF : (side + 1) * HALF]
                shares_ref[k, 4 + 2 * side + part] = piece
    for to in range(4):
        g = nn(nt_ref[to * SHARD : (to + 1) * SHARD, :], dup_ref[...]).astype(BF)
        slot = jnp.bitwise_xor(lax.axis_index("wshard"), to)
        for k in range(8):
            r, c = (k // 2) * QUART, (k % 2) * HALF
            shares_ref[k, slot] = g[r : r + QUART, c : c + HALF]


def feed_grads(ns, cots, actives, dups):
    length = 4 * TILE
    return call(
        feed_grads_kernel,
        "feed_grads",
        [WHOLE] * 12,
        [((8, 8, QUART, HALF), BF)],
        [
            pltpu.VMEM((D, length), BF),
            pltpu.VMEM((D, length), BF),
            pltpu.VMEM((length, D), BF),
        ],
        3 * 10**9,
        (*ns, cots, *actives, *dups),
    )[0]


def summed(keep_ref, a_ref, a_more_ref, b_ref, b_more_ref):
    first = a_ref[0].astype(F32) + a_more_ref[...].astype(F32)
    second = b_ref[0].astype(F32) + b_more_ref[...].astype(F32)
    return keep_ref[...] + jnp.concatenate([first, second])


def give_kernel(hidden_ref, keep_ref, a_ref, a_more_ref, b_ref, b_more_ref, rkeep_ref, rsend_ref, result_ref, sems):
    core = lax.axis_index("ctx") % 2
    result = (hidden_ref[...] + summed(keep_ref, a_ref, a_more_ref, b_ref, b_more_ref)).astype(BF)
    half = TILE // 2
    result_ref[0], result_ref[1] = result[:half], result[half:]
    run_copies(((result_ref.at[1 - core], rsend_ref), (result_ref.at[core], rkeep_ref)), sems)


def give(hidden, keep, parts):
    half = TILE // 2
    return call(
        give_kernel,
        "give",
        [WHOLE] * 6,
        [((half, D), BF)] * 2,
        [pltpu.VMEM((2, half, D), BF), pltpu.SemaphoreType.DMA((2,))],
        10**6,
        (hidden, keep, *parts),
        [ANYWHERE] * 2,
    )


def turn_kernel(hidden_ref, gain_ref, dkeep_ref, a_ref, a_more_ref, b_ref, b_more_ref, cot_ref, wout_ref,
                dhidden_ref, datt_ref, dbranch_ref, dgain_ref):
    gain = gain_ref[1:2]
    xhat, inverse = normalised(hidden_ref[...])
    dy = summed(dkeep_ref, a_ref, a_more_ref, b_ref, b_more_ref)
    dgain_ref[...] = jnp.sum(dy * xhat, axis=0, keepdims=True)
    d_hidden = cot_ref[...].astype(F32) + norm_back(xhat, inverse, gain, dy)
    dhidden_ref[...] = d_hidden
    d_branch = d_hidden.astype(BF)
    dbranch_ref[...] = d_branch
    d_att = nt(wout_ref[...], d_branch).astype(BF)
    for k in range(4):
        datt_ref[k] = d_att[k * OWN : (k + 1) * OWN]


def turn(hidden, gain, dkeep, parts, cot, w_out):
    rows = hidden.shape[0]
    return call(
        turn_kernel,
        "turn",
        [WHOLE] * 9,
        [((rows, D), F32), ((4, OWN, rows), BF), ((rows, D), BF), ((1, D), F32)],
        [],
        6 * 10**8,
        (hidden, gain, dkeep, *parts, cot, w_out),
    )


def out_grad_kernel(att_ref, dbranch_ref, keep_ref, send_ref, grad_ref, sems):
    core = lax.axis_index("ctx") % 2
    place = lax.axis_index("wshard")
    for to in range(4):
        e = jnp.bitwise_xor(place, to)
        e_x, e_y = jnp.bitwise_and(e, 1), e // 2
        g = nn(att_ref[to * SHARD : (to + 1) * SHARD, :], dbranch_ref[...]).astype(BF)
        for side in range(2):
            for half in range(2):
                piece = g[side * PART : (side + 1) * PART, half * HALF : (half + 1) * HALF]
                grad_ref[side, e_y, e_x, half * PART : (half + 1) * PART] = piece
    rows = pl.ds(HEAD_ROWS, SHARD)
    pairs = ((grad_ref.at[1 - core], send_ref.at[:, :, rows]), (grad_ref.at[core], keep_ref.at[:, :, rows]))
    run_copies(pairs, sems)


def out_grad(att_home, d_branch):
    return call(
        out_grad_kernel,
        "out_grad",
        [WHOLE] * 2,
        [((2, 2, HEAD_ROWS + SHARD, HALF), BF)] * 2,
        [pltpu.VMEM((2, 2, 2, SHARD, HALF), BF), pltpu.SemaphoreType.DMA((2,))],
        3 * 10**8,
        (att_home, d_branch),
        [ANYWHERE] * 2,
    )


def attend_back_kernel(kv_ref, mixt_ref, att_ref, lse_ref, dout_ref, normed_in, w_in, gain_ref, dgain_ref, _, __,
                       f0_ref, f1_ref, f2_ref, f3_ref, gkeep_ref, gsend_ref,
                       dq_ref, dk_ref, dv_ref, dm_ref, mix_ref, total_ref, first_ref, head_ref, sems,
                       normed_ref, w_ref, in_sems):
    length = kv_ref.shape[1]
    loads = [
        pltpu.make_async_copy(normed_in, normed_ref, in_sems.at[0]),
        pltpu.make_async_copy(w_in, w_ref, in_sems.at[1]),
    ]
    for load in loads:
        load.start()
    scale = BF(HEAD_DIM**-0.5)
    core = lax.axis_index("ctx") % 2
    z = lax.axis_index("ctx") // 2
    place = lax.axis_index("wshard")

    @pl.loop(0, OWN_HEADS)
    def _(h):
        base = pl.multiple_of(h * HEAD_DIM, HEAD_DIM)
        for block in range(4):
            here = slice(block * TILE, (block + 1) * TILE)
            queries = mixt_ref[pl.ds(base, HEAD_DIM), here] * scale
            dout = dout_ref[block, pl.ds(base, HEAD_DIM), :]
            delta = jnp.sum(dout.astype(F32) * att_ref[pl.ds(base, HEAD_DIM), here], axis=0, keepdims=True)
            lse = lse_ref[pl.ds(h, 1), here]
            acc = jnp.zeros((HEAD_DIM, TILE), F32)
            for other in range(block + 1):
                there = slice(other * TILE, (other + 1) * TILE)
                s = nn(kv_ref[h, there, 0:HEAD_DIM], queries)
                ds = nn(kv_ref[h, there, HEAD_DIM:], dout)
                square = s * s + 1.0
                r = lax.rsqrt(square)
                chance = jnp.exp(square * r - lse)
                if other == block:
                    chance = jnp.where(causal_tile(), chance, 0.0)
                tilted = s * r
                signed = (tilted * chance).astype(BF)
                slope = r * r * r + tilted * tilted
                dsc = (chance * (ds * slope - tilted * delta)).astype(BF)
                acc = acc + nn(mixt_ref[pl.ds(OWN + base, HEAD_DIM), there], dsc)
                dk = nt(dsc, queries)
                dv = nt(signed, dout)
                if other == block:
                    dk_ref[there, :] = dk
                    dv_ref[there, :] = dv
                else:
                    dk_ref[there, :] += dk
                    dv_ref[there, :] += dv
            dq_ref[:, here] = acc * HEAD_DIM**-0.5
        dm_ref[h, :, 0:HEAD_DIM] = dq_ref[...].T.astype(BF)
        dm_ref[h, :, HEAD_DIM : 2 * HEAD_DIM] = dk_ref[...].astype(BF)
        dm_ref[h, :, 2 * HEAD_DIM :] = dv_ref[...].astype(BF)

    for h in range(OWN_HEADS):
        for kind in range(3):
            to = kind * OWN + h * HEAD_DIM
            mix_ref[:, to : to + HEAD_DIM] = dm_ref[h, :, kind * HEAD_DIM : (kind + 1) * HEAD_DIM]
    total_ref[...] = jnp.zeros_like(total_ref)
    for load in loads:
        load.wait()
    for block in range(4):
        here = slice(block * TILE, (block + 1) * TILE)
        first = nt(mix_ref[here, :], w_ref[...])
        first_ref[block] = first.astype(BF)
        total_ref[...] += jnp.sum(first * normed_ref[here, :].astype(F32), axis=0, keepdims=True)
    outs = (f3_ref, f2_ref, f1_ref, f0_ref)
    copies = [
        pltpu.make_async_copy(first_ref.at[jnp.bitwise_xor(z, 3 - k)], ref, sems.at[k]) for k, ref in enumerate(outs)
    ]
    for copy in copies:
        copy.start()
    gain_one = total_ref[...] / gain_ref[0:1]
    gain_two = dgain_ref[...]
    for to in range(4):
        e = jnp.bitwise_xor(place, to)
        e_x, e_y = jnp.bitwise_and(e, 1), e // 2
        g = nn(normed_ref[:, to * SHARD : (to + 1) * SHARD].T, mix_ref[...]).astype(BF)
        span = slice(to * SHARD, (to + 1) * SHARD)
        gains = jnp.concatenate([gain_one[:, span], gain_two[:, span], jnp.zeros((14, SHARD), F32)], axis=0)
        gains = jnp.concatenate([gains, jnp.zeros((16, HALF - SHARD), F32)], axis=1).astype(BF)
        for side in range(2):
            at = side * PART
            head_ref[side, e_y, e_x, 0:PART] = g[at : at + PART, 0:HALF]
            head_ref[side, e_y, e_x, PART : PART + QUART, 0:OWN] = g[at : at + QUART, HALF:]
            head_ref[side, e_y, e_x, PART : PART + QUART, OWN:] = g[at + QUART : at + PART, HALF:]
            head_ref[side, e_y, e_x, PART + QUART :] = gains if side == 0 else jnp.zeros_like(gains)
    more = [
        pltpu.make_async_copy(head_ref.at[1 - core], gsend_ref.at[:, :, pl.ds(0, HEAD_ROWS)], sems.at[4]),
        pltpu.make_async_copy(head_ref.at[core], gkeep_ref.at[:, :, pl.ds(0, HEAD_ROWS)], sems.at[5]),
    ]
    for copy in more:
        copy.start()
    for copy in copies + more:
        copy.wait()


def attend_back(kv, mixt, att, lse, dout, normed, w, gain, dgain, keep, send):
    length = normed.shape[0]
    return pl.pallas_call(
        attend_back_kernel,
        in_specs=[WHOLE] * 5 + [ANYWHERE] * 2 + [WHOLE] * 2 + [ANYWHERE] * 2,
        out_specs=[ANYWHERE] * 6,
        out_shape=[jax.ShapeDtypeStruct((TILE, D), BF)] * 4 + [jax.ShapeDtypeStruct(keep.shape, BF)] * 2,
        input_output_aliases={9: 4, 10: 5},
        scratch_shapes=[
            pltpu.VMEM((HEAD_DIM, length), F32),
            pltpu.VMEM((length, HEAD_DIM), F32),
            pltpu.VMEM((length, HEAD_DIM), F32),
            pltpu.VMEM((OWN_HEADS, length, 3 * HEAD_DIM), BF),
            pltpu.VMEM((length, MIX), BF),
            pltpu.VMEM((1, D), F32),
            pltpu.VMEM((4, TILE, D), BF),
            pltpu.VMEM((2, 2, 2, HEAD_ROWS, HALF), BF),
            pltpu.SemaphoreType.DMA((6,)),
            pltpu.VMEM((length, D), BF),
            pltpu.VMEM((D, MIX), BF),
            pltpu.SemaphoreType.DMA((2,)),
        ],
        compiler_params=pltpu.CompilerParams(vmem_limit_bytes=VMEM_LIMIT),
        cost_estimate=pl.CostEstimate(flops=1000, bytes_accessed=1000, transcendentals=0),
        name="attend_back",
    )(kv, mixt, att, lse, dout, normed, w, gain, dgain, keep, send)


def is_inner():
    z = lax.axis_index("ctx") // 2
    return (z == 1) | (z == 2)


def last_kernel(first_ref, pair_ref, middle_ref, x_ref, gain_ref, dhidden_ref, keep_ref, send_ref, grad_ref, sems):
    core = lax.axis_index("ctx") % 2
    rows = x_ref.shape[0] // 2
    dy = first_ref[...].astype(F32) + pair_ref[...].astype(F32)
    dy = dy + jnp.where(is_inner(), middle_ref[...].astype(F32), 0.0)
    xhat, inverse = normalised(x_ref[...].astype(F32))
    grad = dhidden_ref[...] + norm_back(xhat, inverse, gain_ref[0:1], dy)
    grad_ref[0], grad_ref[1] = grad[:rows], grad[rows:]
    run_copies(((grad_ref.at[1 - core], send_ref), (grad_ref.at[core], keep_ref)), sems)


def last(*args):
    rows = TILE // 2
    return call(
        last_kernel,
        "last",
        [WHOLE] * 6,
        [((rows, D), F32), ((rows, D), F32)],
        [pltpu.VMEM((2, rows, D), F32), pltpu.SemaphoreType.DMA((2,))],
        10**7,
        args,
        [ANYWHERE] * 2,
    )


def line_slots():
    z = lax.axis_index("ctx") // 2
    return z, jnp.bitwise_xor(z, 1), jnp.where(z < 2, 2, 1), jnp.where(z < 2, 3, 0)


def finish_feed_kernel(*refs):
    mine, theirs, (gup_ref, gdown_ref) = refs[:4], refs[4:8], refs[8:]
    core = lax.axis_index("ctx") % 2
    place = lax.axis_index("wshard")
    rows = D // 8
    for group, side in ((mine, core), (theirs, 1 - core)):
        for ref, slot in zip(group, line_slots()):
            at = pl.multiple_of(slot * QUART, 16)
            for k in range(4):
                to = pl.multiple_of(jnp.bitwise_xor(place, k) * D + side * HALF, 128)
                gup_ref[pl.ds(at, QUART), pl.ds(to, HALF)] = ref[k * QUART : (k + 1) * QUART].astype(F32)
            at = pl.multiple_of((2 * slot + side) * rows, 32)
            for half in range(2):
                share = ref[SHARD + half * rows : SHARD + (half + 1) * rows]
                gdown_ref[pl.ds(at, rows), half * HALF : (half + 1) * HALF] = share.astype(F32)


def finish_feed(*args):
    return call(
        finish_feed_kernel, "finish_feed", [WHOLE] * 8, [((SHARD, 4 * D), F32), ((D, D), F32)], [], 10**7, args
    )


def finish_heads_kernel(*refs):
    mine, theirs, outs, (gout_ref, gqkv_ref, one_ref, two_ref) = refs[:4], refs[4:8], refs[8:10], refs[10:]
    slots = line_slots()
    first = lax.axis_index("ctx") % 2 == 0
    out, other_out = [ref[...].astype(F32) for ref in outs]
    for half in range(2):
        here, cols = slice(half * PART, (half + 1) * PART), slice(half * HALF, (half + 1) * HALF)
        gout_ref[0:PART, cols] = jnp.where(first, out[here], other_out[here])
        gout_ref[PART:, cols] = jnp.where(first, other_out[here], out[here])
    mine, theirs = [[ref[...].astype(F32) for ref in group] for group in (mine, theirs)]
    low = [jnp.where(first, a, b) for a, b in zip(mine, theirs)]
    high = [jnp.where(first, b, a) for a, b in zip(mine, theirs)]
    gains = sum(block[PART + QUART :, 0:SHARD] for block in low)
    one_ref[...], two_ref[...] = gains[0], gains[1]
    for slot in range(4):
        for side, group in enumerate((low, high)):
            block = jnp.where(
                slot == slots[0],
                group[0],
                jnp.where(slot == slots[1], group[1], jnp.where(slot == slots[2], group[2], group[3])),
            )
            at, to = side * PART, slot * OWN
            gqkv_ref[at : at + PART, to : to + OWN] = block[0:PART, 0:OWN]
            gqkv_ref[at : at + PART, D + to : D + to + OWN] = block[0:PART, OWN:]
            gqkv_ref[at : at + QUART, 2 * D + to : 2 * D + to + OWN] = block[PART : PART + QUART, 0:OWN]
            gqkv_ref[at + QUART : at + PART, 2 * D + to : 2 * D + to + OWN] = block[PART : PART + QUART, OWN:]


def finish_heads(*args):
    return call(
        finish_heads_kernel,
        "finish_heads",
        [WHOLE] * 10,
        [((SHARD, D), F32), ((SHARD, 3 * D), F32), ((SHARD,), F32), ((SHARD,), F32)],
        [],
        10**7,
        args,
    )


def pick(value, index, axis=0):
    return lax.dynamic_index_in_dim(value, index, axis, keepdims=False)


def across_w(value, flip):
    return lax.ppermute(value, "wshard", [(i, i ^ flip) for i in range(4)])


def across_core(value):
    return lax.ppermute(value, "ctx", [(i, i ^ 1) for i in range(8)])


def between_z(value, pairs):
    return lax.ppermute(value, "ctx", [(2 * a + c, 2 * b + c) for a, b in pairs for c in range(2)])


Z_GROUPS = [[0, 2, 4, 6], [1, 3, 5, 7]]


def after(value, *others):
    return lax.optimization_barrier((value, *others))[0]


PAIRS = [(0, 1), (1, 0), (2, 3), (3, 2)]
MIDDLE = [(1, 2), (2, 1), (0, 0), (3, 3)]


def line_z(block):
    pair = between_z(block, PAIRS)
    mid_near = between_z(block, MIDDLE)
    near = between_z(mid_near, PAIRS)
    mid_far = between_z(pair, MIDDLE)
    far = between_z(mid_far, PAIRS)
    return block, pair, near, far, mid_near, mid_far


TO_MIDDLE = [(0, 1), (3, 2)]
TO_ENDS = [(1, 0), (2, 3)]
ACROSS = [(1, 2), (2, 1)]


def own_slot(slots, x_first):
    one, two = (1, 2) if x_first else (2, 1)
    got = across_w(slots[1], one)
    far = slots[0, 1] + got[1]
    return (slots[0, 0] + got[0]) + across_w(far, two)


def gather_plane(block, *others):
    half = block.shape[0] // 2
    from_x, from_y = across_w(block, 1), across_w(block, 2)
    first, second = from_x[:half], from_y[half:]
    if others:
        first, second, *_ = tied(first, second, *others)
    return block, from_x, from_y, across_w(first, 2), across_w(second, 1)


def tied(*values):
    return lax.optimization_barrier(values)


def local_grid(tokens, gain_one, w_qkv, w_out, gain_two, w_up, w_down, cotangent):
    core = lax.axis_index("ctx") % 2
    z = lax.axis_index("ctx") // 2
    place = lax.axis_index("wshard")
    inner = (z == 1) | (z == 2)

    def both_micros(kept, got):
        return jnp.where(core == 0, jnp.stack([kept, got]), jnp.stack([got, kept]))[:, None]

    tok, cot = tokens[:, 0], cotangent[:, 0]
    kept = jnp.concatenate([pick(tok, core), pick(cot, core)])
    got = across_core(jnp.concatenate([pick(tok, 1 - core), pick(cot, 1 - core)]))
    half = TILE // 2
    own = [jnp.where(core == 0, a, b) for a, b in ((kept, got), (got, kept))]
    x_block = jnp.concatenate([own[0][:half], own[1][:half]])
    cot = jnp.concatenate([own[0][half:], own[1][half:]])

    w_heads = pick(w_qkv.reshape(SHARD, 3, 4, OWN), z, 2).reshape(SHARD, MIX)
    gains = jnp.pad(jnp.stack([gain_one, gain_two]), ((0, 30), (0, MIX - SHARD)))
    x_all = lax.all_to_all(
        jnp.broadcast_to(x_block, (4,) + x_block.shape), "ctx", 0, 0, tiled=True, axis_index_groups=Z_GROUPS
    )
    x_on, x_rest, y_on, y_rest = parcels(cot, w_out, w_up)
    x_on, y_on = across_w(x_on, 1), across_w(y_on, 2)
    x_on, y_on, w_heads = tied(x_on, y_on, jnp.concatenate([w_heads, gains]))
    heads = gather_plane(w_heads)
    corner_a, corner_b = across_w(x_on, 2), across_w(y_on, 1)
    x_rest, y_rest, *heads = tied(x_rest, y_rest, *heads)
    x_rest, y_rest = across_w(x_rest, 1), across_w(y_rest, 2)
    normed_all, kv, mixt, att, att_low, lse, w_full, gains = attend(x_all, heads)
    shared = x_on, x_rest, y_on, y_rest, corner_a, corner_b
    att_low, *shared = tied(att_low, *shared)
    att_home = lax.all_to_all(att_low, "ctx", 0, 0, tiled=True, axis_index_groups=Z_GROUPS).reshape(D, -1)
    wout_full, up, cots = assemble(cot, w_out, w_up, shared)
    hidden, normed_two = project(att_home, x_block, gains, wout_full)

    active0, dup0, out0, dout0 = feed_own(normed_two, cots, up, w_down)
    ns = gather_plane(normed_two, active0)
    active1, dup1, out1, dout1 = feed_near(ns[1], ns[2], cots, up, w_down)
    active2, dup2, *parts = feed_far(ns[3], ns[4], cots, out1, dout1, up, w_down)
    parts, (a, a_far, b, b_far) = parts[:4], parts[4:]
    got_a, got_b = across_w(a, 1), across_w(b, 2)
    shares = feed_grads(ns, cots, (active0, active1, active2), (dup0, dup1, dup2))
    shares, got_a, got_b = tied(shares, got_a, got_b)
    shares = lax.psum_scatter(shares, "ctx", scatter_dimension=0)
    more_a, more_b = across_w(a_far + got_a[1], 2), across_w(b_far + got_b[1], 1)
    d_hidden, d_att, d_branch, d_gain_two = turn(
        hidden, gains, dout0, (got_a, more_a, got_b, more_b), cot, wout_full
    )
    d_out = lax.all_to_all(d_att, "ctx", 0, 0, tiled=True, axis_index_groups=Z_GROUPS)
    keep, send = out_grad(att_home, d_branch)
    d_out, keep, send = tied(d_out, keep, send)
    a, a_far, b, b_far = parts
    got_a, got_b = across_w(a, 1), across_w(b, 2)
    *firsts, keep, send = attend_back(
        kv, mixt, att, lse, d_out, normed_all, w_full, gains, d_gain_two, keep, send
    )
    *firsts, keep, send, shares, got_a, got_b = tied(*firsts, keep, send, shares, got_a, got_b)

    got = between_z(firsts[3], TO_MIDDLE)
    both = firsts[2] + jnp.where(inner, got, BF(0))
    outer, middle = between_z(both, TO_MIDDLE), between_z(both, ACROSS)
    pair = between_z(firsts[1] + jnp.where(inner, middle, BF(0)), PAIRS)
    middle = between_z(firsts[3] + outer, ACROSS)

    ups = [shares[0]] + [across_w(shares[e], e) for e in (1, 2, 3)]
    share = jnp.concatenate(ups + [shares[4:].reshape(SHARD, HALF)])
    share_pair, share_mid = between_z(share, PAIRS), between_z(share, ACROSS)
    share_near, share_mid_far = between_z(share_mid, TO_ENDS), between_z(share_pair, ACROSS)
    share_far = between_z(share_mid_far, TO_ENDS)
    blocks = share, share_pair, jnp.where(inner, share_mid, share_near), jnp.where(inner, share_mid_far, share_far)
    grad_up, grad_down = finish_feed(*blocks, *(across_core(block) for block in blocks))

    sums, a_far, b_far = tied(keep + across_core(send), a_far, b_far)
    sums_got = across_w(sums[1], 2)
    sums_far = across_w(sums[0, 1] + sums_got[1], 1)
    sums, a_far, b_far = tied((sums[0, 0] + sums_got[0]) + sums_far, a_far, b_far)
    more_a, more_b = across_w(a_far + got_a[1], 2), across_w(b_far + got_b[1], 1)
    result_keep, result_send = give(hidden, out0, (got_a, more_a, got_b, more_b))
    out_result = both_micros(result_keep, across_core(result_send))
    sums_pair, head_mid = between_z(sums, PAIRS), between_z(sums[:HEAD_ROWS], ACROSS)
    out = sums[HEAD_ROWS:] + sums_pair[HEAD_ROWS:]
    head_near = between_z(head_mid, TO_ENDS)
    sums_far = between_z(jnp.concatenate([sums_pair[:HEAD_ROWS], out]), ACROSS)
    pair, middle, out_result, sums_far, head_near = tied(pair, middle, out_result, sums_far, head_near)
    sums_far = jnp.concatenate([sums_far[:HEAD_ROWS], out + sums_far[HEAD_ROWS:]])
    sums_last = between_z(sums_far, TO_ENDS)
    grad_keep, grad_send = last(firsts[0], pair, middle, x_block, gains, d_hidden)
    out_tokens = both_micros(grad_keep, across_core(grad_send))
    sums_last = jnp.where(inner, sums_far, sums_last)
    head_near = jnp.where(inner, head_mid, head_near)
    blocks = sums[:HEAD_ROWS], sums_pair[:HEAD_ROWS], head_near, sums_last[:HEAD_ROWS]
    others = [across_core(block) for block in (*blocks[:3], sums_last)]
    grad_out, grad_qkv, gain_one, gain_two = finish_heads(
        *blocks, *others[:3], others[3][:HEAD_ROWS], sums_last[HEAD_ROWS:], others[3][HEAD_ROWS:]
    )
    return (
        out_result,
        out_tokens,
        gain_one,
        grad_qkv,
        grad_out,
        gain_two,
        grad_up,
        grad_down,
    )


def local(tokens, *rest):
    fits = (
        lax.axis_size("wshard") == 4
        and lax.axis_size("ctx") == 8
        and tokens.shape[:2] == (2, 1)
        and 2 * tokens.shape[2] == TILE
    )
    return (local_grid if fits else local_any)(tokens, *rest)


def solution(mesh):
    placed = (
        P(None, "wshard", "ctx", None),
        P("wshard"),
        P("wshard", None),
        P("wshard", None),
        P("wshard"),
        P("wshard", None),
        P("wshard", None),
        P(None, "wshard", "ctx", None),
    )
    return jax.shard_map(
        local,
        mesh=mesh,
        in_specs=placed,
        out_specs=(
            P(None, "wshard", "ctx", None),
            P(None, "wshard", "ctx", None),
            P("wshard"),
            P("wshard", None),
            P("wshard", None),
            P("wshard"),
            P("wshard", None),
            P("wshard", None),
        ),
        check_vma=False,
    )
```

```python
import jax
import jax.numpy as jnp
from jax import lax
from jax.experimental import pallas as pl
from jax.experimental.pallas import tpu as pltpu
from jax.sharding import PartitionSpec as P

D = 768
HEADS = 12
HEAD_DIM = 64


EPSILON = 1e-05


def passed_along(value, axis, by):
    count = lax.axis_size(axis)
    return lax.ppermute(value, axis, [(i, (i + by) % count) for i in range(count)])


def layer_norm(inputs, scaling):
    centred = inputs - jnp.mean(inputs, axis=-1, keepdims=True)
    variance = jnp.mean(centred * centred, axis=-1, keepdims=True)
    return centred * lax.rsqrt(variance + EPSILON) * scaling


def gelu_smooth(values_in):
    return jax.nn.gelu(values_in, approximate=True)


def contract_rows(left_side, right_side):
    return lax.dot_general(
        left_side, right_side, (((0,), (0,)), ((), ())), preferred_element_type=jnp.float32
    )


def times_rows(left_side, right_side):
    return lax.dot_general(
        left_side, right_side, (((1,), (1,)), ((), ())), preferred_element_type=jnp.float32
    )


def pair_grads(query_h, dout_h, log_total, row_delta, query_pos, key_h, value_h, key_pos):
    scaling = HEAD_DIM ** (-0.5)
    scores = (
        jnp.einsum("qhe,khe->hqk", query_h, key_h, preferred_element_type=jnp.float32) * scaling
    )
    visible = key_pos[None, None, :] <= query_pos[None, :, None]
    magnitude = jnp.sqrt(scores * scores + 1.0)
    tilted = scores / magnitude
    chance = jnp.exp(jnp.where(visible, magnitude - log_total[:, :, None], -1e30))
    signed = (tilted * chance).astype(jnp.bfloat16)
    d_signed = jnp.einsum("qhe,khe->hqk", dout_h, value_h, preferred_element_type=jnp.float32)
    slope = 1.0 / (magnitude * magnitude * magnitude) + tilted * tilted
    d_scores = (chance * (d_signed * slope - tilted * row_delta[:, :, None])).astype(jnp.bfloat16)
    d_query = (
        jnp.einsum("hqk,khe->qhe", d_scores, key_h, preferred_element_type=jnp.float32) * scaling
    )
    d_key = (
        jnp.einsum("hqk,qhe->khe", d_scores, query_h, preferred_element_type=jnp.float32) * scaling
    )
    d_value = jnp.einsum("hqk,qhe->khe", signed, dout_h, preferred_element_type=jnp.float32)
    return (d_query, d_key, d_value)


def keep_state(loop_state):
    return loop_state


def local_any(tokens, gain_one, w_qkv, w_out, gain_two, w_up, w_down, cotangent):
    gathered = (
        lax.all_gather(gain_one, "wshard", axis=0, tiled=True),
        lax.all_gather(w_qkv, "wshard", axis=0, tiled=True),
        lax.all_gather(w_out, "wshard", axis=0, tiled=True),
        lax.all_gather(gain_two, "wshard", axis=0, tiled=True),
        lax.all_gather(w_up, "wshard", axis=0, tiled=True),
        lax.all_gather(w_down, "wshard", axis=0, tiled=True),
    )
    full_gain_one, full_qkv, full_out, full_gain_two, full_up, full_down = gathered
    gain_first = full_gain_one.astype(jnp.float32)
    gain_second = full_gain_two.astype(jnp.float32)
    cycle_size = lax.axis_size("ctx")
    cycle_place = lax.axis_index("ctx")
    micro_count = tokens.shape[0]
    local_len = tokens.shape[2]
    scaling = HEAD_DIM ** (-0.5)
    query_pos = cycle_place * local_len + jnp.arange(local_len, dtype=jnp.int32)
    sum_gain_one = jnp.zeros((D,), jnp.float32)
    sum_gain_two = jnp.zeros((D,), jnp.float32)
    sum_qkv = jnp.zeros(full_qkv.shape, jnp.float32)
    sum_out = jnp.zeros(full_out.shape, jnp.float32)
    sum_up = jnp.zeros(full_up.shape, jnp.float32)
    sum_down = jnp.zeros(full_down.shape, jnp.float32)
    results = []
    grad_list = []
    for micro_index in range(micro_count):
        inputs = tokens[micro_index, 0].astype(jnp.float32)
        normed_f, norm_back = jax.vjp(layer_norm, inputs, gain_first)
        normed = normed_f.astype(jnp.bfloat16)
        mixed_all = jnp.dot(normed, full_qkv, preferred_element_type=jnp.float32).astype(
            jnp.bfloat16
        )
        keys_flat = mixed_all[:, D : 2 * D]
        values_flat = mixed_all[:, 2 * D :]
        query_h = mixed_all[:, :D].reshape(local_len, HEADS, HEAD_DIM)
        key_h = keys_flat.reshape(local_len, HEADS, HEAD_DIM)
        value_h = values_flat.reshape(local_len, HEADS, HEAD_DIM)
        start_state = (
            jnp.zeros((HEADS, local_len, HEAD_DIM), jnp.float32),
            jnp.ones((HEADS, local_len), jnp.float32),
            jnp.zeros((HEADS, local_len), jnp.float32),
        )
        shard_piece = (
            lax.all_gather(keys_flat, "ctx", axis=0, tiled=True),
            lax.all_gather(values_flat, "ctx", axis=0, tiled=True),
        )

        def compute(loop_state):
            accumulated, top_value, totals = loop_state
            key_piece = shard_piece[0].reshape(-1, HEADS, HEAD_DIM)
            value_piece = shard_piece[1].reshape(-1, HEADS, HEAD_DIM)
            key_pos = jnp.arange(key_piece.shape[0], dtype=jnp.int32)
            scores = (
                jnp.einsum("qhe,khe->hqk", query_h, key_piece, preferred_element_type=jnp.float32)
                * scaling
            )
            visible = key_pos[None, None, :] <= query_pos[None, :, None]
            magnitude = jnp.sqrt(scores * scores + 1.0)
            new_top = jnp.maximum(top_value, jnp.max(jnp.where(visible, magnitude, 0.0), axis=-1))
            weighted = jnp.exp(jnp.where(visible, magnitude - new_top[:, :, None], -1e30))
            signed = (scores / magnitude * weighted).astype(jnp.bfloat16)
            accumulated = jnp.einsum(
                "hqk,khe->hqe", signed, value_piece, preferred_element_type=jnp.float32
            )
            totals = jnp.sum(weighted, axis=-1)
            return (accumulated, new_top, totals)

        accumulated, top_value, totals = lax.cond(
            jnp.int32(0) <= query_pos[-1], compute, keep_state, start_state
        )
        attended_h = accumulated / totals[:, :, None]
        log_total = top_value + jnp.log(totals)
        attended = jnp.transpose(attended_h, (1, 0, 2)).reshape(local_len, D)
        attended_low = attended.astype(jnp.bfloat16)
        hidden = inputs + jnp.dot(attended_low, full_out, preferred_element_type=jnp.float32)
        normed_two_f, norm_two_back = jax.vjp(layer_norm, hidden, gain_second)
        normed_two = normed_two_f.astype(jnp.bfloat16)
        upward = jnp.dot(normed_two, full_up, preferred_element_type=jnp.float32)
        active_f, gelu_back = jax.vjp(gelu_smooth, upward)
        active = active_f.astype(jnp.bfloat16)
        result_rows = hidden + jnp.dot(active, full_down, preferred_element_type=jnp.float32)
        results.append(result_rows.astype(jnp.bfloat16))
        d_result = cotangent[micro_index, 0]
        sum_down = sum_down + contract_rows(active, d_result)
        d_active = times_rows(d_result, full_down)
        d_upward = gelu_back(d_active)[0].astype(jnp.bfloat16)
        sum_up = sum_up + contract_rows(normed_two, d_upward)
        d_normed_two = times_rows(d_upward, full_up)
        d_hidden_norm, d_gain_two = norm_two_back(d_normed_two)
        sum_gain_two = sum_gain_two + d_gain_two
        d_hidden = d_result.astype(jnp.float32) + d_hidden_norm
        d_branch = d_hidden.astype(jnp.bfloat16)
        sum_out = sum_out + contract_rows(attended_low, d_branch)
        d_attended = times_rows(d_branch, full_out).astype(jnp.bfloat16)
        dout_h = d_attended.reshape(local_len, HEADS, HEAD_DIM)
        row_delta = jnp.einsum("qhe,hqe->hq", dout_h.astype(jnp.float32), attended_h)
        zero_block = jnp.zeros((local_len, HEADS, HEAD_DIM), jnp.float32)

        def turn_keys(turn_index, loop_state):
            key_b, value_b, d_key_b, d_value_b, d_query = loop_state
            owner_index = (cycle_place + turn_index) % cycle_size
            key_pos = owner_index * local_len + jnp.arange(local_len, dtype=jnp.int32)

            def work(partial_sums):
                contrib = pair_grads(
                    query_h, dout_h, log_total, row_delta, query_pos, key_b, value_b, key_pos
                )
                return (
                    partial_sums[0] + contrib[0],
                    partial_sums[1] + contrib[1],
                    partial_sums[2] + contrib[2],
                )

            needed = (turn_index == 0) | (cycle_place + turn_index >= cycle_size)
            d_query, d_key_b, d_value_b = lax.cond(
                needed, work, keep_state, (d_query, d_key_b, d_value_b)
            )
            key_b, value_b = passed_along((key_b, value_b), "ctx", -1)
            d_key_b, d_value_b = (
                passed_along(d_key_b.astype(jnp.bfloat16), "ctx", -1).astype(d_key_b.dtype),
                passed_along(d_value_b.astype(jnp.bfloat16), "ctx", -1).astype(d_value_b.dtype),
            )
            return (key_b, value_b, d_key_b, d_value_b, d_query)

        final_state = lax.fori_loop(
            0, cycle_size, turn_keys, (key_h, value_h, zero_block, zero_block, zero_block)
        )
        d_key = final_state[2]
        d_value = final_state[3]
        d_query = final_state[4]
        d_mixed = jnp.concatenate(
            [
                d_query.reshape(local_len, D),
                d_key.reshape(local_len, D),
                d_value.reshape(local_len, D),
            ],
            axis=1,
        ).astype(jnp.bfloat16)
        sum_qkv = sum_qkv + contract_rows(normed, d_mixed)
        d_normed = times_rows(d_mixed, full_qkv)
        d_inputs_norm, d_gain_one = norm_back(d_normed)
        sum_gain_one = sum_gain_one + d_gain_one
        grad_list.append(d_hidden + d_inputs_norm)
    shares = (
        lax.psum_scatter(
            sum_gain_one.astype(jnp.bfloat16), "wshard", scatter_dimension=0, tiled=True
        ).astype(jnp.float32),
        lax.psum_scatter(
            sum_qkv.astype(jnp.bfloat16), "wshard", scatter_dimension=0, tiled=True
        ).astype(jnp.float32),
        lax.psum_scatter(
            sum_out.astype(jnp.bfloat16), "wshard", scatter_dimension=0, tiled=True
        ).astype(jnp.float32),
        lax.psum_scatter(
            sum_gain_two.astype(jnp.bfloat16), "wshard", scatter_dimension=0, tiled=True
        ).astype(jnp.float32),
        lax.psum_scatter(
            sum_up.astype(jnp.bfloat16), "wshard", scatter_dimension=0, tiled=True
        ).astype(jnp.float32),
        lax.psum_scatter(
            sum_down.astype(jnp.bfloat16), "wshard", scatter_dimension=0, tiled=True
        ).astype(jnp.float32),
    )
    summed = (
        lax.psum(shares[0].astype(jnp.bfloat16), "ctx").astype(jnp.float32),
        lax.psum(shares[1].astype(jnp.bfloat16), "ctx").astype(jnp.float32),
        lax.psum(shares[2].astype(jnp.bfloat16), "ctx").astype(jnp.float32),
        lax.psum(shares[3].astype(jnp.bfloat16), "ctx").astype(jnp.float32),
        lax.psum(shares[4].astype(jnp.bfloat16), "ctx").astype(jnp.float32),
        lax.psum(shares[5].astype(jnp.bfloat16), "ctx").astype(jnp.float32),
    )
    result_out = jnp.stack(results)[:, None]
    grad_out_tokens = jnp.stack(grad_list)[:, None]
    return (
        result_out,
        grad_out_tokens,
        summed[0],
        summed[1],
        summed[2],
        summed[3],
        summed[4],
        summed[5],
    )


BF = jnp.bfloat16
F32 = jnp.float32
TILE = 256
SHARD = D // 4
OWN_HEADS = HEADS // 4
OWN = OWN_HEADS * HEAD_DIM
MIX = 3 * OWN
HEAD_ROWS = 160
PART = SHARD // 2
QUART = SHARD // 4
HALF = D // 2
MIDDLE_ROW = 224
VMEM_LIMIT = 56 * 1024 * 1024
WHOLE = pl.BlockSpec(memory_space=pltpu.VMEM)
ANYWHERE = pl.BlockSpec(memory_space=pl.ANY)


def nn(a, b):
    return lax.dot_general(a, b, (((1,), (0,)), ((), ())), preferred_element_type=F32)


def nt(a, b):
    return lax.dot_general(a, b, (((1,), (1,)), ((), ())), preferred_element_type=F32)


def normalised(x):
    centred = x - jnp.mean(x, axis=-1, keepdims=True)
    variance = jnp.mean(centred * centred, axis=-1, keepdims=True)
    inverse = lax.rsqrt(variance + EPSILON)
    return centred * inverse, inverse


def norm_back(xhat, inverse, gain, dy):
    g = dy * gain
    mean_g = jnp.mean(g, axis=-1, keepdims=True)
    mean_gx = jnp.mean(g * xhat, axis=-1, keepdims=True)
    return (g - mean_g - xhat * mean_gx) * inverse


def causal_tile():
    rows = lax.broadcasted_iota(jnp.int32, (TILE, TILE), 0)
    cols = lax.broadcasted_iota(jnp.int32, (TILE, TILE), 1)
    return rows <= cols


def call(kernel, name, ins, outs, scratch, flops, args, out_specs=None):
    moved = sum(a.size * a.dtype.itemsize for a in args)
    return pl.pallas_call(
        kernel,
        in_specs=ins,
        out_specs=out_specs or [WHOLE] * len(outs),
        out_shape=[jax.ShapeDtypeStruct(shape, kind) for shape, kind in outs],
        scratch_shapes=scratch,
        compiler_params=pltpu.CompilerParams(vmem_limit_bytes=VMEM_LIMIT),
        cost_estimate=pl.CostEstimate(flops=1000, bytes_accessed=1000, transcendentals=0),
        name=name,
    )(*args)


def shard_rows_of(pieces, which, first, count):
    if which < 3:
        return pieces[which].at[pl.ds(first, count)]
    half = pieces[3].shape[0]
    if first < half:
        return pieces[3].at[pl.ds(first, count)]
    return pieces[4].at[pl.ds(first - half, count)]


def run_copies(pairs, sems):
    copies = [pltpu.make_async_copy(src, dst, sems.at[i]) for i, (src, dst) in enumerate(pairs)]
    for copy in copies:
        copy.start()
    for copy in copies:
        copy.wait()


def attend_kernel(x_ref, w0, w1, w2, w3, w4,
                  normed_out, kv_out, mixt_out, att_ref, low_ref, lse_ref, wfull_out, gains_ref,
                  normed_ref, kv_ref, mixt_ref, wfull_ref, s_ref, g_ref, wsems, sems):
    place = lax.axis_index("wshard")
    pieces = (w0, w1, w2, w3, w4)
    half = w3.shape[0]
    pairs = []
    for k in range(4):
        to = pl.multiple_of(jnp.bitwise_xor(place, k) * SHARD, SHARD)
        if k < 3:
            pairs.append((shard_rows_of(pieces, k, 0, SHARD), wfull_ref.at[pl.ds(to, SHARD)]))
        else:
            pairs.append((w3, wfull_ref.at[pl.ds(to, half)]))
            pairs.append((w4.at[pl.ds(0, SHARD - half)], wfull_ref.at[pl.ds(to + half, SHARD - half)]))
        source = w4.at[pl.ds(SHARD - half, 16)] if k == 3 else pieces[k].at[pl.ds(SHARD, 16)]
        pairs.append((source, g_ref.at[k]))
    run_copies(pairs, wsems)
    gains = jnp.concatenate([g_ref[jnp.bitwise_xor(place, j)][0:8, 0:SHARD].astype(F32) for j in range(4)], axis=1)
    gains_ref[...] = gains
    for row in range(4):
        here = slice(row * TILE, (row + 1) * TILE)
        xhat, _ = normalised(x_ref[row].astype(F32))
        normed = (xhat * gains[0:1]).astype(BF)
        normed_ref[here, :] = normed
        mix = nn(normed, wfull_ref[...]).astype(BF)
        mixt_ref[:, here] = mix.T
        for h in range(OWN_HEADS):
            kv_ref[h, here, 0:HEAD_DIM] = mix[:, OWN + h * HEAD_DIM : OWN + (h + 1) * HEAD_DIM]
            kv_ref[h, here, HEAD_DIM:] = mix[:, 2 * OWN + h * HEAD_DIM : 2 * OWN + (h + 1) * HEAD_DIM]

    pairs = ((normed_ref, normed_out), (kv_ref, kv_out), (mixt_ref, mixt_out), (wfull_ref, wfull_out))
    copies = [pltpu.make_async_copy(src, dst, sems.at[k]) for k, (src, dst) in enumerate(pairs)]
    for copy in copies:
        copy.start()

    @pl.loop(0, OWN_HEADS)
    def _(h):
        base = pl.multiple_of(h * HEAD_DIM, HEAD_DIM)
        for block in range(4):
            here = slice(block * TILE, (block + 1) * TILE)
            queries = mixt_ref[pl.ds(base, HEAD_DIM), here] * BF(HEAD_DIM**-0.5)
            top = jnp.zeros((1, TILE), F32)
            for other in range(block + 1):
                there = slice(other * TILE, (other + 1) * TILE)
                s = nn(kv_ref[h, there, 0:HEAD_DIM], queries)
                s_ref[there, :] = s
                size = jnp.abs(s)
                if other == block:
                    size = jnp.where(causal_tile(), size, 0.0)
                top = jnp.maximum(top, jnp.max(size, axis=0, keepdims=True))
            top = jnp.sqrt(top * top + 1.0)
            total = jnp.zeros((1, TILE), F32)
            acc = jnp.zeros((HEAD_DIM, TILE), F32)
            for other in range(block + 1):
                there = slice(other * TILE, (other + 1) * TILE)
                s = s_ref[there, :]
                square = s * s + 1.0
                r = lax.rsqrt(square)
                p = jnp.exp(square * r - top)
                if other == block:
                    p = jnp.where(causal_tile(), p, 0.0)
                total = total + jnp.sum(p, axis=0, keepdims=True)
                signed = (s * r * p).astype(BF)
                acc = acc + nn(mixt_ref[pl.ds(2 * OWN + base, HEAD_DIM), there], signed)
            att = acc / total
            att_ref[pl.ds(base, HEAD_DIM), here] = att
            low_ref[block, pl.ds(base, HEAD_DIM), :] = att.astype(BF)
            lse_ref[pl.ds(h, 1), here] = top + jnp.log(total)

    for copy in copies:
        copy.wait()


def attend(x_all, pieces):
    length = 4 * TILE
    return call(
        attend_kernel,
        "attend",
        [WHOLE] + [ANYWHERE] * 5,
        [
            ((length, D), BF),
            ((OWN_HEADS, length, 2 * HEAD_DIM), BF),
            ((MIX, length), BF),
            ((OWN, length), F32),
            ((4, OWN, TILE), BF),
            ((8, length), F32),
            ((D, MIX), BF),
            ((8, D), F32),
        ],
        [
            pltpu.VMEM((length, D), BF),
            pltpu.VMEM((OWN_HEADS, length, 2 * HEAD_DIM), BF),
            pltpu.VMEM((MIX, length), BF),
            pltpu.VMEM((D, MIX), BF),
            pltpu.VMEM((length, TILE), F32),
            pltpu.VMEM((4, 16, MIX), BF),
            pltpu.SemaphoreType.DMA((9,)),
            pltpu.SemaphoreType.DMA((4,)),
        ],
        3 * 10**9,
        (x_all, *pieces),
        [ANYWHERE] * 3 + [WHOLE] * 3 + [ANYWHERE, WHOLE],
    )


def parcel_kernel(cot_ref, wout_ref, wup_ref, x_on_ref, x_ref, y_on_ref, y_ref, sems):
    place = lax.axis_index("wshard")

    def columns(k, first, count):
        at = pl.multiple_of(jnp.bitwise_xor(place, k) * D, D)
        return wup_ref.at[pl.ds(first, count), pl.ds(at, D)]

    low, high = cot_ref.at[pl.ds(0, MIDDLE_ROW)], cot_ref.at[pl.ds(MIDDLE_ROW, 32)]
    pairs = (
        (low, x_on_ref.at[pl.ds(0, MIDDLE_ROW)]),
        (columns(3, 0, PART), x_on_ref.at[pl.ds(MIDDLE_ROW, PART)]),
        (high, y_on_ref.at[pl.ds(0, 32)]),
        (wout_ref, y_on_ref.at[pl.ds(32, SHARD)]),
        (columns(3, PART, PART), y_on_ref.at[pl.ds(MIDDLE_ROW, PART)]),
        (columns(1, 0, SHARD), x_ref.at[pl.ds(0, SHARD)]),
        (high, x_ref.at[pl.ds(SHARD, 32)]),
        (wout_ref, x_ref.at[pl.ds(SHARD + 32, SHARD)]),
        (columns(2, 0, SHARD), y_ref.at[pl.ds(0, SHARD)]),
        (low, y_ref.at[pl.ds(SHARD, MIDDLE_ROW)]),
    )
    run_copies(pairs, sems)


def parcels(cot, w_out, w_up):
    on, rest = MIDDLE_ROW + PART, SHARD + MIDDLE_ROW
    return call(
        parcel_kernel,
        "parcels",
        [ANYWHERE] * 3,
        [((on, D), BF), ((rest, D), BF)] * 2,
        [pltpu.SemaphoreType.DMA((10,))],
        10**6,
        (cot, w_out, w_up),
    )


def assemble_kernel(cot_ref, own_ref, wup_ref, x_on, x_rest, y_on, y_rest, corner_a, corner_b,
                    wout_ref, up_ref, cots_ref, sems):
    place = lax.axis_index("wshard")
    at = [pl.multiple_of(jnp.bitwise_xor(place, k) * SHARD, SHARD) for k in range(4)]
    half = PART
    mine = pl.multiple_of(place * D, D)
    pairs = (
        (own_ref, wout_ref.at[pl.ds(at[0], SHARD)]),
        (x_rest.at[pl.ds(SHARD + 32, SHARD)], wout_ref.at[pl.ds(at[1], SHARD)]),
        (y_on.at[pl.ds(32, SHARD)], wout_ref.at[pl.ds(at[2], SHARD)]),
        (corner_b.at[pl.ds(32, SHARD)], wout_ref.at[pl.ds(at[3], SHARD)]),
        (wup_ref.at[:, pl.ds(mine, D)], up_ref.at[pl.ds(at[0], SHARD)]),
        (x_rest.at[pl.ds(0, SHARD)], up_ref.at[pl.ds(at[1], SHARD)]),
        (y_rest.at[pl.ds(0, SHARD)], up_ref.at[pl.ds(at[2], SHARD)]),
        (corner_a.at[pl.ds(MIDDLE_ROW, half)], up_ref.at[pl.ds(at[3], half)]),
        (corner_b.at[pl.ds(MIDDLE_ROW, half)], up_ref.at[pl.ds(at[3] + half, half)]),
        (cot_ref, cots_ref.at[pl.ds(0, TILE)]),
        (x_on.at[pl.ds(0, MIDDLE_ROW)], cots_ref.at[pl.ds(TILE, MIDDLE_ROW)]),
        (x_rest.at[pl.ds(SHARD, 32)], cots_ref.at[pl.ds(TILE + MIDDLE_ROW, 32)]),
        (y_rest.at[pl.ds(SHARD, MIDDLE_ROW)], cots_ref.at[pl.ds(2 * TILE, MIDDLE_ROW)]),
        (y_on.at[pl.ds(0, 32)], cots_ref.at[pl.ds(2 * TILE + MIDDLE_ROW, 32)]),
        (corner_a.at[pl.ds(0, MIDDLE_ROW)], cots_ref.at[pl.ds(3 * TILE, MIDDLE_ROW)]),
        (corner_b.at[pl.ds(0, 32)], cots_ref.at[pl.ds(3 * TILE + MIDDLE_ROW, 32)]),
    )
    run_copies(pairs, sems)


def assemble(cot, w_out, w_up, shared):
    return call(
        assemble_kernel,
        "assemble",
        [ANYWHERE] * 9,
        [((D, D), BF), ((D, D), BF), ((4 * TILE, D), BF)],
        [pltpu.SemaphoreType.DMA((16,))],
        10**6,
        (cot, w_out, w_up, *shared),
    )


def project_kernel(att_ref, x_ref, gain_ref, wout_ref, hidden_ref, normed_ref):
    hidden = x_ref[...].astype(F32) + nn(att_ref[...].T, wout_ref[...])
    hidden_ref[...] = hidden
    xhat, _ = normalised(hidden)
    normed_ref[...] = (xhat * gain_ref[1:2]).astype(BF)


def project(att_home, x_block, gain, w_out):
    rows = x_block.shape[0]
    return call(
        project_kernel,
        "project",
        [WHOLE] * 4,
        [((rows, D), F32), ((rows, D), BF)],
        [],
        3 * 10**8,
        (att_home, x_block, gain, w_out),
    )


SLOPE = (2.0 / 3.141592653589793) ** 0.5


def feed_rows(n, cot, up_ref, down_ref, active_ref, dup_ref, here):
    for first in range(0, D, TILE):
        cols = slice(first, first + TILE)
        u = nn(n, up_ref[:, cols])
        square = u * u
        t = jnp.tanh(SLOPE * (u + 0.044715 * (square * u)))
        side = 0.5 + 0.5 * t
        active_ref[here, cols] = (u * side).astype(BF)
        grad = side + (0.5 * SLOPE) * u * (1.0 - t * t) * (1.0 + 0.134145 * square)
        dup_ref[here, cols] = (grad * nt(cot, down_ref[cols, :])).astype(BF)
    return nn(active_ref[here, :], down_ref[...]), nt(dup_ref[here, :], up_ref[...])


def feed_own_kernel(n_ref, cot_ref, up_ref, down_ref, active_ref, dup_ref, out_ref, dout_ref):
    out_ref[...], dout_ref[...] = feed_rows(
        n_ref[...], cot_ref[0:TILE, :], up_ref, down_ref, active_ref, dup_ref, slice(0, TILE)
    )


def feed_own(n, cots, up, down):
    return call(
        feed_own_kernel,
        "feed_own",
        [WHOLE] * 4,
        [((TILE, D), BF), ((TILE, D), BF), ((TILE, D), F32), ((TILE, D), F32)],
        [],
        2 * 10**9,
        (n, cots, up, down),
    )


def feed_near_kernel(nx_ref, ny_ref, cot_ref, up_ref, down_ref, active_ref, dup_ref, out_ref, dout_ref):
    for k, n_ref in enumerate((nx_ref, ny_ref)):
        here = slice(k * TILE, (k + 1) * TILE)
        out, dout = feed_rows(n_ref[...], cot_ref[(k + 1) * TILE : (k + 2) * TILE, :], up_ref, down_ref, active_ref, dup_ref, here)
        out_ref[here, :], dout_ref[here, :] = out.astype(BF), dout.astype(BF)


def feed_near(nx, ny, cots, up, down):
    return call(
        feed_near_kernel,
        "feed_near",
        [WHOLE] * 5,
        [((2 * TILE, D), BF)] * 4,
        [],
        4 * 10**9,
        (nx, ny, cots, up, down),
    )


def feed_far_kernel(na_ref, nb_ref, cot_ref, out_ref, dout_ref, up_ref, down_ref,
                    active_ref, dup_ref, oa_ref, oaf_ref, ob_ref, obf_ref, da_ref, daf_ref, db_ref, dbf_ref):
    n = jnp.concatenate([na_ref[...], nb_ref[...]])
    cot = cot_ref[3 * TILE :, :]
    half = TILE // 2
    out, dout = feed_rows(n, cot, up_ref, down_ref, active_ref, dup_ref, slice(0, TILE))
    for far, near, a, af, b, bf in (
        (out, out_ref, oa_ref, oaf_ref, ob_ref, obf_ref),
        (dout, dout_ref, da_ref, daf_ref, db_ref, dbf_ref),
    ):
        far = far.astype(BF)
        a[0], a[1] = near[0:half, :], far[0:half]
        b[0], b[1] = near[TILE + half :, :], far[half:]
        af[...] = near[TILE : TILE + half, :]
        bf[...] = near[half:TILE, :]


def feed_far(na, nb, cots, out, dout, up, down):
    half = TILE // 2
    return call(
        feed_far_kernel,
        "feed_far",
        [WHOLE] * 7,
        [((TILE, D), BF)] * 2 + [((2, half, D), BF), ((half, D), BF)] * 4,
        [],
        2 * 10**9,
        (na, nb, cots, out, dout, up, down),
    )


def feed_grads_kernel(n0, n1, n2, n3, n4, cot_ref, a0, a1, a2, d0, d1, d2,
                      shares_ref, nt_ref, at_ref, dup_ref):
    for k, piece in enumerate((n0, n1, n2)):
        nt_ref[:, k * TILE : (k + 1) * TILE] = piece[...].T
    nt_ref[:, 3 * TILE :] = jnp.concatenate([n3[...], n4[...]]).T
    at_ref[:, 0:TILE] = a0[...].T
    at_ref[:, TILE : 3 * TILE] = a1[...].T
    at_ref[:, 3 * TILE :] = a2[...].T
    dup_ref[0:TILE] = d0[...]
    dup_ref[TILE : 3 * TILE] = d1[...]
    dup_ref[3 * TILE :] = d2[...]
    rows = D // 8
    for k in range(8):
        g = nn(at_ref[k * rows : (k + 1) * rows, :], cot_ref[...]).astype(BF)
        for side in range(2):
            for part in range(2):
                piece = g[part * QUART : (part + 1) * QUART, side * HALF : (side + 1) * HALF]
                shares_ref[k, 4 + 2 * side + part] = piece
    for to in range(4):
        g = nn(nt_ref[to * SHARD : (to + 1) * SHARD, :], dup_ref[...]).astype(BF)
        slot = jnp.bitwise_xor(lax.axis_index("wshard"), to)
        for k in range(8):
            r, c = (k // 2) * QUART, (k % 2) * HALF
            shares_ref[k, slot] = g[r : r + QUART, c : c + HALF]


def feed_grads(ns, cots, actives, dups):
    length = 4 * TILE
    return call(
        feed_grads_kernel,
        "feed_grads",
        [WHOLE] * 12,
        [((8, 8, QUART, HALF), BF)],
        [
            pltpu.VMEM((D, length), BF),
            pltpu.VMEM((D, length), BF),
            pltpu.VMEM((length, D), BF),
        ],
        3 * 10**9,
        (*ns, cots, *actives, *dups),
    )[0]


def summed(keep_ref, a_ref, a_more_ref, b_ref, b_more_ref):
    first = a_ref[0].astype(F32) + a_more_ref[...].astype(F32)
    second = b_ref[0].astype(F32) + b_more_ref[...].astype(F32)
    return keep_ref[...] + jnp.concatenate([first, second])


def give_kernel(hidden_ref, keep_ref, a_ref, a_more_ref, b_ref, b_more_ref, rkeep_ref, rsend_ref, result_ref, sems):
    core = lax.axis_index("ctx") % 2
    result = (hidden_ref[...] + summed(keep_ref, a_ref, a_more_ref, b_ref, b_more_ref)).astype(BF)
    half = TILE // 2
    result_ref[0], result_ref[1] = result[:half], result[half:]
    run_copies(((result_ref.at[1 - core], rsend_ref), (result_ref.at[core], rkeep_ref)), sems)


def give(hidden, keep, parts):
    half = TILE // 2
    return call(
        give_kernel,
        "give",
        [WHOLE] * 6,
        [((half, D), BF)] * 2,
        [pltpu.VMEM((2, half, D), BF), pltpu.SemaphoreType.DMA((2,))],
        10**6,
        (hidden, keep, *parts),
        [ANYWHERE] * 2,
    )


def turn_kernel(hidden_ref, gain_ref, dkeep_ref, a_ref, a_more_ref, b_ref, b_more_ref, cot_ref, wout_ref,
                dhidden_ref, datt_ref, dbranch_ref, dgain_ref):
    gain = gain_ref[1:2]
    xhat, inverse = normalised(hidden_ref[...])
    dy = summed(dkeep_ref, a_ref, a_more_ref, b_ref, b_more_ref)
    dgain_ref[...] = jnp.sum(dy * xhat, axis=0, keepdims=True)
    d_hidden = cot_ref[...].astype(F32) + norm_back(xhat, inverse, gain, dy)
    dhidden_ref[...] = d_hidden
    d_branch = d_hidden.astype(BF)
    dbranch_ref[...] = d_branch
    d_att = nt(wout_ref[...], d_branch).astype(BF)
    for k in range(4):
        datt_ref[k] = d_att[k * OWN : (k + 1) * OWN]


def turn(hidden, gain, dkeep, parts, cot, w_out):
    rows = hidden.shape[0]
    return call(
        turn_kernel,
        "turn",
        [WHOLE] * 9,
        [((rows, D), F32), ((4, OWN, rows), BF), ((rows, D), BF), ((1, D), F32)],
        [],
        6 * 10**8,
        (hidden, gain, dkeep, *parts, cot, w_out),
    )


def out_grad_kernel(att_ref, dbranch_ref, keep_ref, send_ref, grad_ref, sems):
    core = lax.axis_index("ctx") % 2
    place = lax.axis_index("wshard")
    for to in range(4):
        e = jnp.bitwise_xor(place, to)
        e_x, e_y = jnp.bitwise_and(e, 1), e // 2
        g = nn(att_ref[to * SHARD : (to + 1) * SHARD, :], dbranch_ref[...]).astype(BF)
        for side in range(2):
            for half in range(2):
                piece = g[side * PART : (side + 1) * PART, half * HALF : (half + 1) * HALF]
                grad_ref[side, e_y, e_x, half * PART : (half + 1) * PART] = piece
    rows = pl.ds(HEAD_ROWS, SHARD)
    pairs = ((grad_ref.at[1 - core], send_ref.at[:, :, rows]), (grad_ref.at[core], keep_ref.at[:, :, rows]))
    run_copies(pairs, sems)


def out_grad(att_home, d_branch):
    return call(
        out_grad_kernel,
        "out_grad",
        [WHOLE] * 2,
        [((2, 2, HEAD_ROWS + SHARD, HALF), BF)] * 2,
        [pltpu.VMEM((2, 2, 2, SHARD, HALF), BF), pltpu.SemaphoreType.DMA((2,))],
        3 * 10**8,
        (att_home, d_branch),
        [ANYWHERE] * 2,
    )


def attend_back_kernel(kv_ref, mixt_ref, att_ref, lse_ref, dout_ref, normed_in, w_in, gain_ref, dgain_ref, _, __,
                       f0_ref, f1_ref, f2_ref, f3_ref, gkeep_ref, gsend_ref,
                       dq_ref, dk_ref, dv_ref, dm_ref, mix_ref, total_ref, first_ref, head_ref, sems,
                       normed_ref, w_ref, in_sems):
    length = kv_ref.shape[1]
    loads = [
        pltpu.make_async_copy(normed_in, normed_ref, in_sems.at[0]),
        pltpu.make_async_copy(w_in, w_ref, in_sems.at[1]),
    ]
    for load in loads:
        load.start()
    scale = BF(HEAD_DIM**-0.5)
    core = lax.axis_index("ctx") % 2
    z = lax.axis_index("ctx") // 2
    place = lax.axis_index("wshard")

    @pl.loop(0, OWN_HEADS)
    def _(h):
        base = pl.multiple_of(h * HEAD_DIM, HEAD_DIM)
        for block in range(4):
            here = slice(block * TILE, (block + 1) * TILE)
            queries = mixt_ref[pl.ds(base, HEAD_DIM), here] * scale
            dout = dout_ref[block, pl.ds(base, HEAD_DIM), :]
            delta = jnp.sum(dout.astype(F32) * att_ref[pl.ds(base, HEAD_DIM), here], axis=0, keepdims=True)
            lse = lse_ref[pl.ds(h, 1), here]
            acc = jnp.zeros((HEAD_DIM, TILE), F32)
            for other in range(block + 1):
                there = slice(other * TILE, (other + 1) * TILE)
                s = nn(kv_ref[h, there, 0:HEAD_DIM], queries)
                ds = nn(kv_ref[h, there, HEAD_DIM:], dout)
                square = s * s + 1.0
                r = lax.rsqrt(square)
                chance = jnp.exp(square * r - lse)
                if other == block:
                    chance = jnp.where(causal_tile(), chance, 0.0)
                tilted = s * r
                signed = (tilted * chance).astype(BF)
                slope = r * r * r + tilted * tilted
                dsc = (chance * (ds * slope - tilted * delta)).astype(BF)
                acc = acc + nn(mixt_ref[pl.ds(OWN + base, HEAD_DIM), there], dsc)
                dk = nt(dsc, queries)
                dv = nt(signed, dout)
                if other == block:
                    dk_ref[there, :] = dk
                    dv_ref[there, :] = dv
                else:
                    dk_ref[there, :] += dk
                    dv_ref[there, :] += dv
            dq_ref[:, here] = acc * HEAD_DIM**-0.5
        dm_ref[h, :, 0:HEAD_DIM] = dq_ref[...].T.astype(BF)
        dm_ref[h, :, HEAD_DIM : 2 * HEAD_DIM] = dk_ref[...].astype(BF)
        dm_ref[h, :, 2 * HEAD_DIM :] = dv_ref[...].astype(BF)

    for h in range(OWN_HEADS):
        for kind in range(3):
            to = kind * OWN + h * HEAD_DIM
            mix_ref[:, to : to + HEAD_DIM] = dm_ref[h, :, kind * HEAD_DIM : (kind + 1) * HEAD_DIM]
    total_ref[...] = jnp.zeros_like(total_ref)
    for load in loads:
        load.wait()
    for block in range(4):
        here = slice(block * TILE, (block + 1) * TILE)
        first = nt(mix_ref[here, :], w_ref[...])
        first_ref[block] = first.astype(BF)
        total_ref[...] += jnp.sum(first * normed_ref[here, :].astype(F32), axis=0, keepdims=True)
    outs = (f3_ref, f2_ref, f1_ref, f0_ref)
    copies = [
        pltpu.make_async_copy(first_ref.at[jnp.bitwise_xor(z, 3 - k)], ref, sems.at[k]) for k, ref in enumerate(outs)
    ]
    for copy in copies:
        copy.start()
    gain_one = total_ref[...] / gain_ref[0:1]
    gain_two = dgain_ref[...]
    for to in range(4):
        e = jnp.bitwise_xor(place, to)
        e_x, e_y = jnp.bitwise_and(e, 1), e // 2
        g = nn(normed_ref[:, to * SHARD : (to + 1) * SHARD].T, mix_ref[...]).astype(BF)
        span = slice(to * SHARD, (to + 1) * SHARD)
        gains = jnp.concatenate([gain_one[:, span], gain_two[:, span], jnp.zeros((14, SHARD), F32)], axis=0)
        gains = jnp.concatenate([gains, jnp.zeros((16, HALF - SHARD), F32)], axis=1).astype(BF)
        for side in range(2):
            at = side * PART
            head_ref[side, e_y, e_x, 0:PART] = g[at : at + PART, 0:HALF]
            head_ref[side, e_y, e_x, PART : PART + QUART, 0:OWN] = g[at : at + QUART, HALF:]
            head_ref[side, e_y, e_x, PART : PART + QUART, OWN:] = g[at + QUART : at + PART, HALF:]
            head_ref[side, e_y, e_x, PART + QUART :] = gains if side == 0 else jnp.zeros_like(gains)
    more = [
        pltpu.make_async_copy(head_ref.at[1 - core], gsend_ref.at[:, :, pl.ds(0, HEAD_ROWS)], sems.at[4]),
        pltpu.make_async_copy(head_ref.at[core], gkeep_ref.at[:, :, pl.ds(0, HEAD_ROWS)], sems.at[5]),
    ]
    for copy in more:
        copy.start()
    for copy in copies + more:
        copy.wait()


def attend_back(kv, mixt, att, lse, dout, normed, w, gain, dgain, keep, send):
    length = normed.shape[0]
    return pl.pallas_call(
        attend_back_kernel,
        in_specs=[WHOLE] * 5 + [ANYWHERE] * 2 + [WHOLE] * 2 + [ANYWHERE] * 2,
        out_specs=[ANYWHERE] * 6,
        out_shape=[jax.ShapeDtypeStruct((TILE, D), BF)] * 4 + [jax.ShapeDtypeStruct(keep.shape, BF)] * 2,
        input_output_aliases={9: 4, 10: 5},
        scratch_shapes=[
            pltpu.VMEM((HEAD_DIM, length), F32),
            pltpu.VMEM((length, HEAD_DIM), F32),
            pltpu.VMEM((length, HEAD_DIM), F32),
            pltpu.VMEM((OWN_HEADS, length, 3 * HEAD_DIM), BF),
            pltpu.VMEM((length, MIX), BF),
            pltpu.VMEM((1, D), F32),
            pltpu.VMEM((4, TILE, D), BF),
            pltpu.VMEM((2, 2, 2, HEAD_ROWS, HALF), BF),
            pltpu.SemaphoreType.DMA((6,)),
            pltpu.VMEM((length, D), BF),
            pltpu.VMEM((D, MIX), BF),
            pltpu.SemaphoreType.DMA((2,)),
        ],
        compiler_params=pltpu.CompilerParams(vmem_limit_bytes=VMEM_LIMIT),
        cost_estimate=pl.CostEstimate(flops=1000, bytes_accessed=1000, transcendentals=0),
        name="attend_back",
    )(kv, mixt, att, lse, dout, normed, w, gain, dgain, keep, send)


def is_inner():
    z = lax.axis_index("ctx") // 2
    return (z == 1) | (z == 2)


def last_kernel(first_ref, pair_ref, middle_ref, x_ref, gain_ref, dhidden_ref, keep_ref, send_ref, grad_ref, sems):
    core = lax.axis_index("ctx") % 2
    rows = x_ref.shape[0] // 2
    dy = first_ref[...].astype(F32) + pair_ref[...].astype(F32)
    dy = dy + jnp.where(is_inner(), middle_ref[...].astype(F32), 0.0)
    xhat, inverse = normalised(x_ref[...].astype(F32))
    grad = dhidden_ref[...] + norm_back(xhat, inverse, gain_ref[0:1], dy)
    grad_ref[0], grad_ref[1] = grad[:rows], grad[rows:]
    run_copies(((grad_ref.at[1 - core], send_ref), (grad_ref.at[core], keep_ref)), sems)


def last(*args):
    rows = TILE // 2
    return call(
        last_kernel,
        "last",
        [WHOLE] * 6,
        [((rows, D), F32), ((rows, D), F32)],
        [pltpu.VMEM((2, rows, D), F32), pltpu.SemaphoreType.DMA((2,))],
        10**7,
        args,
        [ANYWHERE] * 2,
    )


def line_slots():
    z = lax.axis_index("ctx") // 2
    return z, jnp.bitwise_xor(z, 1), jnp.where(z < 2, 2, 1), jnp.where(z < 2, 3, 0)


def finish_feed_kernel(*refs):
    mine, theirs, (gup_ref, gdown_ref) = refs[:4], refs[4:8], refs[8:]
    core = lax.axis_index("ctx") % 2
    place = lax.axis_index("wshard")
    rows = D // 8
    for group, side in ((mine, core), (theirs, 1 - core)):
        for ref, slot in zip(group, line_slots()):
            at = pl.multiple_of(slot * QUART, 16)
            for k in range(4):
                to = pl.multiple_of(jnp.bitwise_xor(place, k) * D + side * HALF, 128)
                gup_ref[pl.ds(at, QUART), pl.ds(to, HALF)] = ref[k * QUART : (k + 1) * QUART].astype(F32)
            at = pl.multiple_of((2 * slot + side) * rows, 32)
            for half in range(2):
                share = ref[SHARD + half * rows : SHARD + (half + 1) * rows]
                gdown_ref[pl.ds(at, rows), half * HALF : (half + 1) * HALF] = share.astype(F32)


def finish_feed(*args):
    return call(
        finish_feed_kernel, "finish_feed", [WHOLE] * 8, [((SHARD, 4 * D), F32), ((D, D), F32)], [], 10**7, args
    )


def finish_heads_kernel(*refs):
    mine, theirs, outs, (gout_ref, gqkv_ref, one_ref, two_ref) = refs[:4], refs[4:8], refs[8:10], refs[10:]
    slots = line_slots()
    first = lax.axis_index("ctx") % 2 == 0
    out, other_out = [ref[...].astype(F32) for ref in outs]
    for half in range(2):
        here, cols = slice(half * PART, (half + 1) * PART), slice(half * HALF, (half + 1) * HALF)
        gout_ref[0:PART, cols] = jnp.where(first, out[here], other_out[here])
        gout_ref[PART:, cols] = jnp.where(first, other_out[here], out[here])
    mine, theirs = [[ref[...].astype(F32) for ref in group] for group in (mine, theirs)]
    low = [jnp.where(first, a, b) for a, b in zip(mine, theirs)]
    high = [jnp.where(first, b, a) for a, b in zip(mine, theirs)]
    gains = sum(block[PART + QUART :, 0:SHARD] for block in low)
    one_ref[...], two_ref[...] = gains[0], gains[1]
    for slot in range(4):
        for side, group in enumerate((low, high)):
            block = jnp.where(
                slot == slots[0],
                group[0],
                jnp.where(slot == slots[1], group[1], jnp.where(slot == slots[2], group[2], group[3])),
            )
            at, to = side * PART, slot * OWN
            gqkv_ref[at : at + PART, to : to + OWN] = block[0:PART, 0:OWN]
            gqkv_ref[at : at + PART, D + to : D + to + OWN] = block[0:PART, OWN:]
            gqkv_ref[at : at + QUART, 2 * D + to : 2 * D + to + OWN] = block[PART : PART + QUART, 0:OWN]
            gqkv_ref[at + QUART : at + PART, 2 * D + to : 2 * D + to + OWN] = block[PART : PART + QUART, OWN:]


def finish_heads(*args):
    return call(
        finish_heads_kernel,
        "finish_heads",
        [WHOLE] * 10,
        [((SHARD, D), F32), ((SHARD, 3 * D), F32), ((SHARD,), F32), ((SHARD,), F32)],
        [],
        10**7,
        args,
    )


def pick(value, index, axis=0):
    return lax.dynamic_index_in_dim(value, index, axis, keepdims=False)


def across_w(value, flip):
    return lax.ppermute(value, "wshard", [(i, i ^ flip) for i in range(4)])


def across_core(value):
    return lax.ppermute(value, "ctx", [(i, i ^ 1) for i in range(8)])


def between_z(value, pairs):
    return lax.ppermute(value, "ctx", [(2 * a + c, 2 * b + c) for a, b in pairs for c in range(2)])


Z_GROUPS = [[0, 2, 4, 6], [1, 3, 5, 7]]


def after(value, *others):
    return lax.optimization_barrier((value, *others))[0]


PAIRS = [(0, 1), (1, 0), (2, 3), (3, 2)]
MIDDLE = [(1, 2), (2, 1), (0, 0), (3, 3)]


def line_z(block):
    pair = between_z(block, PAIRS)
    mid_near = between_z(block, MIDDLE)
    near = between_z(mid_near, PAIRS)
    mid_far = between_z(pair, MIDDLE)
    far = between_z(mid_far, PAIRS)
    return block, pair, near, far, mid_near, mid_far


TO_MIDDLE = [(0, 1), (3, 2)]
TO_ENDS = [(1, 0), (2, 3)]
ACROSS = [(1, 2), (2, 1)]


def own_slot(slots, x_first):
    one, two = (1, 2) if x_first else (2, 1)
    got = across_w(slots[1], one)
    far = slots[0, 1] + got[1]
    return (slots[0, 0] + got[0]) + across_w(far, two)


def gather_plane(block, *others):
    half = block.shape[0] // 2
    from_x, from_y = across_w(block, 1), across_w(block, 2)
    first, second = from_x[:half], from_y[half:]
    if others:
        first, second, *_ = tied(first, second, *others)
    return block, from_x, from_y, across_w(first, 2), across_w(second, 1)


def tied(*values):
    return lax.optimization_barrier(values)


def local_grid(tokens, gain_one, w_qkv, w_out, gain_two, w_up, w_down, cotangent):
    core = lax.axis_index("ctx") % 2
    z = lax.axis_index("ctx") // 2
    place = lax.axis_index("wshard")
    inner = (z == 1) | (z == 2)

    def both_micros(kept, got):
        return jnp.where(core == 0, jnp.stack([kept, got]), jnp.stack([got, kept]))[:, None]

    tok, cot = tokens[:, 0], cotangent[:, 0]
    kept = jnp.concatenate([pick(tok, core), pick(cot, core)])
    got = across_core(jnp.concatenate([pick(tok, 1 - core), pick(cot, 1 - core)]))
    half = TILE // 2
    own = [jnp.where(core == 0, a, b) for a, b in ((kept, got), (got, kept))]
    x_block = jnp.concatenate([own[0][:half], own[1][:half]])
    cot = jnp.concatenate([own[0][half:], own[1][half:]])

    w_heads = pick(w_qkv.reshape(SHARD, 3, 4, OWN), z, 2).reshape(SHARD, MIX)
    gains = jnp.pad(jnp.stack([gain_one, gain_two]), ((0, 30), (0, MIX - SHARD)))
    x_all = lax.all_to_all(
        jnp.broadcast_to(x_block, (4,) + x_block.shape), "ctx", 0, 0, tiled=True, axis_index_groups=Z_GROUPS
    )
    x_on, x_rest, y_on, y_rest = parcels(cot, w_out, w_up)
    x_on, y_on = across_w(x_on, 1), across_w(y_on, 2)
    x_on, y_on, w_heads = tied(x_on, y_on, jnp.concatenate([w_heads, gains]))
    heads = gather_plane(w_heads)
    corner_a, corner_b = across_w(x_on, 2), across_w(y_on, 1)
    x_rest, y_rest, corner_a, corner_b = tied(x_rest, y_rest, corner_a, corner_b)
    x_rest, y_rest = across_w(x_rest, 1), across_w(y_rest, 2)
    normed_all, kv, mixt, att, att_low, lse, w_full, gains = attend(x_all, heads)
    shared = x_on, x_rest, y_on, y_rest, corner_a, corner_b
    att_home = lax.all_to_all(att_low, "ctx", 0, 0, tiled=True, axis_index_groups=Z_GROUPS).reshape(D, -1)
    wout_full, up, cots = assemble(cot, w_out, w_up, shared)
    hidden, normed_two = project(att_home, x_block, gains, wout_full)

    active0, dup0, out0, dout0 = feed_own(normed_two, cots, up, w_down)
    ns = gather_plane(normed_two, active0)
    active1, dup1, out1, dout1 = feed_near(ns[1], ns[2], cots, up, w_down)
    active2, dup2, *parts = feed_far(ns[3], ns[4], cots, out1, dout1, up, w_down)
    parts, (a, a_far, b, b_far) = parts[:4], parts[4:]
    got_a, got_b = across_w(a, 1), across_w(b, 2)
    shares = feed_grads(ns, cots, (active0, active1, active2), (dup0, dup1, dup2))
    shares, got_a, got_b = tied(shares, got_a, got_b)
    shares = lax.psum_scatter(shares, "ctx", scatter_dimension=0)
    more_a, more_b = across_w(a_far + got_a[1], 2), across_w(b_far + got_b[1], 1)
    d_hidden, d_att, d_branch, d_gain_two = turn(
        hidden, gains, dout0, (got_a, more_a, got_b, more_b), cot, wout_full
    )
    d_out = lax.all_to_all(d_att, "ctx", 0, 0, tiled=True, axis_index_groups=Z_GROUPS)
    keep, send = out_grad(att_home, d_branch)
    d_out, keep, send = tied(d_out, keep, send)
    a, a_far, b, b_far = parts
    got_a, got_b = across_w(a, 1), across_w(b, 2)
    *firsts, keep, send = attend_back(
        kv, mixt, att, lse, d_out, normed_all, w_full, gains, d_gain_two, keep, send
    )
    *firsts, keep, send, shares, got_a, got_b = tied(*firsts, keep, send, shares, got_a, got_b)

    got = between_z(firsts[3], TO_MIDDLE)
    both = firsts[2] + jnp.where(inner, got, BF(0))
    outer, middle = between_z(both, TO_MIDDLE), between_z(both, ACROSS)
    pair = between_z(firsts[1] + jnp.where(inner, middle, BF(0)), PAIRS)
    middle = between_z(firsts[3] + outer, ACROSS)

    ups = [shares[0]] + [across_w(shares[e], e) for e in (1, 2, 3)]
    share = jnp.concatenate(ups + [shares[4:].reshape(SHARD, HALF)])
    share_pair, share_mid = between_z(share, PAIRS), between_z(share, ACROSS)
    share_near, share_mid_far = between_z(share_mid, TO_ENDS), between_z(share_pair, ACROSS)
    share_far = between_z(share_mid_far, TO_ENDS)
    blocks = share, share_pair, jnp.where(inner, share_mid, share_near), jnp.where(inner, share_mid_far, share_far)
    grad_up, grad_down = finish_feed(*blocks, *(across_core(block) for block in blocks))

    sums, a_far, b_far = tied(keep + across_core(send), a_far, b_far)
    sums_got = across_w(sums[1], 2)
    sums_far = across_w(sums[0, 1] + sums_got[1], 1)
    sums, a_far, b_far = tied((sums[0, 0] + sums_got[0]) + sums_far, a_far, b_far)
    more_a, more_b = across_w(a_far + got_a[1], 2), across_w(b_far + got_b[1], 1)
    result_keep, result_send = give(hidden, out0, (got_a, more_a, got_b, more_b))
    out_result = both_micros(result_keep, across_core(result_send))
    sums_pair, head_mid = between_z(sums, PAIRS), between_z(sums[:HEAD_ROWS], ACROSS)
    out = sums[HEAD_ROWS:] + sums_pair[HEAD_ROWS:]
    head_near = between_z(head_mid, TO_ENDS)
    sums_far = between_z(jnp.concatenate([sums_pair[:HEAD_ROWS], out]), ACROSS)
    pair, middle, out_result, sums_far, head_near = tied(pair, middle, out_result, sums_far, head_near)
    sums_far = jnp.concatenate([sums_far[:HEAD_ROWS], out + sums_far[HEAD_ROWS:]])
    sums_last = between_z(sums_far, TO_ENDS)
    grad_keep, grad_send = last(firsts[0], pair, middle, x_block, gains, d_hidden)
    out_tokens = both_micros(grad_keep, across_core(grad_send))
    sums_last = jnp.where(inner, sums_far, sums_last)
    head_near = jnp.where(inner, head_mid, head_near)
    blocks = sums[:HEAD_ROWS], sums_pair[:HEAD_ROWS], head_near, sums_last[:HEAD_ROWS]
    others = [across_core(block) for block in (*blocks[:3], sums_last)]
    grad_out, grad_qkv, gain_one, gain_two = finish_heads(
        *blocks, *others[:3], others[3][:HEAD_ROWS], sums_last[HEAD_ROWS:], others[3][HEAD_ROWS:]
    )
    return (
        out_result,
        out_tokens,
        gain_one,
        grad_qkv,
        grad_out,
        gain_two,
        grad_up,
        grad_down,
    )


def local(tokens, *rest):
    fits = (
        lax.axis_size("wshard") == 4
        and lax.axis_size("ctx") == 8
        and tokens.shape[:2] == (2, 1)
        and 2 * tokens.shape[2] == TILE
    )
    return (local_grid if fits else local_any)(tokens, *rest)


def solution(mesh):
    placed = (
        P(None, "wshard", "ctx", None),
        P("wshard"),
        P("wshard", None),
        P("wshard", None),
        P("wshard"),
        P("wshard", None),
        P("wshard", None),
        P(None, "wshard", "ctx", None),
    )
    return jax.shard_map(
        local,
        mesh=mesh,
        in_specs=placed,
        out_specs=(
            P(None, "wshard", "ctx", None),
            P(None, "wshard", "ctx", None),
            P("wshard"),
            P("wshard", None),
            P("wshard", None),
            P("wshard"),
            P("wshard", None),
            P("wshard", None),
        ),
        check_vma=False,
    )
```

```python
import jax
import jax.numpy as jnp
from jax import lax
from jax.experimental import pallas as pl
from jax.experimental.pallas import tpu as pltpu
from jax.sharding import PartitionSpec as P

D = 768
HEADS = 12
HEAD_DIM = 64


EPSILON = 1e-05


def passed_along(value, axis, by):
    count = lax.axis_size(axis)
    return lax.ppermute(value, axis, [(i, (i + by) % count) for i in range(count)])


def layer_norm(inputs, scaling):
    centred = inputs - jnp.mean(inputs, axis=-1, keepdims=True)
    variance = jnp.mean(centred * centred, axis=-1, keepdims=True)
    return centred * lax.rsqrt(variance + EPSILON) * scaling


def gelu_smooth(values_in):
    return jax.nn.gelu(values_in, approximate=True)


def contract_rows(left_side, right_side):
    return lax.dot_general(
        left_side, right_side, (((0,), (0,)), ((), ())), preferred_element_type=jnp.float32
    )


def times_rows(left_side, right_side):
    return lax.dot_general(
        left_side, right_side, (((1,), (1,)), ((), ())), preferred_element_type=jnp.float32
    )


def pair_grads(query_h, dout_h, log_total, row_delta, query_pos, key_h, value_h, key_pos):
    scaling = HEAD_DIM ** (-0.5)
    scores = (
        jnp.einsum("qhe,khe->hqk", query_h, key_h, preferred_element_type=jnp.float32) * scaling
    )
    visible = key_pos[None, None, :] <= query_pos[None, :, None]
    magnitude = jnp.sqrt(scores * scores + 1.0)
    tilted = scores / magnitude
    chance = jnp.exp(jnp.where(visible, magnitude - log_total[:, :, None], -1e30))
    signed = (tilted * chance).astype(jnp.bfloat16)
    d_signed = jnp.einsum("qhe,khe->hqk", dout_h, value_h, preferred_element_type=jnp.float32)
    slope = 1.0 / (magnitude * magnitude * magnitude) + tilted * tilted
    d_scores = (chance * (d_signed * slope - tilted * row_delta[:, :, None])).astype(jnp.bfloat16)
    d_query = (
        jnp.einsum("hqk,khe->qhe", d_scores, key_h, preferred_element_type=jnp.float32) * scaling
    )
    d_key = (
        jnp.einsum("hqk,qhe->khe", d_scores, query_h, preferred_element_type=jnp.float32) * scaling
    )
    d_value = jnp.einsum("hqk,qhe->khe", signed, dout_h, preferred_element_type=jnp.float32)
    return (d_query, d_key, d_value)


def keep_state(loop_state):
    return loop_state


def local_any(tokens, gain_one, w_qkv, w_out, gain_two, w_up, w_down, cotangent):
    gathered = (
        lax.all_gather(gain_one, "wshard", axis=0, tiled=True),
        lax.all_gather(w_qkv, "wshard", axis=0, tiled=True),
        lax.all_gather(w_out, "wshard", axis=0, tiled=True),
        lax.all_gather(gain_two, "wshard", axis=0, tiled=True),
        lax.all_gather(w_up, "wshard", axis=0, tiled=True),
        lax.all_gather(w_down, "wshard", axis=0, tiled=True),
    )
    full_gain_one, full_qkv, full_out, full_gain_two, full_up, full_down = gathered
    gain_first = full_gain_one.astype(jnp.float32)
    gain_second = full_gain_two.astype(jnp.float32)
    cycle_size = lax.axis_size("ctx")
    cycle_place = lax.axis_index("ctx")
    micro_count = tokens.shape[0]
    local_len = tokens.shape[2]
    scaling = HEAD_DIM ** (-0.5)
    query_pos = cycle_place * local_len + jnp.arange(local_len, dtype=jnp.int32)
    sum_gain_one = jnp.zeros((D,), jnp.float32)
    sum_gain_two = jnp.zeros((D,), jnp.float32)
    sum_qkv = jnp.zeros(full_qkv.shape, jnp.float32)
    sum_out = jnp.zeros(full_out.shape, jnp.float32)
    sum_up = jnp.zeros(full_up.shape, jnp.float32)
    sum_down = jnp.zeros(full_down.shape, jnp.float32)
    results = []
    grad_list = []
    for micro_index in range(micro_count):
        inputs = tokens[micro_index, 0].astype(jnp.float32)
        normed_f, norm_back = jax.vjp(layer_norm, inputs, gain_first)
        normed = normed_f.astype(jnp.bfloat16)
        mixed_all = jnp.dot(normed, full_qkv, preferred_element_type=jnp.float32).astype(
            jnp.bfloat16
        )
        keys_flat = mixed_all[:, D : 2 * D]
        values_flat = mixed_all[:, 2 * D :]
        query_h = mixed_all[:, :D].reshape(local_len, HEADS, HEAD_DIM)
        key_h = keys_flat.reshape(local_len, HEADS, HEAD_DIM)
        value_h = values_flat.reshape(local_len, HEADS, HEAD_DIM)
        start_state = (
            jnp.zeros((HEADS, local_len, HEAD_DIM), jnp.float32),
            jnp.ones((HEADS, local_len), jnp.float32),
            jnp.zeros((HEADS, local_len), jnp.float32),
        )
        shard_piece = (
            lax.all_gather(keys_flat, "ctx", axis=0, tiled=True),
            lax.all_gather(values_flat, "ctx", axis=0, tiled=True),
        )

        def compute(loop_state):
            accumulated, top_value, totals = loop_state
            key_piece = shard_piece[0].reshape(-1, HEADS, HEAD_DIM)
            value_piece = shard_piece[1].reshape(-1, HEADS, HEAD_DIM)
            key_pos = jnp.arange(key_piece.shape[0], dtype=jnp.int32)
            scores = (
                jnp.einsum("qhe,khe->hqk", query_h, key_piece, preferred_element_type=jnp.float32)
                * scaling
            )
            visible = key_pos[None, None, :] <= query_pos[None, :, None]
            magnitude = jnp.sqrt(scores * scores + 1.0)
            new_top = jnp.maximum(top_value, jnp.max(jnp.where(visible, magnitude, 0.0), axis=-1))
            weighted = jnp.exp(jnp.where(visible, magnitude - new_top[:, :, None], -1e30))
            signed = (scores / magnitude * weighted).astype(jnp.bfloat16)
            accumulated = jnp.einsum(
                "hqk,khe->hqe", signed, value_piece, preferred_element_type=jnp.float32
            )
            totals = jnp.sum(weighted, axis=-1)
            return (accumulated, new_top, totals)

        accumulated, top_value, totals = lax.cond(
            jnp.int32(0) <= query_pos[-1], compute, keep_state, start_state
        )
        attended_h = accumulated / totals[:, :, None]
        log_total = top_value + jnp.log(totals)
        attended = jnp.transpose(attended_h, (1, 0, 2)).reshape(local_len, D)
        attended_low = attended.astype(jnp.bfloat16)
        hidden = inputs + jnp.dot(attended_low, full_out, preferred_element_type=jnp.float32)
        normed_two_f, norm_two_back = jax.vjp(layer_norm, hidden, gain_second)
        normed_two = normed_two_f.astype(jnp.bfloat16)
        upward = jnp.dot(normed_two, full_up, preferred_element_type=jnp.float32)
        active_f, gelu_back = jax.vjp(gelu_smooth, upward)
        active = active_f.astype(jnp.bfloat16)
        result_rows = hidden + jnp.dot(active, full_down, preferred_element_type=jnp.float32)
        results.append(result_rows.astype(jnp.bfloat16))
        d_result = cotangent[micro_index, 0]
        sum_down = sum_down + contract_rows(active, d_result)
        d_active = times_rows(d_result, full_down)
        d_upward = gelu_back(d_active)[0].astype(jnp.bfloat16)
        sum_up = sum_up + contract_rows(normed_two, d_upward)
        d_normed_two = times_rows(d_upward, full_up)
        d_hidden_norm, d_gain_two = norm_two_back(d_normed_two)
        sum_gain_two = sum_gain_two + d_gain_two
        d_hidden = d_result.astype(jnp.float32) + d_hidden_norm
        d_branch = d_hidden.astype(jnp.bfloat16)
        sum_out = sum_out + contract_rows(attended_low, d_branch)
        d_attended = times_rows(d_branch, full_out).astype(jnp.bfloat16)
        dout_h = d_attended.reshape(local_len, HEADS, HEAD_DIM)
        row_delta = jnp.einsum("qhe,hqe->hq", dout_h.astype(jnp.float32), attended_h)
        zero_block = jnp.zeros((local_len, HEADS, HEAD_DIM), jnp.float32)

        def turn_keys(turn_index, loop_state):
            key_b, value_b, d_key_b, d_value_b, d_query = loop_state
            owner_index = (cycle_place + turn_index) % cycle_size
            key_pos = owner_index * local_len + jnp.arange(local_len, dtype=jnp.int32)

            def work(partial_sums):
                contrib = pair_grads(
                    query_h, dout_h, log_total, row_delta, query_pos, key_b, value_b, key_pos
                )
                return (
                    partial_sums[0] + contrib[0],
                    partial_sums[1] + contrib[1],
                    partial_sums[2] + contrib[2],
                )

            needed = (turn_index == 0) | (cycle_place + turn_index >= cycle_size)
            d_query, d_key_b, d_value_b = lax.cond(
                needed, work, keep_state, (d_query, d_key_b, d_value_b)
            )
            key_b, value_b = passed_along((key_b, value_b), "ctx", -1)
            d_key_b, d_value_b = (
                passed_along(d_key_b.astype(jnp.bfloat16), "ctx", -1).astype(d_key_b.dtype),
                passed_along(d_value_b.astype(jnp.bfloat16), "ctx", -1).astype(d_value_b.dtype),
            )
            return (key_b, value_b, d_key_b, d_value_b, d_query)

        final_state = lax.fori_loop(
            0, cycle_size, turn_keys, (key_h, value_h, zero_block, zero_block, zero_block)
        )
        d_key = final_state[2]
        d_value = final_state[3]
        d_query = final_state[4]
        d_mixed = jnp.concatenate(
            [
                d_query.reshape(local_len, D),
                d_key.reshape(local_len, D),
                d_value.reshape(local_len, D),
            ],
            axis=1,
        ).astype(jnp.bfloat16)
        sum_qkv = sum_qkv + contract_rows(normed, d_mixed)
        d_normed = times_rows(d_mixed, full_qkv)
        d_inputs_norm, d_gain_one = norm_back(d_normed)
        sum_gain_one = sum_gain_one + d_gain_one
        grad_list.append(d_hidden + d_inputs_norm)
    shares = (
        lax.psum_scatter(
            sum_gain_one.astype(jnp.bfloat16), "wshard", scatter_dimension=0, tiled=True
        ).astype(jnp.float32),
        lax.psum_scatter(
            sum_qkv.astype(jnp.bfloat16), "wshard", scatter_dimension=0, tiled=True
        ).astype(jnp.float32),
        lax.psum_scatter(
            sum_out.astype(jnp.bfloat16), "wshard", scatter_dimension=0, tiled=True
        ).astype(jnp.float32),
        lax.psum_scatter(
            sum_gain_two.astype(jnp.bfloat16), "wshard", scatter_dimension=0, tiled=True
        ).astype(jnp.float32),
        lax.psum_scatter(
            sum_up.astype(jnp.bfloat16), "wshard", scatter_dimension=0, tiled=True
        ).astype(jnp.float32),
        lax.psum_scatter(
            sum_down.astype(jnp.bfloat16), "wshard", scatter_dimension=0, tiled=True
        ).astype(jnp.float32),
    )
    summed = (
        lax.psum(shares[0].astype(jnp.bfloat16), "ctx").astype(jnp.float32),
        lax.psum(shares[1].astype(jnp.bfloat16), "ctx").astype(jnp.float32),
        lax.psum(shares[2].astype(jnp.bfloat16), "ctx").astype(jnp.float32),
        lax.psum(shares[3].astype(jnp.bfloat16), "ctx").astype(jnp.float32),
        lax.psum(shares[4].astype(jnp.bfloat16), "ctx").astype(jnp.float32),
        lax.psum(shares[5].astype(jnp.bfloat16), "ctx").astype(jnp.float32),
    )
    result_out = jnp.stack(results)[:, None]
    grad_out_tokens = jnp.stack(grad_list)[:, None]
    return (
        result_out,
        grad_out_tokens,
        summed[0],
        summed[1],
        summed[2],
        summed[3],
        summed[4],
        summed[5],
    )


BF = jnp.bfloat16
F32 = jnp.float32
TILE = 256
SHARD = D // 4
OWN_HEADS = HEADS // 4
OWN = OWN_HEADS * HEAD_DIM
MIX = 3 * OWN
HEAD_ROWS = 160
PART = SHARD // 2
QUART = SHARD // 4
HALF = D // 2
MIDDLE_ROW = 224
VMEM_LIMIT = 56 * 1024 * 1024
WHOLE = pl.BlockSpec(memory_space=pltpu.VMEM)
ANYWHERE = pl.BlockSpec(memory_space=pl.ANY)


def nn(a, b):
    return lax.dot_general(a, b, (((1,), (0,)), ((), ())), preferred_element_type=F32)


def nt(a, b):
    return lax.dot_general(a, b, (((1,), (1,)), ((), ())), preferred_element_type=F32)


def normalised(x):
    centred = x - jnp.mean(x, axis=-1, keepdims=True)
    variance = jnp.mean(centred * centred, axis=-1, keepdims=True)
    inverse = lax.rsqrt(variance + EPSILON)
    return centred * inverse, inverse


def norm_back(xhat, inverse, gain, dy):
    g = dy * gain
    mean_g = jnp.mean(g, axis=-1, keepdims=True)
    mean_gx = jnp.mean(g * xhat, axis=-1, keepdims=True)
    return (g - mean_g - xhat * mean_gx) * inverse


def causal_tile():
    rows = lax.broadcasted_iota(jnp.int32, (TILE, TILE), 0)
    cols = lax.broadcasted_iota(jnp.int32, (TILE, TILE), 1)
    return rows <= cols


def call(kernel, name, ins, outs, scratch, flops, args, out_specs=None):
    moved = sum(a.size * a.dtype.itemsize for a in args)
    return pl.pallas_call(
        kernel,
        in_specs=ins,
        out_specs=out_specs or [WHOLE] * len(outs),
        out_shape=[jax.ShapeDtypeStruct(shape, kind) for shape, kind in outs],
        scratch_shapes=scratch,
        compiler_params=pltpu.CompilerParams(vmem_limit_bytes=VMEM_LIMIT),
        cost_estimate=pl.CostEstimate(flops=1000, bytes_accessed=1000, transcendentals=0),
        name=name,
    )(*args)


def shard_rows_of(pieces, which, first, count):
    if which < 3:
        return pieces[which].at[pl.ds(first, count)]
    half = pieces[3].shape[0]
    if first < half:
        return pieces[3].at[pl.ds(first, count)]
    return pieces[4].at[pl.ds(first - half, count)]


def run_copies(pairs, sems):
    copies = [pltpu.make_async_copy(src, dst, sems.at[i]) for i, (src, dst) in enumerate(pairs)]
    for copy in copies:
        copy.start()
    for copy in copies:
        copy.wait()


def attend_kernel(x_ref, w0, w1, w2, w3, w4,
                  normed_out, kv_out, mixt_out, att_ref, low_ref, lse_ref, wfull_out, gains_ref,
                  normed_ref, kv_ref, mixt_ref, wfull_ref, s_ref, g_ref, wsems, sems):
    place = lax.axis_index("wshard")
    pieces = (w0, w1, w2, w3, w4)
    half = w3.shape[0]
    pairs = []
    for k in range(4):
        to = pl.multiple_of(jnp.bitwise_xor(place, k) * SHARD, SHARD)
        if k < 3:
            pairs.append((shard_rows_of(pieces, k, 0, SHARD), wfull_ref.at[pl.ds(to, SHARD)]))
        else:
            pairs.append((w3, wfull_ref.at[pl.ds(to, half)]))
            pairs.append((w4.at[pl.ds(0, SHARD - half)], wfull_ref.at[pl.ds(to + half, SHARD - half)]))
        source = w4.at[pl.ds(SHARD - half, 16)] if k == 3 else pieces[k].at[pl.ds(SHARD, 16)]
        pairs.append((source, g_ref.at[k]))
    run_copies(pairs, wsems)
    gains = jnp.concatenate([g_ref[jnp.bitwise_xor(place, j)][0:8, 0:SHARD].astype(F32) for j in range(4)], axis=1)
    gains_ref[...] = gains
    for row in range(4):
        here = slice(row * TILE, (row + 1) * TILE)
        xhat, _ = normalised(x_ref[row].astype(F32))
        normed = (xhat * gains[0:1]).astype(BF)
        normed_ref[here, :] = normed
        mix = nn(normed, wfull_ref[...]).astype(BF)
        mixt_ref[:, here] = mix.T
        for h in range(OWN_HEADS):
            kv_ref[h, here, 0:HEAD_DIM] = mix[:, OWN + h * HEAD_DIM : OWN + (h + 1) * HEAD_DIM]
            kv_ref[h, here, HEAD_DIM:] = mix[:, 2 * OWN + h * HEAD_DIM : 2 * OWN + (h + 1) * HEAD_DIM]

    pairs = ((normed_ref, normed_out), (kv_ref, kv_out), (mixt_ref, mixt_out), (wfull_ref, wfull_out))
    copies = [pltpu.make_async_copy(src, dst, sems.at[k]) for k, (src, dst) in enumerate(pairs)]
    for copy in copies:
        copy.start()

    @pl.loop(0, OWN_HEADS)
    def _(h):
        base = pl.multiple_of(h * HEAD_DIM, HEAD_DIM)
        for block in range(4):
            here = slice(block * TILE, (block + 1) * TILE)
            queries = mixt_ref[pl.ds(base, HEAD_DIM), here] * BF(HEAD_DIM**-0.5)
            top = jnp.zeros((1, TILE), F32)
            for other in range(block + 1):
                there = slice(other * TILE, (other + 1) * TILE)
                s = nn(kv_ref[h, there, 0:HEAD_DIM], queries)
                s_ref[there, :] = s
                size = jnp.abs(s)
                if other == block:
                    size = jnp.where(causal_tile(), size, 0.0)
                top = jnp.maximum(top, jnp.max(size, axis=0, keepdims=True))
            top = jnp.sqrt(top * top + 1.0)
            total = jnp.zeros((1, TILE), F32)
            acc = jnp.zeros((HEAD_DIM, TILE), F32)
            for other in range(block + 1):
                there = slice(other * TILE, (other + 1) * TILE)
                s = s_ref[there, :]
                square = s * s + 1.0
                r = lax.rsqrt(square)
                p = jnp.exp(square * r - top)
                if other == block:
                    p = jnp.where(causal_tile(), p, 0.0)
                total = total + jnp.sum(p, axis=0, keepdims=True)
                signed = (s * r * p).astype(BF)
                acc = acc + nn(mixt_ref[pl.ds(2 * OWN + base, HEAD_DIM), there], signed)
            att = acc / total
            att_ref[pl.ds(base, HEAD_DIM), here] = att
            low_ref[block, pl.ds(base, HEAD_DIM), :] = att.astype(BF)
            lse_ref[pl.ds(h, 1), here] = top + jnp.log(total)

    for copy in copies:
        copy.wait()


def attend(x_all, pieces):
    length = 4 * TILE
    return call(
        attend_kernel,
        "attend",
        [WHOLE] + [ANYWHERE] * 5,
        [
            ((length, D), BF),
            ((OWN_HEADS, length, 2 * HEAD_DIM), BF),
            ((MIX, length), BF),
            ((OWN, length), F32),
            ((4, OWN, TILE), BF),
            ((8, length), F32),
            ((D, MIX), BF),
            ((8, D), F32),
        ],
        [
            pltpu.VMEM((length, D), BF),
            pltpu.VMEM((OWN_HEADS, length, 2 * HEAD_DIM), BF),
            pltpu.VMEM((MIX, length), BF),
            pltpu.VMEM((D, MIX), BF),
            pltpu.VMEM((length, TILE), F32),
            pltpu.VMEM((4, 16, MIX), BF),
            pltpu.SemaphoreType.DMA((9,)),
            pltpu.SemaphoreType.DMA((4,)),
        ],
        3 * 10**9,
        (x_all, *pieces),
        [ANYWHERE] * 3 + [WHOLE] * 3 + [ANYWHERE, WHOLE],
    )


def parcel_kernel(cot_ref, wout_ref, wup_ref, x_on_ref, x_ref, y_on_ref, y_ref, sems):
    place = lax.axis_index("wshard")

    def columns(k, first, count):
        at = pl.multiple_of(jnp.bitwise_xor(place, k) * D, D)
        return wup_ref.at[pl.ds(first, count), pl.ds(at, D)]

    low, high = cot_ref.at[pl.ds(0, MIDDLE_ROW)], cot_ref.at[pl.ds(MIDDLE_ROW, 32)]
    pairs = (
        (low, x_on_ref.at[pl.ds(0, MIDDLE_ROW)]),
        (columns(3, 0, PART), x_on_ref.at[pl.ds(MIDDLE_ROW, PART)]),
        (high, y_on_ref.at[pl.ds(0, 32)]),
        (wout_ref, y_on_ref.at[pl.ds(32, SHARD)]),
        (columns(3, PART, PART), y_on_ref.at[pl.ds(MIDDLE_ROW, PART)]),
        (columns(1, 0, SHARD), x_ref.at[pl.ds(0, SHARD)]),
        (high, x_ref.at[pl.ds(SHARD, 32)]),
        (wout_ref, x_ref.at[pl.ds(SHARD + 32, SHARD)]),
        (columns(2, 0, SHARD), y_ref.at[pl.ds(0, SHARD)]),
        (low, y_ref.at[pl.ds(SHARD, MIDDLE_ROW)]),
    )
    run_copies(pairs, sems)


def parcels(cot, w_out, w_up):
    on, rest = MIDDLE_ROW + PART, SHARD + MIDDLE_ROW
    return call(
        parcel_kernel,
        "parcels",
        [ANYWHERE] * 3,
        [((on, D), BF), ((rest, D), BF)] * 2,
        [pltpu.SemaphoreType.DMA((10,))],
        10**6,
        (cot, w_out, w_up),
    )


def assemble_kernel(cot_ref, own_ref, wup_ref, x_on, x_rest, y_on, y_rest, corner_a, corner_b,
                    wout_ref, up_ref, cots_ref, sems):
    place = lax.axis_index("wshard")
    at = [pl.multiple_of(jnp.bitwise_xor(place, k) * SHARD, SHARD) for k in range(4)]
    half = PART
    mine = pl.multiple_of(place * D, D)
    pairs = (
        (own_ref, wout_ref.at[pl.ds(at[0], SHARD)]),
        (x_rest.at[pl.ds(SHARD + 32, SHARD)], wout_ref.at[pl.ds(at[1], SHARD)]),
        (y_on.at[pl.ds(32, SHARD)], wout_ref.at[pl.ds(at[2], SHARD)]),
        (corner_b.at[pl.ds(32, SHARD)], wout_ref.at[pl.ds(at[3], SHARD)]),
        (wup_ref.at[:, pl.ds(mine, D)], up_ref.at[pl.ds(at[0], SHARD)]),
        (x_rest.at[pl.ds(0, SHARD)], up_ref.at[pl.ds(at[1], SHARD)]),
        (y_rest.at[pl.ds(0, SHARD)], up_ref.at[pl.ds(at[2], SHARD)]),
        (corner_a.at[pl.ds(MIDDLE_ROW, half)], up_ref.at[pl.ds(at[3], half)]),
        (corner_b.at[pl.ds(MIDDLE_ROW, half)], up_ref.at[pl.ds(at[3] + half, half)]),
        (cot_ref, cots_ref.at[pl.ds(0, TILE)]),
        (x_on.at[pl.ds(0, MIDDLE_ROW)], cots_ref.at[pl.ds(TILE, MIDDLE_ROW)]),
        (x_rest.at[pl.ds(SHARD, 32)], cots_ref.at[pl.ds(TILE + MIDDLE_ROW, 32)]),
        (y_rest.at[pl.ds(SHARD, MIDDLE_ROW)], cots_ref.at[pl.ds(2 * TILE, MIDDLE_ROW)]),
        (y_on.at[pl.ds(0, 32)], cots_ref.at[pl.ds(2 * TILE + MIDDLE_ROW, 32)]),
        (corner_a.at[pl.ds(0, MIDDLE_ROW)], cots_ref.at[pl.ds(3 * TILE, MIDDLE_ROW)]),
        (corner_b.at[pl.ds(0, 32)], cots_ref.at[pl.ds(3 * TILE + MIDDLE_ROW, 32)]),
    )
    run_copies(pairs, sems)


def assemble(cot, w_out, w_up, shared):
    return call(
        assemble_kernel,
        "assemble",
        [ANYWHERE] * 9,
        [((D, D), BF), ((D, D), BF), ((4 * TILE, D), BF)],
        [pltpu.SemaphoreType.DMA((16,))],
        10**6,
        (cot, w_out, w_up, *shared),
    )


def project_kernel(att_ref, x_ref, gain_ref, wout_ref, hidden_ref, normed_ref):
    hidden = x_ref[...].astype(F32) + nn(att_ref[...].T, wout_ref[...])
    hidden_ref[...] = hidden
    xhat, _ = normalised(hidden)
    normed_ref[...] = (xhat * gain_ref[1:2]).astype(BF)


def project(att_home, x_block, gain, w_out):
    rows = x_block.shape[0]
    return call(
        project_kernel,
        "project",
        [WHOLE] * 4,
        [((rows, D), F32), ((rows, D), BF)],
        [],
        3 * 10**8,
        (att_home, x_block, gain, w_out),
    )


SLOPE = (2.0 / 3.141592653589793) ** 0.5


def feed_rows(n, cot, up_ref, down_ref, active_ref, dup_ref, here):
    for first in range(0, D, TILE):
        cols = slice(first, first + TILE)
        u = nn(n, up_ref[:, cols])
        square = u * u
        t = jnp.tanh(SLOPE * (u + 0.044715 * (square * u)))
        side = 0.5 + 0.5 * t
        active_ref[here, cols] = (u * side).astype(BF)
        grad = side + (0.5 * SLOPE) * u * (1.0 - t * t) * (1.0 + 0.134145 * square)
        dup_ref[here, cols] = (grad * nt(cot, down_ref[cols, :])).astype(BF)
    return nn(active_ref[here, :], down_ref[...]), nt(dup_ref[here, :], up_ref[...])


def feed_own_kernel(n_ref, cot_ref, up_ref, down_ref, active_ref, dup_ref, out_ref, dout_ref):
    out_ref[...], dout_ref[...] = feed_rows(
        n_ref[...], cot_ref[0:TILE, :], up_ref, down_ref, active_ref, dup_ref, slice(0, TILE)
    )


def feed_own(n, cots, up, down):
    return call(
        feed_own_kernel,
        "feed_own",
        [WHOLE] * 4,
        [((TILE, D), BF), ((TILE, D), BF), ((TILE, D), F32), ((TILE, D), F32)],
        [],
        2 * 10**9,
        (n, cots, up, down),
    )


def feed_near_kernel(nx_ref, ny_ref, cot_ref, up_ref, down_ref, active_ref, dup_ref, out_ref, dout_ref):
    for k, n_ref in enumerate((nx_ref, ny_ref)):
        here = slice(k * TILE, (k + 1) * TILE)
        out, dout = feed_rows(n_ref[...], cot_ref[(k + 1) * TILE : (k + 2) * TILE, :], up_ref, down_ref, active_ref, dup_ref, here)
        out_ref[here, :], dout_ref[here, :] = out.astype(BF), dout.astype(BF)


def feed_near(nx, ny, cots, up, down):
    return call(
        feed_near_kernel,
        "feed_near",
        [WHOLE] * 5,
        [((2 * TILE, D), BF)] * 4,
        [],
        4 * 10**9,
        (nx, ny, cots, up, down),
    )


def feed_far_kernel(na_ref, nb_ref, cot_ref, out_ref, dout_ref, up_ref, down_ref,
                    active_ref, dup_ref, oa_ref, oaf_ref, ob_ref, obf_ref, da_ref, daf_ref, db_ref, dbf_ref):
    n = jnp.concatenate([na_ref[...], nb_ref[...]])
    cot = cot_ref[3 * TILE :, :]
    half = TILE // 2
    out, dout = feed_rows(n, cot, up_ref, down_ref, active_ref, dup_ref, slice(0, TILE))
    for far, near, a, af, b, bf in (
        (out, out_ref, oa_ref, oaf_ref, ob_ref, obf_ref),
        (dout, dout_ref, da_ref, daf_ref, db_ref, dbf_ref),
    ):
        far = far.astype(BF)
        a[0], a[1] = near[0:half, :], far[0:half]
        b[0], b[1] = near[TILE + half :, :], far[half:]
        af[...] = near[TILE : TILE + half, :]
        bf[...] = near[half:TILE, :]


def feed_far(na, nb, cots, out, dout, up, down):
    half = TILE // 2
    return call(
        feed_far_kernel,
        "feed_far",
        [WHOLE] * 7,
        [((TILE, D), BF)] * 2 + [((2, half, D), BF), ((half, D), BF)] * 4,
        [],
        2 * 10**9,
        (na, nb, cots, out, dout, up, down),
    )


def feed_grads_kernel(n0, n1, n2, n3, n4, cot_ref, a0, a1, a2, d0, d1, d2,
                      shares_ref, nt_ref, at_ref, dup_ref):
    for k, piece in enumerate((n0, n1, n2)):
        nt_ref[:, k * TILE : (k + 1) * TILE] = piece[...].T
    nt_ref[:, 3 * TILE :] = jnp.concatenate([n3[...], n4[...]]).T
    at_ref[:, 0:TILE] = a0[...].T
    at_ref[:, TILE : 3 * TILE] = a1[...].T
    at_ref[:, 3 * TILE :] = a2[...].T
    dup_ref[0:TILE] = d0[...]
    dup_ref[TILE : 3 * TILE] = d1[...]
    dup_ref[3 * TILE :] = d2[...]
    rows = D // 8
    for k in range(8):
        g = nn(at_ref[k * rows : (k + 1) * rows, :], cot_ref[...]).astype(BF)
        for side in range(2):
            for part in range(2):
                piece = g[part * QUART : (part + 1) * QUART, side * HALF : (side + 1) * HALF]
                shares_ref[k, 4 + 2 * side + part] = piece
    for to in range(4):
        g = nn(nt_ref[to * SHARD : (to + 1) * SHARD, :], dup_ref[...]).astype(BF)
        slot = jnp.bitwise_xor(lax.axis_index("wshard"), to)
        for k in range(8):
            r, c = (k // 2) * QUART, (k % 2) * HALF
            shares_ref[k, slot] = g[r : r + QUART, c : c + HALF]


def feed_grads(ns, cots, actives, dups):
    length = 4 * TILE
    return call(
        feed_grads_kernel,
        "feed_grads",
        [WHOLE] * 12,
        [((8, 8, QUART, HALF), BF)],
        [
            pltpu.VMEM((D, length), BF),
            pltpu.VMEM((D, length), BF),
            pltpu.VMEM((length, D), BF),
        ],
        3 * 10**9,
        (*ns, cots, *actives, *dups),
    )[0]


def summed(keep_ref, a_ref, a_more_ref, b_ref, b_more_ref):
    first = a_ref[0].astype(F32) + a_more_ref[...].astype(F32)
    second = b_ref[0].astype(F32) + b_more_ref[...].astype(F32)
    return keep_ref[...] + jnp.concatenate([first, second])


def give_kernel(hidden_ref, keep_ref, a_ref, a_more_ref, b_ref, b_more_ref, rkeep_ref, rsend_ref, result_ref, sems):
    core = lax.axis_index("ctx") % 2
    result = (hidden_ref[...] + summed(keep_ref, a_ref, a_more_ref, b_ref, b_more_ref)).astype(BF)
    half = TILE // 2
    result_ref[0], result_ref[1] = result[:half], result[half:]
    run_copies(((result_ref.at[1 - core], rsend_ref), (result_ref.at[core], rkeep_ref)), sems)


def give(hidden, keep, parts):
    half = TILE // 2
    return call(
        give_kernel,
        "give",
        [WHOLE] * 6,
        [((half, D), BF)] * 2,
        [pltpu.VMEM((2, half, D), BF), pltpu.SemaphoreType.DMA((2,))],
        10**6,
        (hidden, keep, *parts),
        [ANYWHERE] * 2,
    )


def turn_kernel(hidden_ref, gain_ref, dkeep_ref, a_ref, a_more_ref, b_ref, b_more_ref, cot_ref, wout_ref,
                dhidden_ref, datt_ref, dbranch_ref, dgain_ref):
    gain = gain_ref[1:2]
    xhat, inverse = normalised(hidden_ref[...])
    dy = summed(dkeep_ref, a_ref, a_more_ref, b_ref, b_more_ref)
    dgain_ref[...] = jnp.sum(dy * xhat, axis=0, keepdims=True)
    d_hidden = cot_ref[...].astype(F32) + norm_back(xhat, inverse, gain, dy)
    dhidden_ref[...] = d_hidden
    d_branch = d_hidden.astype(BF)
    dbranch_ref[...] = d_branch
    d_att = nt(wout_ref[...], d_branch).astype(BF)
    for k in range(4):
        datt_ref[k] = d_att[k * OWN : (k + 1) * OWN]


def turn(hidden, gain, dkeep, parts, cot, w_out):
    rows = hidden.shape[0]
    return call(
        turn_kernel,
        "turn",
        [WHOLE] * 9,
        [((rows, D), F32), ((4, OWN, rows), BF), ((rows, D), BF), ((1, D), F32)],
        [],
        6 * 10**8,
        (hidden, gain, dkeep, *parts, cot, w_out),
    )


def out_grad_kernel(att_ref, dbranch_ref, keep_ref, send_ref, grad_ref, sems):
    core = lax.axis_index("ctx") % 2
    place = lax.axis_index("wshard")
    for to in range(4):
        e = jnp.bitwise_xor(place, to)
        e_x, e_y = jnp.bitwise_and(e, 1), e // 2
        g = nn(att_ref[to * SHARD : (to + 1) * SHARD, :], dbranch_ref[...]).astype(BF)
        for side in range(2):
            for half in range(2):
                piece = g[side * PART : (side + 1) * PART, half * HALF : (half + 1) * HALF]
                grad_ref[side, e_y, e_x, half * PART : (half + 1) * PART] = piece
    rows = pl.ds(HEAD_ROWS, SHARD)
    pairs = ((grad_ref.at[1 - core], send_ref.at[:, :, rows]), (grad_ref.at[core], keep_ref.at[:, :, rows]))
    run_copies(pairs, sems)


def out_grad(att_home, d_branch):
    return call(
        out_grad_kernel,
        "out_grad",
        [WHOLE] * 2,
        [((2, 2, HEAD_ROWS + SHARD, HALF), BF)] * 2,
        [pltpu.VMEM((2, 2, 2, SHARD, HALF), BF), pltpu.SemaphoreType.DMA((2,))],
        3 * 10**8,
        (att_home, d_branch),
        [ANYWHERE] * 2,
    )


def attend_back_kernel(kv_ref, mixt_ref, att_ref, lse_ref, dout_ref, normed_in, w_in, gain_ref, dgain_ref, _, __,
                       f0_ref, f1_ref, f2_ref, f3_ref, gkeep_ref, gsend_ref,
                       dq_ref, dk_ref, dv_ref, dm_ref, mix_ref, total_ref, first_ref, head_ref, sems,
                       normed_ref, w_ref, in_sems):
    length = kv_ref.shape[1]
    loads = [
        pltpu.make_async_copy(normed_in, normed_ref, in_sems.at[0]),
        pltpu.make_async_copy(w_in, w_ref, in_sems.at[1]),
    ]
    for load in loads:
        load.start()
    scale = BF(HEAD_DIM**-0.5)
    core = lax.axis_index("ctx") % 2
    z = lax.axis_index("ctx") // 2
    place = lax.axis_index("wshard")

    @pl.loop(0, OWN_HEADS)
    def _(h):
        base = pl.multiple_of(h * HEAD_DIM, HEAD_DIM)
        for block in range(4):
            here = slice(block * TILE, (block + 1) * TILE)
            queries = mixt_ref[pl.ds(base, HEAD_DIM), here] * scale
            dout = dout_ref[block, pl.ds(base, HEAD_DIM), :]
            delta = jnp.sum(dout.astype(F32) * att_ref[pl.ds(base, HEAD_DIM), here], axis=0, keepdims=True)
            lse = lse_ref[pl.ds(h, 1), here]
            acc = jnp.zeros((HEAD_DIM, TILE), F32)
            for other in range(block + 1):
                there = slice(other * TILE, (other + 1) * TILE)
                s = nn(kv_ref[h, there, 0:HEAD_DIM], queries)
                ds = nn(kv_ref[h, there, HEAD_DIM:], dout)
                square = s * s + 1.0
                r = lax.rsqrt(square)
                chance = jnp.exp(square * r - lse)
                if other == block:
                    chance = jnp.where(causal_tile(), chance, 0.0)
                tilted = s * r
                signed = (tilted * chance).astype(BF)
                slope = r * r * r + tilted * tilted
                dsc = (chance * (ds * slope - tilted * delta)).astype(BF)
                acc = acc + nn(mixt_ref[pl.ds(OWN + base, HEAD_DIM), there], dsc)
                dk = nt(dsc, queries)
                dv = nt(signed, dout)
                if other == block:
                    dk_ref[there, :] = dk
                    dv_ref[there, :] = dv
                else:
                    dk_ref[there, :] += dk
                    dv_ref[there, :] += dv
            dq_ref[:, here] = acc * HEAD_DIM**-0.5
        dm_ref[h, :, 0:HEAD_DIM] = dq_ref[...].T.astype(BF)
        dm_ref[h, :, HEAD_DIM : 2 * HEAD_DIM] = dk_ref[...].astype(BF)
        dm_ref[h, :, 2 * HEAD_DIM :] = dv_ref[...].astype(BF)

    for h in range(OWN_HEADS):
        for kind in range(3):
            to = kind * OWN + h * HEAD_DIM
            mix_ref[:, to : to + HEAD_DIM] = dm_ref[h, :, kind * HEAD_DIM : (kind + 1) * HEAD_DIM]
    total_ref[...] = jnp.zeros_like(total_ref)
    for load in loads:
        load.wait()
    for block in range(4):
        here = slice(block * TILE, (block + 1) * TILE)
        first = nt(mix_ref[here, :], w_ref[...])
        first_ref[block] = first.astype(BF)
        total_ref[...] += jnp.sum(first * normed_ref[here, :].astype(F32), axis=0, keepdims=True)
    outs = (f3_ref, f2_ref, f1_ref, f0_ref)
    copies = [
        pltpu.make_async_copy(first_ref.at[jnp.bitwise_xor(z, 3 - k)], ref, sems.at[k]) for k, ref in enumerate(outs)
    ]
    for copy in copies:
        copy.start()
    gain_one = total_ref[...] / gain_ref[0:1]
    gain_two = dgain_ref[...]
    for to in range(4):
        e = jnp.bitwise_xor(place, to)
        e_x, e_y = jnp.bitwise_and(e, 1), e // 2
        g = nn(normed_ref[:, to * SHARD : (to + 1) * SHARD].T, mix_ref[...]).astype(BF)
        span = slice(to * SHARD, (to + 1) * SHARD)
        gains = jnp.concatenate([gain_one[:, span], gain_two[:, span], jnp.zeros((14, SHARD), F32)], axis=0)
        gains = jnp.concatenate([gains, jnp.zeros((16, HALF - SHARD), F32)], axis=1).astype(BF)
        for side in range(2):
            at = side * PART
            head_ref[side, e_y, e_x, 0:PART] = g[at : at + PART, 0:HALF]
            head_ref[side, e_y, e_x, PART : PART + QUART, 0:OWN] = g[at : at + QUART, HALF:]
            head_ref[side, e_y, e_x, PART : PART + QUART, OWN:] = g[at + QUART : at + PART, HALF:]
            head_ref[side, e_y, e_x, PART + QUART :] = gains if side == 0 else jnp.zeros_like(gains)
    more = [
        pltpu.make_async_copy(head_ref.at[1 - core], gsend_ref.at[:, :, pl.ds(0, HEAD_ROWS)], sems.at[4]),
        pltpu.make_async_copy(head_ref.at[core], gkeep_ref.at[:, :, pl.ds(0, HEAD_ROWS)], sems.at[5]),
    ]
    for copy in more:
        copy.start()
    for copy in copies + more:
        copy.wait()


def attend_back(kv, mixt, att, lse, dout, normed, w, gain, dgain, keep, send):
    length = normed.shape[0]
    return pl.pallas_call(
        attend_back_kernel,
        in_specs=[WHOLE] * 5 + [ANYWHERE] * 2 + [WHOLE] * 2 + [ANYWHERE] * 2,
        out_specs=[ANYWHERE] * 6,
        out_shape=[jax.ShapeDtypeStruct((TILE, D), BF)] * 4 + [jax.ShapeDtypeStruct(keep.shape, BF)] * 2,
        input_output_aliases={9: 4, 10: 5},
        scratch_shapes=[
            pltpu.VMEM((HEAD_DIM, length), F32),
            pltpu.VMEM((length, HEAD_DIM), F32),
            pltpu.VMEM((length, HEAD_DIM), F32),
            pltpu.VMEM((OWN_HEADS, length, 3 * HEAD_DIM), BF),
            pltpu.VMEM((length, MIX), BF),
            pltpu.VMEM((1, D), F32),
            pltpu.VMEM((4, TILE, D), BF),
            pltpu.VMEM((2, 2, 2, HEAD_ROWS, HALF), BF),
            pltpu.SemaphoreType.DMA((6,)),
            pltpu.VMEM((length, D), BF),
            pltpu.VMEM((D, MIX), BF),
            pltpu.SemaphoreType.DMA((2,)),
        ],
        compiler_params=pltpu.CompilerParams(vmem_limit_bytes=VMEM_LIMIT),
        cost_estimate=pl.CostEstimate(flops=1000, bytes_accessed=1000, transcendentals=0),
        name="attend_back",
    )(kv, mixt, att, lse, dout, normed, w, gain, dgain, keep, send)


def is_inner():
    z = lax.axis_index("ctx") // 2
    return (z == 1) | (z == 2)


def last_kernel(first_ref, pair_ref, middle_ref, x_ref, gain_ref, dhidden_ref, keep_ref, send_ref, grad_ref, sems):
    core = lax.axis_index("ctx") % 2
    rows = x_ref.shape[0] // 2
    dy = first_ref[...].astype(F32) + pair_ref[...].astype(F32)
    dy = dy + jnp.where(is_inner(), middle_ref[...].astype(F32), 0.0)
    xhat, inverse = normalised(x_ref[...].astype(F32))
    grad = dhidden_ref[...] + norm_back(xhat, inverse, gain_ref[0:1], dy)
    grad_ref[0], grad_ref[1] = grad[:rows], grad[rows:]
    run_copies(((grad_ref.at[1 - core], send_ref), (grad_ref.at[core], keep_ref)), sems)


def last(*args):
    rows = TILE // 2
    return call(
        last_kernel,
        "last",
        [WHOLE] * 6,
        [((rows, D), F32), ((rows, D), F32)],
        [pltpu.VMEM((2, rows, D), F32), pltpu.SemaphoreType.DMA((2,))],
        10**7,
        args,
        [ANYWHERE] * 2,
    )


def line_slots():
    z = lax.axis_index("ctx") // 2
    return z, jnp.bitwise_xor(z, 1), jnp.where(z < 2, 2, 1), jnp.where(z < 2, 3, 0)


def finish_feed_kernel(*refs):
    mine, theirs, (gup_ref, gdown_ref) = refs[:4], refs[4:8], refs[8:]
    core = lax.axis_index("ctx") % 2
    place = lax.axis_index("wshard")
    rows = D // 8
    for group, side in ((mine, core), (theirs, 1 - core)):
        for ref, slot in zip(group, line_slots()):
            at = pl.multiple_of(slot * QUART, 16)
            for k in range(4):
                to = pl.multiple_of(jnp.bitwise_xor(place, k) * D + side * HALF, 128)
                gup_ref[pl.ds(at, QUART), pl.ds(to, HALF)] = ref[k * QUART : (k + 1) * QUART].astype(F32)
            at = pl.multiple_of((2 * slot + side) * rows, 32)
            for half in range(2):
                share = ref[SHARD + half * rows : SHARD + (half + 1) * rows]
                gdown_ref[pl.ds(at, rows), half * HALF : (half + 1) * HALF] = share.astype(F32)


def finish_feed(*args):
    return call(
        finish_feed_kernel, "finish_feed", [WHOLE] * 8, [((SHARD, 4 * D), F32), ((D, D), F32)], [], 10**7, args
    )


def finish_heads_kernel(*refs):
    mine, theirs, outs, (gout_ref, gqkv_ref, one_ref, two_ref) = refs[:4], refs[4:8], refs[8:10], refs[10:]
    slots = line_slots()
    first = lax.axis_index("ctx") % 2 == 0
    out, other_out = [ref[...].astype(F32) for ref in outs]
    for half in range(2):
        here, cols = slice(half * PART, (half + 1) * PART), slice(half * HALF, (half + 1) * HALF)
        gout_ref[0:PART, cols] = jnp.where(first, out[here], other_out[here])
        gout_ref[PART:, cols] = jnp.where(first, other_out[here], out[here])
    mine, theirs = [[ref[...].astype(F32) for ref in group] for group in (mine, theirs)]
    low = [jnp.where(first, a, b) for a, b in zip(mine, theirs)]
    high = [jnp.where(first, b, a) for a, b in zip(mine, theirs)]
    gains = sum(block[PART + QUART :, 0:SHARD] for block in low)
    one_ref[...], two_ref[...] = gains[0], gains[1]
    for slot in range(4):
        for side, group in enumerate((low, high)):
            block = jnp.where(
                slot == slots[0],
                group[0],
                jnp.where(slot == slots[1], group[1], jnp.where(slot == slots[2], group[2], group[3])),
            )
            at, to = side * PART, slot * OWN
            gqkv_ref[at : at + PART, to : to + OWN] = block[0:PART, 0:OWN]
            gqkv_ref[at : at + PART, D + to : D + to + OWN] = block[0:PART, OWN:]
            gqkv_ref[at : at + QUART, 2 * D + to : 2 * D + to + OWN] = block[PART : PART + QUART, 0:OWN]
            gqkv_ref[at + QUART : at + PART, 2 * D + to : 2 * D + to + OWN] = block[PART : PART + QUART, OWN:]


def finish_heads(*args):
    return call(
        finish_heads_kernel,
        "finish_heads",
        [WHOLE] * 10,
        [((SHARD, D), F32), ((SHARD, 3 * D), F32), ((SHARD,), F32), ((SHARD,), F32)],
        [],
        10**7,
        args,
    )


def pick(value, index, axis=0):
    return lax.dynamic_index_in_dim(value, index, axis, keepdims=False)


def across_w(value, flip):
    return lax.ppermute(value, "wshard", [(i, i ^ flip) for i in range(4)])


def across_core(value):
    return lax.ppermute(value, "ctx", [(i, i ^ 1) for i in range(8)])


def between_z(value, pairs):
    return lax.ppermute(value, "ctx", [(2 * a + c, 2 * b + c) for a, b in pairs for c in range(2)])


Z_GROUPS = [[0, 2, 4, 6], [1, 3, 5, 7]]


def after(value, *others):
    return lax.optimization_barrier((value, *others))[0]


PAIRS = [(0, 1), (1, 0), (2, 3), (3, 2)]
MIDDLE = [(1, 2), (2, 1), (0, 0), (3, 3)]


def line_z(block):
    pair = between_z(block, PAIRS)
    mid_near = between_z(block, MIDDLE)
    near = between_z(mid_near, PAIRS)
    mid_far = between_z(pair, MIDDLE)
    far = between_z(mid_far, PAIRS)
    return block, pair, near, far, mid_near, mid_far


TO_MIDDLE = [(0, 1), (3, 2)]
TO_ENDS = [(1, 0), (2, 3)]
ACROSS = [(1, 2), (2, 1)]


def own_slot(slots, x_first):
    one, two = (1, 2) if x_first else (2, 1)
    got = across_w(slots[1], one)
    far = slots[0, 1] + got[1]
    return (slots[0, 0] + got[0]) + across_w(far, two)


def gather_plane(block, *others):
    half = block.shape[0] // 2
    from_x, from_y = across_w(block, 1), across_w(block, 2)
    first, second = from_x[:half], from_y[half:]
    if others:
        first, second, *_ = tied(first, second, *others)
    return block, from_x, from_y, across_w(first, 2), across_w(second, 1)


def tied(*values):
    return lax.optimization_barrier(values)


def local_grid(tokens, gain_one, w_qkv, w_out, gain_two, w_up, w_down, cotangent):
    core = lax.axis_index("ctx") % 2
    z = lax.axis_index("ctx") // 2
    place = lax.axis_index("wshard")
    inner = (z == 1) | (z == 2)

    def both_micros(kept, got):
        return jnp.where(core == 0, jnp.stack([kept, got]), jnp.stack([got, kept]))[:, None]

    tok, cot = tokens[:, 0], cotangent[:, 0]
    kept = jnp.concatenate([pick(tok, core), pick(cot, core)])
    got = across_core(jnp.concatenate([pick(tok, 1 - core), pick(cot, 1 - core)]))
    half = TILE // 2
    own = [jnp.where(core == 0, a, b) for a, b in ((kept, got), (got, kept))]
    x_block = jnp.concatenate([own[0][:half], own[1][:half]])
    cot = jnp.concatenate([own[0][half:], own[1][half:]])

    w_heads = pick(w_qkv.reshape(SHARD, 3, 4, OWN), z, 2).reshape(SHARD, MIX)
    gains = jnp.pad(jnp.stack([gain_one, gain_two]), ((0, 30), (0, MIX - SHARD)))
    x_all = lax.all_to_all(
        jnp.broadcast_to(x_block, (4,) + x_block.shape), "ctx", 0, 0, tiled=True, axis_index_groups=Z_GROUPS
    )
    x_on, x_rest, y_on, y_rest = parcels(cot, w_out, w_up)
    x_on, y_on = across_w(x_on, 1), across_w(y_on, 2)
    x_on, y_on, w_heads = tied(x_on, y_on, jnp.concatenate([w_heads, gains]))
    heads = gather_plane(w_heads)
    x_rest, y_rest, x_on, y_on, *heads = tied(x_rest, y_rest, x_on, y_on, *heads)
    corner_a, corner_b = across_w(x_on, 2), across_w(y_on, 1)
    x_rest, y_rest = across_w(x_rest, 1), across_w(y_rest, 2)
    normed_all, kv, mixt, att, att_low, lse, w_full, gains = attend(x_all, heads)
    att_low, corner_a, corner_b = tied(att_low, corner_a, corner_b)
    shared = x_on, x_rest, y_on, y_rest, corner_a, corner_b
    att_home = lax.all_to_all(att_low, "ctx", 0, 0, tiled=True, axis_index_groups=Z_GROUPS).reshape(D, -1)
    wout_full, up, cots = assemble(cot, w_out, w_up, shared)
    hidden, normed_two = project(att_home, x_block, gains, wout_full)

    active0, dup0, out0, dout0 = feed_own(normed_two, cots, up, w_down)
    ns = gather_plane(normed_two, active0)
    active1, dup1, out1, dout1 = feed_near(ns[1], ns[2], cots, up, w_down)
    active2, dup2, *parts = feed_far(ns[3], ns[4], cots, out1, dout1, up, w_down)
    parts, (a, a_far, b, b_far) = parts[:4], parts[4:]
    got_a, got_b = across_w(a, 1), across_w(b, 2)
    shares = feed_grads(ns, cots, (active0, active1, active2), (dup0, dup1, dup2))
    shares, got_a, got_b = tied(shares, got_a, got_b)
    shares = lax.psum_scatter(shares, "ctx", scatter_dimension=0)
    more_a, more_b = across_w(a_far + got_a[1], 2), across_w(b_far + got_b[1], 1)
    d_hidden, d_att, d_branch, d_gain_two = turn(
        hidden, gains, dout0, (got_a, more_a, got_b, more_b), cot, wout_full
    )
    d_out = lax.all_to_all(d_att, "ctx", 0, 0, tiled=True, axis_index_groups=Z_GROUPS)
    keep, send = out_grad(att_home, d_branch)
    d_out, keep, send = tied(d_out, keep, send)
    a, a_far, b, b_far = parts
    got_a, got_b = across_w(a, 1), across_w(b, 2)
    *firsts, keep, send = attend_back(
        kv, mixt, att, lse, d_out, normed_all, w_full, gains, d_gain_two, keep, send
    )
    *firsts, keep, send, shares, got_a, got_b = tied(*firsts, keep, send, shares, got_a, got_b)

    got = between_z(firsts[3], TO_MIDDLE)
    both = firsts[2] + jnp.where(inner, got, BF(0))
    outer, middle = between_z(both, TO_MIDDLE), between_z(both, ACROSS)
    pair = between_z(firsts[1] + jnp.where(inner, middle, BF(0)), PAIRS)
    middle = between_z(firsts[3] + outer, ACROSS)

    ups = [shares[0]] + [across_w(shares[e], e) for e in (1, 2, 3)]
    share = jnp.concatenate(ups + [shares[4:].reshape(SHARD, HALF)])
    share_pair, share_mid = between_z(share, PAIRS), between_z(share, ACROSS)
    share_near, share_mid_far = between_z(share_mid, TO_ENDS), between_z(share_pair, ACROSS)
    share_far = between_z(share_mid_far, TO_ENDS)
    blocks = share, share_pair, jnp.where(inner, share_mid, share_near), jnp.where(inner, share_mid_far, share_far)
    grad_up, grad_down = finish_feed(*blocks, *(across_core(block) for block in blocks))

    sums, a_far, b_far = tied(keep + across_core(send), a_far, b_far)
    sums_got = across_w(sums[1], 2)
    sums_far = across_w(sums[0, 1] + sums_got[1], 1)
    sums, a_far, b_far = tied((sums[0, 0] + sums_got[0]) + sums_far, a_far, b_far)
    more_a, more_b = across_w(a_far + got_a[1], 2), across_w(b_far + got_b[1], 1)
    result_keep, result_send = give(hidden, out0, (got_a, more_a, got_b, more_b))
    out_result = both_micros(result_keep, across_core(result_send))
    sums_pair, head_mid = between_z(sums, PAIRS), between_z(sums[:HEAD_ROWS], ACROSS)
    out = sums[HEAD_ROWS:] + sums_pair[HEAD_ROWS:]
    head_near = between_z(head_mid, TO_ENDS)
    sums_far = between_z(jnp.concatenate([sums_pair[:HEAD_ROWS], out]), ACROSS)
    pair, middle, out_result, sums_far, head_near = tied(pair, middle, out_result, sums_far, head_near)
    sums_far = jnp.concatenate([sums_far[:HEAD_ROWS], out + sums_far[HEAD_ROWS:]])
    sums_last = between_z(sums_far, TO_ENDS)
    grad_keep, grad_send = last(firsts[0], pair, middle, x_block, gains, d_hidden)
    out_tokens = both_micros(grad_keep, across_core(grad_send))
    sums_last = jnp.where(inner, sums_far, sums_last)
    head_near = jnp.where(inner, head_mid, head_near)
    blocks = sums[:HEAD_ROWS], sums_pair[:HEAD_ROWS], head_near, sums_last[:HEAD_ROWS]
    others = [across_core(block) for block in (*blocks[:3], sums_last)]
    grad_out, grad_qkv, gain_one, gain_two = finish_heads(
        *blocks, *others[:3], others[3][:HEAD_ROWS], sums_last[HEAD_ROWS:], others[3][HEAD_ROWS:]
    )
    return (
        out_result,
        out_tokens,
        gain_one,
        grad_qkv,
        grad_out,
        gain_two,
        grad_up,
        grad_down,
    )


def local(tokens, *rest):
    fits = (
        lax.axis_size("wshard") == 4
        and lax.axis_size("ctx") == 8
        and tokens.shape[:2] == (2, 1)
        and 2 * tokens.shape[2] == TILE
    )
    return (local_grid if fits else local_any)(tokens, *rest)


def solution(mesh):
    placed = (
        P(None, "wshard", "ctx", None),
        P("wshard"),
        P("wshard", None),
        P("wshard", None),
        P("wshard"),
        P("wshard", None),
        P("wshard", None),
        P(None, "wshard", "ctx", None),
    )
    return jax.shard_map(
        local,
        mesh=mesh,
        in_specs=placed,
        out_specs=(
            P(None, "wshard", "ctx", None),
            P(None, "wshard", "ctx", None),
            P("wshard"),
            P("wshard", None),
            P("wshard", None),
            P("wshard"),
            P("wshard", None),
            P("wshard", None),
        ),
        check_vma=False,
    )
```

```python
import jax
import jax.numpy as jnp
from jax import lax
from jax.experimental import pallas as pl
from jax.experimental.pallas import tpu as pltpu
from jax.sharding import PartitionSpec as P

D = 768
HEADS = 12
HEAD_DIM = 64


EPSILON = 1e-05


def passed_along(value, axis, by):
    count = lax.axis_size(axis)
    return lax.ppermute(value, axis, [(i, (i + by) % count) for i in range(count)])


def layer_norm(inputs, scaling):
    centred = inputs - jnp.mean(inputs, axis=-1, keepdims=True)
    variance = jnp.mean(centred * centred, axis=-1, keepdims=True)
    return centred * lax.rsqrt(variance + EPSILON) * scaling


def gelu_smooth(values_in):
    return jax.nn.gelu(values_in, approximate=True)


def contract_rows(left_side, right_side):
    return lax.dot_general(
        left_side, right_side, (((0,), (0,)), ((), ())), preferred_element_type=jnp.float32
    )


def times_rows(left_side, right_side):
    return lax.dot_general(
        left_side, right_side, (((1,), (1,)), ((), ())), preferred_element_type=jnp.float32
    )


def pair_grads(query_h, dout_h, log_total, row_delta, query_pos, key_h, value_h, key_pos):
    scaling = HEAD_DIM ** (-0.5)
    scores = (
        jnp.einsum("qhe,khe->hqk", query_h, key_h, preferred_element_type=jnp.float32) * scaling
    )
    visible = key_pos[None, None, :] <= query_pos[None, :, None]
    magnitude = jnp.sqrt(scores * scores + 1.0)
    tilted = scores / magnitude
    chance = jnp.exp(jnp.where(visible, magnitude - log_total[:, :, None], -1e30))
    signed = (tilted * chance).astype(jnp.bfloat16)
    d_signed = jnp.einsum("qhe,khe->hqk", dout_h, value_h, preferred_element_type=jnp.float32)
    slope = 1.0 / (magnitude * magnitude * magnitude) + tilted * tilted
    d_scores = (chance * (d_signed * slope - tilted * row_delta[:, :, None])).astype(jnp.bfloat16)
    d_query = (
        jnp.einsum("hqk,khe->qhe", d_scores, key_h, preferred_element_type=jnp.float32) * scaling
    )
    d_key = (
        jnp.einsum("hqk,qhe->khe", d_scores, query_h, preferred_element_type=jnp.float32) * scaling
    )
    d_value = jnp.einsum("hqk,qhe->khe", signed, dout_h, preferred_element_type=jnp.float32)
    return (d_query, d_key, d_value)


def keep_state(loop_state):
    return loop_state


def local_any(tokens, gain_one, w_qkv, w_out, gain_two, w_up, w_down, cotangent):
    gathered = (
        lax.all_gather(gain_one, "wshard", axis=0, tiled=True),
        lax.all_gather(w_qkv, "wshard", axis=0, tiled=True),
        lax.all_gather(w_out, "wshard", axis=0, tiled=True),
        lax.all_gather(gain_two, "wshard", axis=0, tiled=True),
        lax.all_gather(w_up, "wshard", axis=0, tiled=True),
        lax.all_gather(w_down, "wshard", axis=0, tiled=True),
    )
    full_gain_one, full_qkv, full_out, full_gain_two, full_up, full_down = gathered
    gain_first = full_gain_one.astype(jnp.float32)
    gain_second = full_gain_two.astype(jnp.float32)
    cycle_size = lax.axis_size("ctx")
    cycle_place = lax.axis_index("ctx")
    micro_count = tokens.shape[0]
    local_len = tokens.shape[2]
    scaling = HEAD_DIM ** (-0.5)
    query_pos = cycle_place * local_len + jnp.arange(local_len, dtype=jnp.int32)
    sum_gain_one = jnp.zeros((D,), jnp.float32)
    sum_gain_two = jnp.zeros((D,), jnp.float32)
    sum_qkv = jnp.zeros(full_qkv.shape, jnp.float32)
    sum_out = jnp.zeros(full_out.shape, jnp.float32)
    sum_up = jnp.zeros(full_up.shape, jnp.float32)
    sum_down = jnp.zeros(full_down.shape, jnp.float32)
    results = []
    grad_list = []
    for micro_index in range(micro_count):
        inputs = tokens[micro_index, 0].astype(jnp.float32)
        normed_f, norm_back = jax.vjp(layer_norm, inputs, gain_first)
        normed = normed_f.astype(jnp.bfloat16)
        mixed_all = jnp.dot(normed, full_qkv, preferred_element_type=jnp.float32).astype(
            jnp.bfloat16
        )
        keys_flat = mixed_all[:, D : 2 * D]
        values_flat = mixed_all[:, 2 * D :]
        query_h = mixed_all[:, :D].reshape(local_len, HEADS, HEAD_DIM)
        key_h = keys_flat.reshape(local_len, HEADS, HEAD_DIM)
        value_h = values_flat.reshape(local_len, HEADS, HEAD_DIM)
        start_state = (
            jnp.zeros((HEADS, local_len, HEAD_DIM), jnp.float32),
            jnp.ones((HEADS, local_len), jnp.float32),
            jnp.zeros((HEADS, local_len), jnp.float32),
        )
        shard_piece = (
            lax.all_gather(keys_flat, "ctx", axis=0, tiled=True),
            lax.all_gather(values_flat, "ctx", axis=0, tiled=True),
        )

        def compute(loop_state):
            accumulated, top_value, totals = loop_state
            key_piece = shard_piece[0].reshape(-1, HEADS, HEAD_DIM)
            value_piece = shard_piece[1].reshape(-1, HEADS, HEAD_DIM)
            key_pos = jnp.arange(key_piece.shape[0], dtype=jnp.int32)
            scores = (
                jnp.einsum("qhe,khe->hqk", query_h, key_piece, preferred_element_type=jnp.float32)
                * scaling
            )
            visible = key_pos[None, None, :] <= query_pos[None, :, None]
            magnitude = jnp.sqrt(scores * scores + 1.0)
            new_top = jnp.maximum(top_value, jnp.max(jnp.where(visible, magnitude, 0.0), axis=-1))
            weighted = jnp.exp(jnp.where(visible, magnitude - new_top[:, :, None], -1e30))
            signed = (scores / magnitude * weighted).astype(jnp.bfloat16)
            accumulated = jnp.einsum(
                "hqk,khe->hqe", signed, value_piece, preferred_element_type=jnp.float32
            )
            totals = jnp.sum(weighted, axis=-1)
            return (accumulated, new_top, totals)

        accumulated, top_value, totals = lax.cond(
            jnp.int32(0) <= query_pos[-1], compute, keep_state, start_state
        )
        attended_h = accumulated / totals[:, :, None]
        log_total = top_value + jnp.log(totals)
        attended = jnp.transpose(attended_h, (1, 0, 2)).reshape(local_len, D)
        attended_low = attended.astype(jnp.bfloat16)
        hidden = inputs + jnp.dot(attended_low, full_out, preferred_element_type=jnp.float32)
        normed_two_f, norm_two_back = jax.vjp(layer_norm, hidden, gain_second)
        normed_two = normed_two_f.astype(jnp.bfloat16)
        upward = jnp.dot(normed_two, full_up, preferred_element_type=jnp.float32)
        active_f, gelu_back = jax.vjp(gelu_smooth, upward)
        active = active_f.astype(jnp.bfloat16)
        result_rows = hidden + jnp.dot(active, full_down, preferred_element_type=jnp.float32)
        results.append(result_rows.astype(jnp.bfloat16))
        d_result = cotangent[micro_index, 0]
        sum_down = sum_down + contract_rows(active, d_result)
        d_active = times_rows(d_result, full_down)
        d_upward = gelu_back(d_active)[0].astype(jnp.bfloat16)
        sum_up = sum_up + contract_rows(normed_two, d_upward)
        d_normed_two = times_rows(d_upward, full_up)
        d_hidden_norm, d_gain_two = norm_two_back(d_normed_two)
        sum_gain_two = sum_gain_two + d_gain_two
        d_hidden = d_result.astype(jnp.float32) + d_hidden_norm
        d_branch = d_hidden.astype(jnp.bfloat16)
        sum_out = sum_out + contract_rows(attended_low, d_branch)
        d_attended = times_rows(d_branch, full_out).astype(jnp.bfloat16)
        dout_h = d_attended.reshape(local_len, HEADS, HEAD_DIM)
        row_delta = jnp.einsum("qhe,hqe->hq", dout_h.astype(jnp.float32), attended_h)
        zero_block = jnp.zeros((local_len, HEADS, HEAD_DIM), jnp.float32)

        def turn_keys(turn_index, loop_state):
            key_b, value_b, d_key_b, d_value_b, d_query = loop_state
            owner_index = (cycle_place + turn_index) % cycle_size
            key_pos = owner_index * local_len + jnp.arange(local_len, dtype=jnp.int32)

            def work(partial_sums):
                contrib = pair_grads(
                    query_h, dout_h, log_total, row_delta, query_pos, key_b, value_b, key_pos
                )
                return (
                    partial_sums[0] + contrib[0],
                    partial_sums[1] + contrib[1],
                    partial_sums[2] + contrib[2],
                )

            needed = (turn_index == 0) | (cycle_place + turn_index >= cycle_size)
            d_query, d_key_b, d_value_b = lax.cond(
                needed, work, keep_state, (d_query, d_key_b, d_value_b)
            )
            key_b, value_b = passed_along((key_b, value_b), "ctx", -1)
            d_key_b, d_value_b = (
                passed_along(d_key_b.astype(jnp.bfloat16), "ctx", -1).astype(d_key_b.dtype),
                passed_along(d_value_b.astype(jnp.bfloat16), "ctx", -1).astype(d_value_b.dtype),
            )
            return (key_b, value_b, d_key_b, d_value_b, d_query)

        final_state = lax.fori_loop(
            0, cycle_size, turn_keys, (key_h, value_h, zero_block, zero_block, zero_block)
        )
        d_key = final_state[2]
        d_value = final_state[3]
        d_query = final_state[4]
        d_mixed = jnp.concatenate(
            [
                d_query.reshape(local_len, D),
                d_key.reshape(local_len, D),
                d_value.reshape(local_len, D),
            ],
            axis=1,
        ).astype(jnp.bfloat16)
        sum_qkv = sum_qkv + contract_rows(normed, d_mixed)
        d_normed = times_rows(d_mixed, full_qkv)
        d_inputs_norm, d_gain_one = norm_back(d_normed)
        sum_gain_one = sum_gain_one + d_gain_one
        grad_list.append(d_hidden + d_inputs_norm)
    shares = (
        lax.psum_scatter(
            sum_gain_one.astype(jnp.bfloat16), "wshard", scatter_dimension=0, tiled=True
        ).astype(jnp.float32),
        lax.psum_scatter(
            sum_qkv.astype(jnp.bfloat16), "wshard", scatter_dimension=0, tiled=True
        ).astype(jnp.float32),
        lax.psum_scatter(
            sum_out.astype(jnp.bfloat16), "wshard", scatter_dimension=0, tiled=True
        ).astype(jnp.float32),
        lax.psum_scatter(
            sum_gain_two.astype(jnp.bfloat16), "wshard", scatter_dimension=0, tiled=True
        ).astype(jnp.float32),
        lax.psum_scatter(
            sum_up.astype(jnp.bfloat16), "wshard", scatter_dimension=0, tiled=True
        ).astype(jnp.float32),
        lax.psum_scatter(
            sum_down.astype(jnp.bfloat16), "wshard", scatter_dimension=0, tiled=True
        ).astype(jnp.float32),
    )
    summed = (
        lax.psum(shares[0].astype(jnp.bfloat16), "ctx").astype(jnp.float32),
        lax.psum(shares[1].astype(jnp.bfloat16), "ctx").astype(jnp.float32),
        lax.psum(shares[2].astype(jnp.bfloat16), "ctx").astype(jnp.float32),
        lax.psum(shares[3].astype(jnp.bfloat16), "ctx").astype(jnp.float32),
        lax.psum(shares[4].astype(jnp.bfloat16), "ctx").astype(jnp.float32),
        lax.psum(shares[5].astype(jnp.bfloat16), "ctx").astype(jnp.float32),
    )
    result_out = jnp.stack(results)[:, None]
    grad_out_tokens = jnp.stack(grad_list)[:, None]
    return (
        result_out,
        grad_out_tokens,
        summed[0],
        summed[1],
        summed[2],
        summed[3],
        summed[4],
        summed[5],
    )


BF = jnp.bfloat16
F32 = jnp.float32
TILE = 256
SHARD = D // 4
OWN_HEADS = HEADS // 4
OWN = OWN_HEADS * HEAD_DIM
MIX = 3 * OWN
HEAD_ROWS = 160
PART = SHARD // 2
QUART = SHARD // 4
HALF = D // 2
MIDDLE_ROW = 224
VMEM_LIMIT = 56 * 1024 * 1024
WHOLE = pl.BlockSpec(memory_space=pltpu.VMEM)
ANYWHERE = pl.BlockSpec(memory_space=pl.ANY)


def nn(a, b):
    return lax.dot_general(a, b, (((1,), (0,)), ((), ())), preferred_element_type=F32)


def nt(a, b):
    return lax.dot_general(a, b, (((1,), (1,)), ((), ())), preferred_element_type=F32)


def normalised(x):
    centred = x - jnp.mean(x, axis=-1, keepdims=True)
    variance = jnp.mean(centred * centred, axis=-1, keepdims=True)
    inverse = lax.rsqrt(variance + EPSILON)
    return centred * inverse, inverse


def norm_back(xhat, inverse, gain, dy):
    g = dy * gain
    mean_g = jnp.mean(g, axis=-1, keepdims=True)
    mean_gx = jnp.mean(g * xhat, axis=-1, keepdims=True)
    return (g - mean_g - xhat * mean_gx) * inverse


def causal_tile():
    rows = lax.broadcasted_iota(jnp.int32, (TILE, TILE), 0)
    cols = lax.broadcasted_iota(jnp.int32, (TILE, TILE), 1)
    return rows <= cols


def call(kernel, name, ins, outs, scratch, flops, args, out_specs=None):
    moved = sum(a.size * a.dtype.itemsize for a in args)
    return pl.pallas_call(
        kernel,
        in_specs=ins,
        out_specs=out_specs or [WHOLE] * len(outs),
        out_shape=[jax.ShapeDtypeStruct(shape, kind) for shape, kind in outs],
        scratch_shapes=scratch,
        compiler_params=pltpu.CompilerParams(vmem_limit_bytes=VMEM_LIMIT),
        cost_estimate=pl.CostEstimate(flops=1000, bytes_accessed=1000, transcendentals=0),
        name=name,
    )(*args)


def shard_rows_of(pieces, which, first, count):
    if which < 3:
        return pieces[which].at[pl.ds(first, count)]
    half = pieces[3].shape[0]
    if first < half:
        return pieces[3].at[pl.ds(first, count)]
    return pieces[4].at[pl.ds(first - half, count)]


def run_copies(pairs, sems):
    copies = [pltpu.make_async_copy(src, dst, sems.at[i]) for i, (src, dst) in enumerate(pairs)]
    for copy in copies:
        copy.start()
    for copy in copies:
        copy.wait()


def attend_kernel(x_ref, w0, w1, w2, w3, w4,
                  normed_out, kv_out, mixt_out, att_ref, low_ref, lse_ref, wfull_out, gains_ref,
                  normed_ref, kv_ref, mixt_ref, wfull_ref, s_ref, g_ref, wsems, sems):
    place = lax.axis_index("wshard")
    pieces = (w0, w1, w2, w3, w4)
    half = w3.shape[0]
    pairs = []
    for k in range(4):
        to = pl.multiple_of(jnp.bitwise_xor(place, k) * SHARD, SHARD)
        if k < 3:
            pairs.append((shard_rows_of(pieces, k, 0, SHARD), wfull_ref.at[pl.ds(to, SHARD)]))
        else:
            pairs.append((w3, wfull_ref.at[pl.ds(to, half)]))
            pairs.append((w4.at[pl.ds(0, SHARD - half)], wfull_ref.at[pl.ds(to + half, SHARD - half)]))
        source = w4.at[pl.ds(SHARD - half, 16)] if k == 3 else pieces[k].at[pl.ds(SHARD, 16)]
        pairs.append((source, g_ref.at[k]))
    run_copies(pairs, wsems)
    gains = jnp.concatenate([g_ref[jnp.bitwise_xor(place, j)][0:8, 0:SHARD].astype(F32) for j in range(4)], axis=1)
    gains_ref[...] = gains
    for row in range(4):
        here = slice(row * TILE, (row + 1) * TILE)
        xhat, _ = normalised(x_ref[row].astype(F32))
        normed = (xhat * gains[0:1]).astype(BF)
        normed_ref[here, :] = normed
        mix = nn(normed, wfull_ref[...]).astype(BF)
        mixt_ref[:, here] = mix.T
        for h in range(OWN_HEADS):
            kv_ref[h, here, 0:HEAD_DIM] = mix[:, OWN + h * HEAD_DIM : OWN + (h + 1) * HEAD_DIM]
            kv_ref[h, here, HEAD_DIM:] = mix[:, 2 * OWN + h * HEAD_DIM : 2 * OWN + (h + 1) * HEAD_DIM]

    pairs = ((normed_ref, normed_out), (kv_ref, kv_out), (mixt_ref, mixt_out), (wfull_ref, wfull_out))
    copies = [pltpu.make_async_copy(src, dst, sems.at[k]) for k, (src, dst) in enumerate(pairs)]
    for copy in copies:
        copy.start()

    for h in range(OWN_HEADS):
        base = h * HEAD_DIM
        for block in range(4):
            here = slice(block * TILE, (block + 1) * TILE)
            queries = mixt_ref[pl.ds(base, HEAD_DIM), here] * BF(HEAD_DIM**-0.5)
            top = jnp.zeros((1, TILE), F32)
            for other in range(block + 1):
                there = slice(other * TILE, (other + 1) * TILE)
                s = nn(kv_ref[h, there, 0:HEAD_DIM], queries)
                s_ref[there, :] = s
                size = jnp.abs(s)
                if other == block:
                    size = jnp.where(causal_tile(), size, 0.0)
                top = jnp.maximum(top, jnp.max(size, axis=0, keepdims=True))
            top = jnp.sqrt(top * top + 1.0)
            total = jnp.zeros((1, TILE), F32)
            acc = jnp.zeros((HEAD_DIM, TILE), F32)
            for other in range(block + 1):
                there = slice(other * TILE, (other + 1) * TILE)
                s = s_ref[there, :]
                square = s * s + 1.0
                r = lax.rsqrt(square)
                p = jnp.exp(square * r - top)
                if other == block:
                    p = jnp.where(causal_tile(), p, 0.0)
                total = total + jnp.sum(p, axis=0, keepdims=True)
                signed = (s * r * p).astype(BF)
                acc = acc + nn(mixt_ref[pl.ds(2 * OWN + base, HEAD_DIM), there], signed)
            att = acc / total
            att_ref[pl.ds(base, HEAD_DIM), here] = att
            low_ref[block, pl.ds(base, HEAD_DIM), :] = att.astype(BF)
            lse_ref[pl.ds(h, 1), here] = top + jnp.log(total)

    for copy in copies:
        copy.wait()


def attend(x_all, pieces):
    length = 4 * TILE
    return call(
        attend_kernel,
        "attend",
        [WHOLE] + [ANYWHERE] * 5,
        [
            ((length, D), BF),
            ((OWN_HEADS, length, 2 * HEAD_DIM), BF),
            ((MIX, length), BF),
            ((OWN, length), F32),
            ((4, OWN, TILE), BF),
            ((8, length), F32),
            ((D, MIX), BF),
            ((8, D), F32),
        ],
        [
            pltpu.VMEM((length, D), BF),
            pltpu.VMEM((OWN_HEADS, length, 2 * HEAD_DIM), BF),
            pltpu.VMEM((MIX, length), BF),
            pltpu.VMEM((D, MIX), BF),
            pltpu.VMEM((length, TILE), F32),
            pltpu.VMEM((4, 16, MIX), BF),
            pltpu.SemaphoreType.DMA((9,)),
            pltpu.SemaphoreType.DMA((4,)),
        ],
        3 * 10**9,
        (x_all, *pieces),
        [ANYWHERE] * 3 + [WHOLE] * 3 + [ANYWHERE, WHOLE],
    )


def parcel_kernel(cot_ref, wout_ref, wup_ref, x_on_ref, x_ref, y_on_ref, y_ref, sems):
    place = lax.axis_index("wshard")

    def columns(k, first, count):
        at = pl.multiple_of(jnp.bitwise_xor(place, k) * D, D)
        return wup_ref.at[pl.ds(first, count), pl.ds(at, D)]

    low, high = cot_ref.at[pl.ds(0, MIDDLE_ROW)], cot_ref.at[pl.ds(MIDDLE_ROW, 32)]
    pairs = (
        (low, x_on_ref.at[pl.ds(0, MIDDLE_ROW)]),
        (columns(3, 0, PART), x_on_ref.at[pl.ds(MIDDLE_ROW, PART)]),
        (high, y_on_ref.at[pl.ds(0, 32)]),
        (wout_ref, y_on_ref.at[pl.ds(32, SHARD)]),
        (columns(3, PART, PART), y_on_ref.at[pl.ds(MIDDLE_ROW, PART)]),
        (columns(1, 0, SHARD), x_ref.at[pl.ds(0, SHARD)]),
        (high, x_ref.at[pl.ds(SHARD, 32)]),
        (wout_ref, x_ref.at[pl.ds(SHARD + 32, SHARD)]),
        (columns(2, 0, SHARD), y_ref.at[pl.ds(0, SHARD)]),
        (low, y_ref.at[pl.ds(SHARD, MIDDLE_ROW)]),
    )
    run_copies(pairs, sems)


def parcels(cot, w_out, w_up):
    on, rest = MIDDLE_ROW + PART, SHARD + MIDDLE_ROW
    return call(
        parcel_kernel,
        "parcels",
        [ANYWHERE] * 3,
        [((on, D), BF), ((rest, D), BF)] * 2,
        [pltpu.SemaphoreType.DMA((10,))],
        10**6,
        (cot, w_out, w_up),
    )


def assemble_kernel(cot_ref, own_ref, wup_ref, x_on, x_rest, y_on, y_rest, corner_a, corner_b,
                    wout_ref, up_ref, cots_ref, sems):
    place = lax.axis_index("wshard")
    at = [pl.multiple_of(jnp.bitwise_xor(place, k) * SHARD, SHARD) for k in range(4)]
    half = PART
    mine = pl.multiple_of(place * D, D)
    pairs = (
        (own_ref, wout_ref.at[pl.ds(at[0], SHARD)]),
        (x_rest.at[pl.ds(SHARD + 32, SHARD)], wout_ref.at[pl.ds(at[1], SHARD)]),
        (y_on.at[pl.ds(32, SHARD)], wout_ref.at[pl.ds(at[2], SHARD)]),
        (corner_b.at[pl.ds(32, SHARD)], wout_ref.at[pl.ds(at[3], SHARD)]),
        (wup_ref.at[:, pl.ds(mine, D)], up_ref.at[pl.ds(at[0], SHARD)]),
        (x_rest.at[pl.ds(0, SHARD)], up_ref.at[pl.ds(at[1], SHARD)]),
        (y_rest.at[pl.ds(0, SHARD)], up_ref.at[pl.ds(at[2], SHARD)]),
        (corner_a.at[pl.ds(MIDDLE_ROW, half)], up_ref.at[pl.ds(at[3], half)]),
        (corner_b.at[pl.ds(MIDDLE_ROW, half)], up_ref.at[pl.ds(at[3] + half, half)]),
        (cot_ref, cots_ref.at[pl.ds(0, TILE)]),
        (x_on.at[pl.ds(0, MIDDLE_ROW)], cots_ref.at[pl.ds(TILE, MIDDLE_ROW)]),
        (x_rest.at[pl.ds(SHARD, 32)], cots_ref.at[pl.ds(TILE + MIDDLE_ROW, 32)]),
        (y_rest.at[pl.ds(SHARD, MIDDLE_ROW)], cots_ref.at[pl.ds(2 * TILE, MIDDLE_ROW)]),
        (y_on.at[pl.ds(0, 32)], cots_ref.at[pl.ds(2 * TILE + MIDDLE_ROW, 32)]),
        (corner_a.at[pl.ds(0, MIDDLE_ROW)], cots_ref.at[pl.ds(3 * TILE, MIDDLE_ROW)]),
        (corner_b.at[pl.ds(0, 32)], cots_ref.at[pl.ds(3 * TILE + MIDDLE_ROW, 32)]),
    )
    run_copies(pairs, sems)


def assemble(cot, w_out, w_up, shared):
    return call(
        assemble_kernel,
        "assemble",
        [ANYWHERE] * 9,
        [((D, D), BF), ((D, D), BF), ((4 * TILE, D), BF)],
        [pltpu.SemaphoreType.DMA((16,))],
        10**6,
        (cot, w_out, w_up, *shared),
    )


def project_kernel(att_ref, x_ref, gain_ref, wout_ref, hidden_ref, normed_ref):
    hidden = x_ref[...].astype(F32) + nn(att_ref[...].T, wout_ref[...])
    hidden_ref[...] = hidden
    xhat, _ = normalised(hidden)
    normed_ref[...] = (xhat * gain_ref[1:2]).astype(BF)


def project(att_home, x_block, gain, w_out):
    rows = x_block.shape[0]
    return call(
        project_kernel,
        "project",
        [WHOLE] * 4,
        [((rows, D), F32), ((rows, D), BF)],
        [],
        3 * 10**8,
        (att_home, x_block, gain, w_out),
    )


SLOPE = (2.0 / 3.141592653589793) ** 0.5


def feed_rows(n, cot, up_ref, down_ref, active_ref, dup_ref, here):
    for first in range(0, D, TILE):
        cols = slice(first, first + TILE)
        u = nn(n, up_ref[:, cols])
        square = u * u
        t = jnp.tanh(SLOPE * (u + 0.044715 * (square * u)))
        side = 0.5 + 0.5 * t
        active_ref[here, cols] = (u * side).astype(BF)
        grad = side + (0.5 * SLOPE) * u * (1.0 - t * t) * (1.0 + 0.134145 * square)
        dup_ref[here, cols] = (grad * nt(cot, down_ref[cols, :])).astype(BF)
    return nn(active_ref[here, :], down_ref[...]), nt(dup_ref[here, :], up_ref[...])


def feed_own_kernel(n_ref, cot_ref, up_ref, down_ref, active_ref, dup_ref, out_ref, dout_ref):
    out_ref[...], dout_ref[...] = feed_rows(
        n_ref[...], cot_ref[0:TILE, :], up_ref, down_ref, active_ref, dup_ref, slice(0, TILE)
    )


def feed_own(n, cots, up, down):
    return call(
        feed_own_kernel,
        "feed_own",
        [WHOLE] * 4,
        [((TILE, D), BF), ((TILE, D), BF), ((TILE, D), F32), ((TILE, D), F32)],
        [],
        2 * 10**9,
        (n, cots, up, down),
    )


def feed_near_kernel(nx_ref, ny_ref, cot_ref, up_ref, down_ref, active_ref, dup_ref, out_ref, dout_ref):
    for k, n_ref in enumerate((nx_ref, ny_ref)):
        here = slice(k * TILE, (k + 1) * TILE)
        out, dout = feed_rows(n_ref[...], cot_ref[(k + 1) * TILE : (k + 2) * TILE, :], up_ref, down_ref, active_ref, dup_ref, here)
        out_ref[here, :], dout_ref[here, :] = out.astype(BF), dout.astype(BF)


def feed_near(nx, ny, cots, up, down):
    return call(
        feed_near_kernel,
        "feed_near",
        [WHOLE] * 5,
        [((2 * TILE, D), BF)] * 4,
        [],
        4 * 10**9,
        (nx, ny, cots, up, down),
    )


def feed_far_kernel(na_ref, nb_ref, cot_ref, out_ref, dout_ref, up_ref, down_ref,
                    active_ref, dup_ref, oa_ref, oaf_ref, ob_ref, obf_ref, da_ref, daf_ref, db_ref, dbf_ref):
    n = jnp.concatenate([na_ref[...], nb_ref[...]])
    cot = cot_ref[3 * TILE :, :]
    half = TILE // 2
    out, dout = feed_rows(n, cot, up_ref, down_ref, active_ref, dup_ref, slice(0, TILE))
    for far, near, a, af, b, bf in (
        (out, out_ref, oa_ref, oaf_ref, ob_ref, obf_ref),
        (dout, dout_ref, da_ref, daf_ref, db_ref, dbf_ref),
    ):
        far = far.astype(BF)
        a[0], a[1] = near[0:half, :], far[0:half]
        b[0], b[1] = near[TILE + half :, :], far[half:]
        af[...] = near[TILE : TILE + half, :]
        bf[...] = near[half:TILE, :]


def feed_far(na, nb, cots, out, dout, up, down):
    half = TILE // 2
    return call(
        feed_far_kernel,
        "feed_far",
        [WHOLE] * 7,
        [((TILE, D), BF)] * 2 + [((2, half, D), BF), ((half, D), BF)] * 4,
        [],
        2 * 10**9,
        (na, nb, cots, out, dout, up, down),
    )


def feed_grads_kernel(n0, n1, n2, n3, n4, cot_ref, a0, a1, a2, d0, d1, d2,
                      shares_ref, nt_ref, at_ref, dup_ref):
    for k, piece in enumerate((n0, n1, n2)):
        nt_ref[:, k * TILE : (k + 1) * TILE] = piece[...].T
    nt_ref[:, 3 * TILE :] = jnp.concatenate([n3[...], n4[...]]).T
    at_ref[:, 0:TILE] = a0[...].T
    at_ref[:, TILE : 3 * TILE] = a1[...].T
    at_ref[:, 3 * TILE :] = a2[...].T
    dup_ref[0:TILE] = d0[...]
    dup_ref[TILE : 3 * TILE] = d1[...]
    dup_ref[3 * TILE :] = d2[...]
    rows = D // 8
    for k in range(8):
        g = nn(at_ref[k * rows : (k + 1) * rows, :], cot_ref[...]).astype(BF)
        for side in range(2):
            for part in range(2):
                piece = g[part * QUART : (part + 1) * QUART, side * HALF : (side + 1) * HALF]
                shares_ref[k, 4 + 2 * side + part] = piece
    for to in range(4):
        g = nn(nt_ref[to * SHARD : (to + 1) * SHARD, :], dup_ref[...]).astype(BF)
        slot = jnp.bitwise_xor(lax.axis_index("wshard"), to)
        for k in range(8):
            r, c = (k // 2) * QUART, (k % 2) * HALF
            shares_ref[k, slot] = g[r : r + QUART, c : c + HALF]


def feed_grads(ns, cots, actives, dups):
    length = 4 * TILE
    return call(
        feed_grads_kernel,
        "feed_grads",
        [WHOLE] * 12,
        [((8, 8, QUART, HALF), BF)],
        [
            pltpu.VMEM((D, length), BF),
            pltpu.VMEM((D, length), BF),
            pltpu.VMEM((length, D), BF),
        ],
        3 * 10**9,
        (*ns, cots, *actives, *dups),
    )[0]


def summed(keep_ref, a_ref, a_more_ref, b_ref, b_more_ref):
    first = a_ref[0].astype(F32) + a_more_ref[...].astype(F32)
    second = b_ref[0].astype(F32) + b_more_ref[...].astype(F32)
    return keep_ref[...] + jnp.concatenate([first, second])


def give_kernel(hidden_ref, keep_ref, a_ref, a_more_ref, b_ref, b_more_ref, rkeep_ref, rsend_ref, result_ref, sems):
    core = lax.axis_index("ctx") % 2
    result = (hidden_ref[...] + summed(keep_ref, a_ref, a_more_ref, b_ref, b_more_ref)).astype(BF)
    half = TILE // 2
    result_ref[0], result_ref[1] = result[:half], result[half:]
    run_copies(((result_ref.at[1 - core], rsend_ref), (result_ref.at[core], rkeep_ref)), sems)


def give(hidden, keep, parts):
    half = TILE // 2
    return call(
        give_kernel,
        "give",
        [WHOLE] * 6,
        [((half, D), BF)] * 2,
        [pltpu.VMEM((2, half, D), BF), pltpu.SemaphoreType.DMA((2,))],
        10**6,
        (hidden, keep, *parts),
        [ANYWHERE] * 2,
    )


def turn_kernel(hidden_ref, gain_ref, dkeep_ref, a_ref, a_more_ref, b_ref, b_more_ref, cot_ref, wout_ref,
                dhidden_ref, datt_ref, dbranch_ref, dgain_ref):
    gain = gain_ref[1:2]
    xhat, inverse = normalised(hidden_ref[...])
    dy = summed(dkeep_ref, a_ref, a_more_ref, b_ref, b_more_ref)
    dgain_ref[...] = jnp.sum(dy * xhat, axis=0, keepdims=True)
    d_hidden = cot_ref[...].astype(F32) + norm_back(xhat, inverse, gain, dy)
    dhidden_ref[...] = d_hidden
    d_branch = d_hidden.astype(BF)
    dbranch_ref[...] = d_branch
    d_att = nt(wout_ref[...], d_branch).astype(BF)
    for k in range(4):
        datt_ref[k] = d_att[k * OWN : (k + 1) * OWN]


def turn(hidden, gain, dkeep, parts, cot, w_out):
    rows = hidden.shape[0]
    return call(
        turn_kernel,
        "turn",
        [WHOLE] * 9,
        [((rows, D), F32), ((4, OWN, rows), BF), ((rows, D), BF), ((1, D), F32)],
        [],
        6 * 10**8,
        (hidden, gain, dkeep, *parts, cot, w_out),
    )


def out_grad_kernel(att_ref, dbranch_ref, keep_ref, send_ref, grad_ref, sems):
    core = lax.axis_index("ctx") % 2
    place = lax.axis_index("wshard")
    for to in range(4):
        e = jnp.bitwise_xor(place, to)
        e_x, e_y = jnp.bitwise_and(e, 1), e // 2
        g = nn(att_ref[to * SHARD : (to + 1) * SHARD, :], dbranch_ref[...]).astype(BF)
        for side in range(2):
            for half in range(2):
                piece = g[side * PART : (side + 1) * PART, half * HALF : (half + 1) * HALF]
                grad_ref[side, e_y, e_x, half * PART : (half + 1) * PART] = piece
    rows = pl.ds(HEAD_ROWS, SHARD)
    pairs = ((grad_ref.at[1 - core], send_ref.at[:, :, rows]), (grad_ref.at[core], keep_ref.at[:, :, rows]))
    run_copies(pairs, sems)


def out_grad(att_home, d_branch):
    return call(
        out_grad_kernel,
        "out_grad",
        [WHOLE] * 2,
        [((2, 2, HEAD_ROWS + SHARD, HALF), BF)] * 2,
        [pltpu.VMEM((2, 2, 2, SHARD, HALF), BF), pltpu.SemaphoreType.DMA((2,))],
        3 * 10**8,
        (att_home, d_branch),
        [ANYWHERE] * 2,
    )


def attend_back_kernel(kv_ref, mixt_ref, att_ref, lse_ref, dout_ref, normed_in, w_in, gain_ref, dgain_ref, _, __,
                       f0_ref, f1_ref, f2_ref, f3_ref, gkeep_ref, gsend_ref,
                       dq_ref, dk_ref, dv_ref, dm_ref, mix_ref, total_ref, first_ref, head_ref, sems,
                       normed_ref, w_ref, in_sems):
    length = kv_ref.shape[1]
    loads = [
        pltpu.make_async_copy(normed_in, normed_ref, in_sems.at[0]),
        pltpu.make_async_copy(w_in, w_ref, in_sems.at[1]),
    ]
    for load in loads:
        load.start()
    scale = BF(HEAD_DIM**-0.5)
    core = lax.axis_index("ctx") % 2
    z = lax.axis_index("ctx") // 2
    place = lax.axis_index("wshard")

    for h in range(OWN_HEADS):
        base = h * HEAD_DIM
        for block in range(4):
            here = slice(block * TILE, (block + 1) * TILE)
            queries = mixt_ref[pl.ds(base, HEAD_DIM), here] * scale
            dout = dout_ref[block, pl.ds(base, HEAD_DIM), :]
            delta = jnp.sum(dout.astype(F32) * att_ref[pl.ds(base, HEAD_DIM), here], axis=0, keepdims=True)
            lse = lse_ref[pl.ds(h, 1), here]
            acc = jnp.zeros((HEAD_DIM, TILE), F32)
            for other in range(block + 1):
                there = slice(other * TILE, (other + 1) * TILE)
                s = nn(kv_ref[h, there, 0:HEAD_DIM], queries)
                ds = nn(kv_ref[h, there, HEAD_DIM:], dout)
                square = s * s + 1.0
                r = lax.rsqrt(square)
                chance = jnp.exp(square * r - lse)
                if other == block:
                    chance = jnp.where(causal_tile(), chance, 0.0)
                tilted = s * r
                signed = (tilted * chance).astype(BF)
                slope = r * r * r + tilted * tilted
                dsc = (chance * (ds * slope - tilted * delta)).astype(BF)
                acc = acc + nn(mixt_ref[pl.ds(OWN + base, HEAD_DIM), there], dsc)
                dk = nt(dsc, queries)
                dv = nt(signed, dout)
                if other == block:
                    dk_ref[there, :] = dk
                    dv_ref[there, :] = dv
                else:
                    dk_ref[there, :] += dk
                    dv_ref[there, :] += dv
            dq_ref[:, here] = acc * HEAD_DIM**-0.5
        dm_ref[h, :, 0:HEAD_DIM] = dq_ref[...].T.astype(BF)
        dm_ref[h, :, HEAD_DIM : 2 * HEAD_DIM] = dk_ref[...].astype(BF)
        dm_ref[h, :, 2 * HEAD_DIM :] = dv_ref[...].astype(BF)

    for h in range(OWN_HEADS):
        for kind in range(3):
            to = kind * OWN + h * HEAD_DIM
            mix_ref[:, to : to + HEAD_DIM] = dm_ref[h, :, kind * HEAD_DIM : (kind + 1) * HEAD_DIM]
    total_ref[...] = jnp.zeros_like(total_ref)
    for load in loads:
        load.wait()
    for block in range(4):
        here = slice(block * TILE, (block + 1) * TILE)
        first = nt(mix_ref[here, :], w_ref[...])
        first_ref[block] = first.astype(BF)
        total_ref[...] += jnp.sum(first * normed_ref[here, :].astype(F32), axis=0, keepdims=True)
    outs = (f3_ref, f2_ref, f1_ref, f0_ref)
    copies = [
        pltpu.make_async_copy(first_ref.at[jnp.bitwise_xor(z, 3 - k)], ref, sems.at[k]) for k, ref in enumerate(outs)
    ]
    for copy in copies:
        copy.start()
    gain_one = total_ref[...] / gain_ref[0:1]
    gain_two = dgain_ref[...]
    for to in range(4):
        e = jnp.bitwise_xor(place, to)
        e_x, e_y = jnp.bitwise_and(e, 1), e // 2
        g = nn(normed_ref[:, to * SHARD : (to + 1) * SHARD].T, mix_ref[...]).astype(BF)
        span = slice(to * SHARD, (to + 1) * SHARD)
        gains = jnp.concatenate([gain_one[:, span], gain_two[:, span], jnp.zeros((14, SHARD), F32)], axis=0)
        gains = jnp.concatenate([gains, jnp.zeros((16, HALF - SHARD), F32)], axis=1).astype(BF)
        for side in range(2):
            at = side * PART
            head_ref[side, e_y, e_x, 0:PART] = g[at : at + PART, 0:HALF]
            head_ref[side, e_y, e_x, PART : PART + QUART, 0:OWN] = g[at : at + QUART, HALF:]
            head_ref[side, e_y, e_x, PART : PART + QUART, OWN:] = g[at + QUART : at + PART, HALF:]
            head_ref[side, e_y, e_x, PART + QUART :] = gains if side == 0 else jnp.zeros_like(gains)
    more = [
        pltpu.make_async_copy(head_ref.at[1 - core], gsend_ref.at[:, :, pl.ds(0, HEAD_ROWS)], sems.at[4]),
        pltpu.make_async_copy(head_ref.at[core], gkeep_ref.at[:, :, pl.ds(0, HEAD_ROWS)], sems.at[5]),
    ]
    for copy in more:
        copy.start()
    for copy in copies + more:
        copy.wait()


def attend_back(kv, mixt, att, lse, dout, normed, w, gain, dgain, keep, send):
    length = normed.shape[0]
    return pl.pallas_call(
        attend_back_kernel,
        in_specs=[WHOLE] * 5 + [ANYWHERE] * 2 + [WHOLE] * 2 + [ANYWHERE] * 2,
        out_specs=[ANYWHERE] * 6,
        out_shape=[jax.ShapeDtypeStruct((TILE, D), BF)] * 4 + [jax.ShapeDtypeStruct(keep.shape, BF)] * 2,
        input_output_aliases={9: 4, 10: 5},
        scratch_shapes=[
            pltpu.VMEM((HEAD_DIM, length), F32),
            pltpu.VMEM((length, HEAD_DIM), F32),
            pltpu.VMEM((length, HEAD_DIM), F32),
            pltpu.VMEM((OWN_HEADS, length, 3 * HEAD_DIM), BF),
            pltpu.VMEM((length, MIX), BF),
            pltpu.VMEM((1, D), F32),
            pltpu.VMEM((4, TILE, D), BF),
            pltpu.VMEM((2, 2, 2, HEAD_ROWS, HALF), BF),
            pltpu.SemaphoreType.DMA((6,)),
            pltpu.VMEM((length, D), BF),
            pltpu.VMEM((D, MIX), BF),
            pltpu.SemaphoreType.DMA((2,)),
        ],
        compiler_params=pltpu.CompilerParams(vmem_limit_bytes=VMEM_LIMIT),
        cost_estimate=pl.CostEstimate(flops=1000, bytes_accessed=1000, transcendentals=0),
        name="attend_back",
    )(kv, mixt, att, lse, dout, normed, w, gain, dgain, keep, send)


def is_inner():
    z = lax.axis_index("ctx") // 2
    return (z == 1) | (z == 2)


def last_kernel(first_ref, pair_ref, middle_ref, x_ref, gain_ref, dhidden_ref, keep_ref, send_ref, grad_ref, sems):
    core = lax.axis_index("ctx") % 2
    rows = x_ref.shape[0] // 2
    dy = first_ref[...].astype(F32) + pair_ref[...].astype(F32)
    dy = dy + jnp.where(is_inner(), middle_ref[...].astype(F32), 0.0)
    xhat, inverse = normalised(x_ref[...].astype(F32))
    grad = dhidden_ref[...] + norm_back(xhat, inverse, gain_ref[0:1], dy)
    grad_ref[0], grad_ref[1] = grad[:rows], grad[rows:]
    run_copies(((grad_ref.at[1 - core], send_ref), (grad_ref.at[core], keep_ref)), sems)


def last(*args):
    rows = TILE // 2
    return call(
        last_kernel,
        "last",
        [WHOLE] * 6,
        [((rows, D), F32), ((rows, D), F32)],
        [pltpu.VMEM((2, rows, D), F32), pltpu.SemaphoreType.DMA((2,))],
        10**7,
        args,
        [ANYWHERE] * 2,
    )


def line_slots():
    z = lax.axis_index("ctx") // 2
    return z, jnp.bitwise_xor(z, 1), jnp.where(z < 2, 2, 1), jnp.where(z < 2, 3, 0)


def finish_feed_kernel(*refs):
    mine, theirs, (gup_ref, gdown_ref) = refs[:4], refs[4:8], refs[8:]
    core = lax.axis_index("ctx") % 2
    place = lax.axis_index("wshard")
    rows = D // 8
    for group, side in ((mine, core), (theirs, 1 - core)):
        for ref, slot in zip(group, line_slots()):
            at = pl.multiple_of(slot * QUART, 16)
            for k in range(4):
                to = pl.multiple_of(jnp.bitwise_xor(place, k) * D + side * HALF, 128)
                gup_ref[pl.ds(at, QUART), pl.ds(to, HALF)] = ref[k * QUART : (k + 1) * QUART].astype(F32)
            at = pl.multiple_of((2 * slot + side) * rows, 32)
            for half in range(2):
                share = ref[SHARD + half * rows : SHARD + (half + 1) * rows]
                gdown_ref[pl.ds(at, rows), half * HALF : (half + 1) * HALF] = share.astype(F32)


def finish_feed(*args):
    return call(
        finish_feed_kernel, "finish_feed", [WHOLE] * 8, [((SHARD, 4 * D), F32), ((D, D), F32)], [], 10**7, args
    )


def finish_heads_kernel(*refs):
    mine, theirs, outs, (gout_ref, gqkv_ref, one_ref, two_ref) = refs[:4], refs[4:8], refs[8:10], refs[10:]
    slots = line_slots()
    first = lax.axis_index("ctx") % 2 == 0
    out, other_out = [ref[...].astype(F32) for ref in outs]
    for half in range(2):
        here, cols = slice(half * PART, (half + 1) * PART), slice(half * HALF, (half + 1) * HALF)
        gout_ref[0:PART, cols] = jnp.where(first, out[here], other_out[here])
        gout_ref[PART:, cols] = jnp.where(first, other_out[here], out[here])
    mine, theirs = [[ref[...].astype(F32) for ref in group] for group in (mine, theirs)]
    low = [jnp.where(first, a, b) for a, b in zip(mine, theirs)]
    high = [jnp.where(first, b, a) for a, b in zip(mine, theirs)]
    gains = sum(block[PART + QUART :, 0:SHARD] for block in low)
    one_ref[...], two_ref[...] = gains[0], gains[1]
    for slot in range(4):
        for side, group in enumerate((low, high)):
            block = jnp.where(
                slot == slots[0],
                group[0],
                jnp.where(slot == slots[1], group[1], jnp.where(slot == slots[2], group[2], group[3])),
            )
            at, to = side * PART, slot * OWN
            gqkv_ref[at : at + PART, to : to + OWN] = block[0:PART, 0:OWN]
            gqkv_ref[at : at + PART, D + to : D + to + OWN] = block[0:PART, OWN:]
            gqkv_ref[at : at + QUART, 2 * D + to : 2 * D + to + OWN] = block[PART : PART + QUART, 0:OWN]
            gqkv_ref[at + QUART : at + PART, 2 * D + to : 2 * D + to + OWN] = block[PART : PART + QUART, OWN:]


def finish_heads(*args):
    return call(
        finish_heads_kernel,
        "finish_heads",
        [WHOLE] * 10,
        [((SHARD, D), F32), ((SHARD, 3 * D), F32), ((SHARD,), F32), ((SHARD,), F32)],
        [],
        10**7,
        args,
    )


def pick(value, index, axis=0):
    return lax.dynamic_index_in_dim(value, index, axis, keepdims=False)


def across_w(value, flip):
    return lax.ppermute(value, "wshard", [(i, i ^ flip) for i in range(4)])


def across_core(value):
    return lax.ppermute(value, "ctx", [(i, i ^ 1) for i in range(8)])


def between_z(value, pairs):
    return lax.ppermute(value, "ctx", [(2 * a + c, 2 * b + c) for a, b in pairs for c in range(2)])


Z_GROUPS = [[0, 2, 4, 6], [1, 3, 5, 7]]


def after(value, *others):
    return lax.optimization_barrier((value, *others))[0]


PAIRS = [(0, 1), (1, 0), (2, 3), (3, 2)]
MIDDLE = [(1, 2), (2, 1), (0, 0), (3, 3)]


def line_z(block):
    pair = between_z(block, PAIRS)
    mid_near = between_z(block, MIDDLE)
    near = between_z(mid_near, PAIRS)
    mid_far = between_z(pair, MIDDLE)
    far = between_z(mid_far, PAIRS)
    return block, pair, near, far, mid_near, mid_far


TO_MIDDLE = [(0, 1), (3, 2)]
TO_ENDS = [(1, 0), (2, 3)]
ACROSS = [(1, 2), (2, 1)]


def own_slot(slots, x_first):
    one, two = (1, 2) if x_first else (2, 1)
    got = across_w(slots[1], one)
    far = slots[0, 1] + got[1]
    return (slots[0, 0] + got[0]) + across_w(far, two)


def gather_plane(block, *others):
    half = block.shape[0] // 2
    from_x, from_y = across_w(block, 1), across_w(block, 2)
    first, second = from_x[:half], from_y[half:]
    if others:
        first, second, *_ = tied(first, second, *others)
    return block, from_x, from_y, across_w(first, 2), across_w(second, 1)


def tied(*values):
    return lax.optimization_barrier(values)


def local_grid(tokens, gain_one, w_qkv, w_out, gain_two, w_up, w_down, cotangent):
    core = lax.axis_index("ctx") % 2
    z = lax.axis_index("ctx") // 2
    place = lax.axis_index("wshard")
    inner = (z == 1) | (z == 2)

    def both_micros(kept, got):
        return jnp.where(core == 0, jnp.stack([kept, got]), jnp.stack([got, kept]))[:, None]

    tok, cot = tokens[:, 0], cotangent[:, 0]
    kept = jnp.concatenate([pick(tok, core), pick(cot, core)])
    got = across_core(jnp.concatenate([pick(tok, 1 - core), pick(cot, 1 - core)]))
    half = TILE // 2
    own = [jnp.where(core == 0, a, b) for a, b in ((kept, got), (got, kept))]
    x_block = jnp.concatenate([own[0][:half], own[1][:half]])
    cot = jnp.concatenate([own[0][half:], own[1][half:]])

    w_heads = pick(w_qkv.reshape(SHARD, 3, 4, OWN), z, 2).reshape(SHARD, MIX)
    gains = jnp.pad(jnp.stack([gain_one, gain_two]), ((0, 30), (0, MIX - SHARD)))
    x_all = lax.all_to_all(
        jnp.broadcast_to(x_block, (4,) + x_block.shape), "ctx", 0, 0, tiled=True, axis_index_groups=Z_GROUPS
    )
    x_on, x_rest, y_on, y_rest = parcels(cot, w_out, w_up)
    x_on, y_on = across_w(x_on, 1), across_w(y_on, 2)
    x_on, y_on, w_heads = tied(x_on, y_on, jnp.concatenate([w_heads, gains]))
    heads = gather_plane(w_heads)
    x_rest, y_rest, x_on, y_on, *heads = tied(x_rest, y_rest, x_on, y_on, *heads)
    corner_a, corner_b = across_w(x_on, 2), across_w(y_on, 1)
    x_rest, y_rest = across_w(x_rest, 1), across_w(y_rest, 2)
    normed_all, kv, mixt, att, att_low, lse, w_full, gains = attend(x_all, heads)
    att_low, corner_a, corner_b = tied(att_low, corner_a, corner_b)
    shared = x_on, x_rest, y_on, y_rest, corner_a, corner_b
    att_home = lax.all_to_all(att_low, "ctx", 0, 0, tiled=True, axis_index_groups=Z_GROUPS).reshape(D, -1)
    wout_full, up, cots = assemble(cot, w_out, w_up, shared)
    hidden, normed_two = project(att_home, x_block, gains, wout_full)

    active0, dup0, out0, dout0 = feed_own(normed_two, cots, up, w_down)
    ns = gather_plane(normed_two, active0)
    active1, dup1, out1, dout1 = feed_near(ns[1], ns[2], cots, up, w_down)
    active2, dup2, *parts = feed_far(ns[3], ns[4], cots, out1, dout1, up, w_down)
    parts, (a, a_far, b, b_far) = parts[:4], parts[4:]
    got_a, got_b = across_w(a, 1), across_w(b, 2)
    shares = feed_grads(ns, cots, (active0, active1, active2), (dup0, dup1, dup2))
    shares, got_a, got_b = tied(shares, got_a, got_b)
    shares = lax.psum_scatter(shares, "ctx", scatter_dimension=0)
    more_a, more_b = across_w(a_far + got_a[1], 2), across_w(b_far + got_b[1], 1)
    d_hidden, d_att, d_branch, d_gain_two = turn(
        hidden, gains, dout0, (got_a, more_a, got_b, more_b), cot, wout_full
    )
    d_out = lax.all_to_all(d_att, "ctx", 0, 0, tiled=True, axis_index_groups=Z_GROUPS)
    keep, send = out_grad(att_home, d_branch)
    d_out, keep, send = tied(d_out, keep, send)
    a, a_far, b, b_far = parts
    got_a, got_b = across_w(a, 1), across_w(b, 2)
    *firsts, keep, send = attend_back(
        kv, mixt, att, lse, d_out, normed_all, w_full, gains, d_gain_two, keep, send
    )
    *firsts, keep, send, shares, got_a, got_b = tied(*firsts, keep, send, shares, got_a, got_b)

    got = between_z(firsts[3], TO_MIDDLE)
    both = firsts[2] + jnp.where(inner, got, BF(0))
    outer, middle = between_z(both, TO_MIDDLE), between_z(both, ACROSS)
    pair = between_z(firsts[1] + jnp.where(inner, middle, BF(0)), PAIRS)
    middle = between_z(firsts[3] + outer, ACROSS)

    ups = [shares[0]] + [across_w(shares[e], e) for e in (1, 2, 3)]
    share = jnp.concatenate(ups + [shares[4:].reshape(SHARD, HALF)])
    share_pair, share_mid = between_z(share, PAIRS), between_z(share, ACROSS)
    share_near, share_mid_far = between_z(share_mid, TO_ENDS), between_z(share_pair, ACROSS)
    share_far = between_z(share_mid_far, TO_ENDS)
    blocks = share, share_pair, jnp.where(inner, share_mid, share_near), jnp.where(inner, share_mid_far, share_far)
    grad_up, grad_down = finish_feed(*blocks, *(across_core(block) for block in blocks))

    sums, a_far, b_far = tied(keep + across_core(send), a_far, b_far)
    sums_got = across_w(sums[1], 2)
    sums_far = across_w(sums[0, 1] + sums_got[1], 1)
    sums, a_far, b_far = tied((sums[0, 0] + sums_got[0]) + sums_far, a_far, b_far)
    more_a, more_b = across_w(a_far + got_a[1], 2), across_w(b_far + got_b[1], 1)
    result_keep, result_send = give(hidden, out0, (got_a, more_a, got_b, more_b))
    out_result = both_micros(result_keep, across_core(result_send))
    sums_pair, head_mid = between_z(sums, PAIRS), between_z(sums[:HEAD_ROWS], ACROSS)
    out = sums[HEAD_ROWS:] + sums_pair[HEAD_ROWS:]
    head_near = between_z(head_mid, TO_ENDS)
    sums_far = between_z(jnp.concatenate([sums_pair[:HEAD_ROWS], out]), ACROSS)
    pair, middle, out_result, sums_far, head_near = tied(pair, middle, out_result, sums_far, head_near)
    sums_far = jnp.concatenate([sums_far[:HEAD_ROWS], out + sums_far[HEAD_ROWS:]])
    sums_last = between_z(sums_far, TO_ENDS)
    grad_keep, grad_send = last(firsts[0], pair, middle, x_block, gains, d_hidden)
    out_tokens = both_micros(grad_keep, across_core(grad_send))
    sums_last = jnp.where(inner, sums_far, sums_last)
    head_near = jnp.where(inner, head_mid, head_near)
    blocks = sums[:HEAD_ROWS], sums_pair[:HEAD_ROWS], head_near, sums_last[:HEAD_ROWS]
    others = [across_core(block) for block in (*blocks[:3], sums_last)]
    grad_out, grad_qkv, gain_one, gain_two = finish_heads(
        *blocks, *others[:3], others[3][:HEAD_ROWS], sums_last[HEAD_ROWS:], others[3][HEAD_ROWS:]
    )
    return (
        out_result,
        out_tokens,
        gain_one,
        grad_qkv,
        grad_out,
        gain_two,
        grad_up,
        grad_down,
    )


def local(tokens, *rest):
    fits = (
        lax.axis_size("wshard") == 4
        and lax.axis_size("ctx") == 8
        and tokens.shape[:2] == (2, 1)
        and 2 * tokens.shape[2] == TILE
    )
    return (local_grid if fits else local_any)(tokens, *rest)


def solution(mesh):
    placed = (
        P(None, "wshard", "ctx", None),
        P("wshard"),
        P("wshard", None),
        P("wshard", None),
        P("wshard"),
        P("wshard", None),
        P("wshard", None),
        P(None, "wshard", "ctx", None),
    )
    return jax.shard_map(
        local,
        mesh=mesh,
        in_specs=placed,
        out_specs=(
            P(None, "wshard", "ctx", None),
            P(None, "wshard", "ctx", None),
            P("wshard"),
            P("wshard", None),
            P("wshard", None),
            P("wshard"),
            P("wshard", None),
            P("wshard", None),
        ),
        check_vma=False,
    )
```
